128 devices in a mesh: segment: 4 (over x), dp: 16 (over z, y), mp: 2 (over core).
Axes of the slice: x: 4, y: 4, z: 4, core: 2. Of those that a mesh axis runs over, the one named last changes fastest.
Arguments:
- teacher_hidden: bfloat16 [4096, 8192], P('dp', 'mp'), may hold values from -6 to 6
- teacher_id: int32 [4096], P('dp'), may hold values from 0 to 2
- destination: int32 [4096], P('dp'), may hold values from 0 to 15, as said below
- row_counts: int32 [16, 16], P('dp'), may hold values from 0 to 32, as said below
- section_gain: bfloat16 [4, 8192], P('segment', 'mp'), may hold values from 0.25 to 1.75
- adapter_down: bfloat16 [4, 8192, 192], P('segment', 'mp'), may hold values from -0.0625 to 0.0625
- adapter_up: bfloat16 [4, 192, 8192], P('segment', None, 'mp'), may hold values from -0.75 to 0.75
- student_in: bfloat16 [8192, 5120], P('dp', 'mp'), may hold values from -6 to 6
- student_gain: float32 [5120], P('mp'), may hold values from 0.25 to 1.75
- student_weight: bfloat16 [5120, 5120], P('mp', 'segment'), may hold values from -0.078125 to 0.078125
- projector: bfloat16 [8192, 5120], P('mp', 'segment'), may hold values from -0.0625 to 0.0625
Outputs:
- weight_grad: float32 [2, 2560, 5120], P('mp', 'dp', 'segment')
- row_loss: float32 [8192], P('dp')
The draws below stay inside these ranges and needn't reach their ends.
Inputs may be any that keep to these rules, and one draw needn't show every extreme that they name: Of the 256 rows of one shard at most 32 have one destination; in every draw one destination gets exactly 32 rows from every shard. row_counts[d, i] is the number of rows of shard i whose destination is d.
All inputs are finite; a program needn't handle non-finite values.
Results may differ from the reference program's by a relative error of at most 0.033.
Values may be sent and summed in bfloat16 or wider, within the bound.
A program may use at most 128 MiB of HBM per device.

```python
import jax
import jax.numpy as jnp
from jax import lax

D = 8192
S = 5120
RANK = 64
TEACH = 3
TOK_DEV = 256
TOKENS = 4096
CAP = 32
SLOTS = 512
ROWS_S = 8192
N_SEGMENT = 4
N_DP = 16
N_MP = 2


def routing_table(key):
    full_dest = jax.random.randint(jax.random.fold_in(key, 101), (), 0, N_DP)
    offsets = jax.random.randint(jax.random.fold_in(key, 102), (N_DP,), 0, 2 ** 19)
    keys = jax.random.split(jax.random.fold_in(key, 103), N_DP)
    slots_all = N_DP * CAP
    grid = jnp.arange(slots_all, dtype=jnp.int32)

    def one_block(block_key):
        score = jax.random.randint(jax.random.fold_in(block_key, 1), (slots_all,), 0, 2 ** 20)
        score = score + offsets[grid // CAP]
        score = jnp.where(grid // CAP == full_dest, -1, score)
        score = score * slots_all + grid
        order = jnp.argsort(score, stable=True)
        chosen = order[:TOK_DEV].astype(jnp.int32)
        shuffled = jax.random.permutation(jax.random.fold_in(block_key, 2), chosen)
        return (shuffled // CAP).astype(jnp.int32)
    return jax.vmap(one_block)(keys).reshape(N_DP * TOK_DEV)


def draw_destination(key, part):
    return routing_table(key)


def draw_row_counts(key, part):
    dest = routing_table(key).reshape(N_DP, TOK_DEV)
    onehot = (dest[:, :, None] == jnp.arange(N_DP, dtype=jnp.int32)[None, None, :]).astype(jnp.int32)
    per_source = jnp.sum(onehot, axis=1)
    return per_source.T.astype(jnp.int32)


def plant(entries, stream_key, low, top_value):
    longest = entries.shape.index(max(entries.shape))
    spots = []
    for shift in (0, 1):
        where = [jax.random.randint(jax.random.fold_in(stream_key, axis), (), 0, length) for axis, length in enumerate(entries.shape)]
        where[longest] = (where[longest] + shift) % entries.shape[longest]
        spots.append(tuple(where))
    return entries.at[spots[0]].set(low).at[spots[1]].set(top_value)


def levels(stream_key, shape, cuts, low, top_value):
    gain = 1.0
    for dim, shards_of in cuts:
        heights = jax.random.uniform(jax.random.fold_in(jax.random.fold_in(stream_key, 6), dim), (shards_of,), jnp.float32, low / len(cuts), top_value / len(cuts))
        gain = gain * jnp.repeat(jnp.exp(heights), shape[dim] // shards_of).reshape((-1,) + (1,) * (len(shape) - 1 - dim))
    return gain


def bell_draw(own_key, extent, width, limit, cuts=(), kind=jnp.bfloat16):
    drawn = jax.random.normal(own_key, extent, jnp.float32) * width
    if len(cuts) > 0:
        drawn = levels(own_key, extent, cuts, -0.22, 0.18) * drawn
    return jnp.clip(drawn, min=-limit, max=limit).astype(kind)


def setup_inputs(seed: int = 0) -> dict:
    streams_of = jax.random.split(jax.random.key(seed), 12)
    teacher_hidden = bell_draw(streams_of[0], (TOKENS, D), 1.0, 6.0, ((0, 16), (1, 2)))
    teacher_id = plant(jax.random.randint(streams_of[1], (TOKENS,), 0, 3), jax.random.fold_in(streams_of[1], 1), 0, 2).astype(jnp.int32)
    destination = draw_destination(jax.random.fold_in(streams_of[11], 71), 0)
    row_counts = draw_row_counts(jax.random.fold_in(streams_of[11], 71), 0)
    section_gain = jnp.clip(1.0 + 0.15 * jax.random.normal(streams_of[4], (N_SEGMENT, D), jnp.float32), 0.25, 1.75).astype(jnp.bfloat16)
    adapter_down = bell_draw(streams_of[5], (N_SEGMENT, D, TEACH * RANK), D ** -0.5, 0.0625, ((0, 4), (1, 2)))
    adapter_up = bell_draw(streams_of[6], (N_SEGMENT, TEACH * RANK, D), RANK ** -0.5, 0.75, ((0, 4), (2, 2)))
    student_in = bell_draw(streams_of[7], (ROWS_S, S), 1.0, 6.0, ((0, 16), (1, 2)))
    student_gain = jnp.clip(1.0 + 0.15 * jax.random.normal(streams_of[8], (S,), jnp.float32), 0.25, 1.75)
    student_weight = bell_draw(streams_of[9], (S, S), S ** -0.5, 0.078125, ((0, 2), (1, 4)))
    projector = bell_draw(streams_of[10], (D, S), D ** -0.5, 0.0625, ((0, 2), (1, 4)))
    return {"teacher_hidden": teacher_hidden, "teacher_id": teacher_id, "destination": destination, "row_counts": row_counts, "section_gain": section_gain, "adapter_down": adapter_down, "adapter_up": adapter_up, "student_in": student_in, "student_gain": student_gain, "student_weight": student_weight, "projector": projector}


def reference(teacher_hidden, teacher_id, destination, row_counts, section_gain, adapter_down, adapter_up, student_in, student_gain, student_weight, projector):
    hidden = teacher_hidden
    column_teacher = jnp.arange(TEACH * RANK, dtype=jnp.int32) // RANK
    pick = column_teacher[None, :] == teacher_id[:, None]
    for section in range(N_SEGMENT):
        wide = hidden.astype(jnp.float32)
        mean_sq = lax.optimization_barrier(jnp.mean(wide * wide, axis=1))
        scaled = (wide * section_gain[section].astype(jnp.float32)[None, :]).astype(jnp.bfloat16)
        latent = jnp.dot(scaled, adapter_down[section], preferred_element_type=jnp.float32)
        latent = latent * lax.rsqrt(mean_sq + 1e-06)[:, None]
        chosen = jnp.where(pick, latent, 0.0).astype(jnp.bfloat16)
        hidden = (wide + jnp.dot(chosen, adapter_up[section], preferred_element_type=jnp.float32)).astype(jnp.bfloat16)
    projected = jnp.dot(hidden, projector, preferred_element_type=jnp.float32)
    blocks = destination.reshape(N_DP, TOK_DEV)
    onehot = (blocks[:, :, None] == jnp.arange(N_DP, dtype=jnp.int32)[None, None, :]).astype(jnp.int32)
    earlier = jnp.cumsum(onehot, axis=1) - onehot
    slot = lax.optimization_barrier(jnp.sum(earlier * onehot, axis=2))
    source = jnp.arange(N_DP, dtype=jnp.int32)[:, None]
    position = ((blocks * N_DP + source) * CAP + slot).reshape(TOKENS).astype(jnp.int32)
    target = jnp.zeros((ROWS_S, S), jnp.float32).at[position].set(projected)
    valid = (jnp.arange(CAP, dtype=jnp.int32)[None, None, :] < row_counts[:, :, None]).reshape(ROWS_S)
    wide_in = student_in.astype(jnp.float32)
    recip = lax.rsqrt(lax.optimization_barrier(jnp.mean(wide_in * wide_in, axis=1)) + 1e-06)
    sgated = (wide_in * student_gain[None, :]).astype(jnp.bfloat16)
    student_out = jnp.dot(sgated, student_weight, preferred_element_type=jnp.float32) * recip[:, None]
    diff = jnp.where(valid[:, None], student_out - target, 0.0)
    row_loss = lax.optimization_barrier(jnp.sum(diff * diff, axis=1)) / S
    normed = (wide_in * student_gain[None, :] * recip[:, None]).astype(jnp.bfloat16)
    grad_rows = diff.astype(jnp.bfloat16)

    def add_shard(total, pair):
        normed_d, grad_d = pair
        partial_value = jnp.dot(normed_d.T, grad_d, preferred_element_type=jnp.float32) / TOK_DEV
        return (total + partial_value.astype(jnp.bfloat16).astype(jnp.float32), None)
    total, _ = lax.scan(add_shard, jnp.zeros((S, S), jnp.float32), (normed.reshape(N_DP, SLOTS, S), grad_rows.reshape(N_DP, SLOTS, S)))
    return (total.reshape(N_MP, S // N_MP, S), row_loss)
```

```python
import jax
import jax.numpy as jnp
from jax import lax
from jax.sharding import PartitionSpec as P

D = 8192
S = 5120
RANK = 64
TOK_DEV = 256
TEACH = 3
bf16 = jnp.bfloat16
f32 = jnp.float32


def dot(a, b):
    return jnp.dot(a, b, preferred_element_type=f32)


def local(
    teacher_hidden,
    teacher_id,
    destination,
    row_counts,
    section_gain,
    adapter_down,
    adapter_up,
    student_in,
    student_gain,
    student_weight,
    projector,
):
    h = teacher_hidden
    tok = h.shape[0]
    half = h.shape[1]
    n_seg = lax.axis_size("segment")
    n_dp = lax.axis_size("dp")
    i = lax.axis_index("dp")
    up = adapter_up[0]
    down = adapter_down[0]
    q = RANK // n_dp
    slots = student_in.shape[0]
    cap = slots // n_dp
    cols = projector.shape[1]
    mine = lax.dynamic_index_in_dim(up.reshape(TEACH, n_dp, q, half), i, 1, keepdims=False)
    u_all = lax.all_gather(mine.reshape(TEACH * q, half), "segment").reshape(n_seg * TEACH * q, half)
    scaled_down = (section_gain[0].astype(f32)[:, None] * down.astype(f32)).astype(bf16)
    up_t = up.T
    hp_part = dot(h, projector).astype(bf16)
    mg = jnp.stack([dot(u_all, scaled_down), dot(u_all, up_t)], axis=1)
    mg = mg.reshape(n_seg, TEACH, q, 2, TEACH, RANK)
    mg = jnp.stack([mg[:, k, :, :, k] for k in range(TEACH)], axis=1)
    mg = mg.reshape(n_seg * TEACH * q, 2 * RANK)
    ids = teacher_id
    pick = (ids[:, None] == jnp.arange(TEACH, dtype=jnp.int32)[None, :]).astype(f32)
    ab = jnp.stack([dot(h, scaled_down), dot(h, up_t)], axis=1).reshape(tok, 2, TEACH, RANK)
    ab = jnp.sum(ab * pick[:, None, :, None], axis=2).reshape(tok, 2 * RANK)
    wide = h.astype(f32)
    sq_part = jnp.sum(wide * wide, axis=1)
    x = student_in.astype(f32)
    sx_part = jnp.sum(x * x, axis=1)
    mg, ab, sq, sx = lax.psum((mg, ab, sq_part, sx_part), "mp")
    upp = lax.psum_scatter(dot(u_all, projector).astype(bf16), "mp", scatter_dimension=1, tiled=True)
    upp = lax.all_gather(upp, "dp")
    mg = lax.all_gather(mg.astype(bf16), ("dp", "segment"))
    mg = mg.reshape(n_dp, n_seg, n_seg, TEACH * q, 2 * RANK)
    hp = lax.psum_scatter(hp_part, "mp", scatter_dimension=1, tiled=True)
    onehot = (destination[:, None] == jnp.arange(n_dp, dtype=jnp.int32)[None, :]).astype(jnp.int32)
    earlier = jnp.cumsum(onehot, axis=0) - onehot
    position = destination * cap + jnp.sum(earlier * onehot, axis=1)
    sel = (position[None, :] == jnp.arange(slots, dtype=jnp.int32)[:, None]).astype(bf16)
    sq_hi = sq.astype(bf16)
    sq_lo = (sq - sq_hi.astype(f32)).astype(bf16)
    meta = jnp.concatenate(
        [ab.astype(bf16), jnp.stack([ids.astype(bf16), sq_hi, sq_lo], axis=1), jnp.zeros((tok, 125), bf16)], axis=1
    )
    send = dot(sel, meta).astype(bf16).reshape(n_dp, cap, -1)
    meta = lax.all_to_all(send, "dp", split_axis=0, concat_axis=0, tiled=True).reshape(slots, -1)
    send = dot(sel, hp).astype(bf16).reshape(n_dp, cap, -1)
    hp = lax.all_to_all(send, "dp", split_axis=0, concat_axis=0, tiled=True).reshape(slots, -1)
    ab = lax.all_gather(meta[:, : 2 * RANK], "segment").astype(f32)
    sid = meta[:, 2 * RANK].astype(f32)
    norm = meta[:, 2 * RANK + 1].astype(f32) + meta[:, 2 * RANK + 2].astype(f32)
    cidx = jnp.arange(n_dp * TEACH * q, dtype=jnp.int32)
    src = (cidx // (TEACH * q)) * q + cidx % q
    spread = (jnp.arange(RANK, dtype=jnp.int32)[:, None] == src[None, :]).astype(bf16)
    keep = ((cidx // q) % TEACH).astype(f32)[None, :] == sid[:, None]
    chosen = []
    for s in range(n_seg):
        a_s, b_s = ab[s, :, :RANK], ab[s, :, RANK:]
        lat = a_s
        cross = 2.0 * b_s
        for t in range(s):
            table = mg[:, s, t].reshape(n_dp * TEACH * q, 2 * RANK)
            both = dot(chosen[t], table)
            lat = lat + both[:, :RANK]
            cross = cross + 2.0 * both[:, RANK:]
        lat = (lat * lax.rsqrt(jnp.maximum(norm, 0.0) / D + 1e-06)[:, None]).astype(bf16)
        wide_c = jnp.where(keep, dot(lat, spread), 0.0).astype(bf16)
        table = mg[:, s, s, :, RANK:].reshape(n_dp * TEACH * q, RANK)
        cross = cross + dot(wide_c, table)
        norm = norm + jnp.sum(cross * lat.astype(f32), axis=1)
        chosen.append(wide_c)
    c_all = jnp.stack(chosen, axis=1).reshape(slots, n_seg, n_dp, TEACH * q)
    c_all = c_all.transpose(0, 2, 1, 3).reshape(slots, -1)
    target = hp.astype(f32) + dot(c_all, upp.reshape(-1, cols // 2))
    recip = lax.rsqrt(sx / S + 1e-06)
    sgated = (x * student_gain[None, :]).astype(bf16)
    so = lax.psum_scatter(dot(sgated, student_weight).astype(bf16), "mp", scatter_dimension=1, tiled=True).astype(f32)
    valid = (jnp.arange(cap, dtype=jnp.int32)[None, :] < row_counts[0][:, None]).reshape(slots)
    diff = jnp.where(valid[:, None], so * recip[:, None] - target, 0.0)
    row_loss = lax.psum(jnp.sum(diff * diff, axis=1), ("segment", "mp")) / S
    normed = (x * student_gain[None, :] * recip[:, None]).astype(bf16)
    grad_rows = lax.all_gather(diff.astype(bf16), "mp", axis=1, tiled=True)
    share = normed.shape[1] // n_dp
    weight_grad = lax.psum_scatter(
        (jnp.einsum("rk,rn->kn", normed, grad_rows, preferred_element_type=f32) / TOK_DEV).astype(bf16),
        "dp",
        scatter_dimension=0,
        tiled=True,
    ).astype(f32)
    return (weight_grad.reshape(1, share, cols), row_loss)


def solution(mesh):
    placed = (
        P("dp", "mp"),
        P("dp"),
        P("dp"),
        P("dp", None),
        P("segment", "mp"),
        P("segment", "mp", None),
        P("segment", None, "mp"),
        P("dp", "mp"),
        P("mp"),
        P("mp", "segment"),
        P("mp", "segment"),
    )
    return jax.shard_map(
        local,
        mesh=mesh,
        in_specs=placed,
        out_specs=(P("mp", "dp", "segment"), P("dp")),
        check_vma=False,
    )
```

```python
import functools

import jax
import jax.numpy as jnp
from jax import lax
from jax.experimental import pallas as pl
from jax.experimental.pallas import tpu as pltpu
from jax.sharding import PartitionSpec as P

D = 8192
S = 5120
RANK = 64
TOK_DEV = 256
TEACH = 3
bf16 = jnp.bfloat16
f32 = jnp.float32


def dot(a, b):
    return jnp.dot(a, b, preferred_element_type=f32)


def remote(src, dst, send, recv, **where):
    return pltpu.make_async_remote_copy(
        src_ref=src,
        dst_ref=dst,
        send_sem=send,
        recv_sem=recv,
        device_id=where,
        device_id_type=pl.DeviceIdType.MESH,
    )


def back_kernel(n_seg, side, sgt, gdh, loss, out, loss_out, gd, part, own, got, part2, got2, losses, ss, rs, ls, lr):
    share = out.shape[0]
    half = gdh.shape[1]
    part_rows = share // 2
    me_s = lax.axis_index("segment")
    me_m = lax.axis_index("mp")
    me_d = lax.axis_index("dp")
    z = me_d // side
    y = me_d % side
    other = 1 - me_m
    y_next = [z * side + (y + step) % side for step in (1, side - 1)]
    z_next = [((z + step) % side) * side + y for step in (1, side - 1)]
    rings = (y_next, z_next)
    places = (y, z)

    barrier = pltpu.get_barrier_semaphore()
    for where in y_next + z_next:
        pl.semaphore_signal(barrier, inc=1, device_id={"dp": where}, device_id_type=pl.DeviceIdType.MESH)
    peers = []
    for ds in range(n_seg):
        for dm in range(2):
            if ds or dm:
                peers.append({"segment": (me_s + ds) % n_seg, "mp": (me_m + dm) % 2})
    for where in peers:
        pl.semaphore_signal(barrier, inc=1, device_id=where, device_id_type=pl.DeviceIdType.MESH)
    pl.semaphore_wait(barrier, 4 + len(peers))

    swap = remote(gdh, gd.at[me_m], ss.at[24], rs.at[24], mp=other)
    swap.start()
    mine = me_s * 2 + me_m
    tells = []
    for n, where in enumerate(peers):
        tell = remote(loss, losses.at[mine], ls.at[n], lr.at[n], **where)
        tell.start()
        tells.append(tell)
    losses[mine] = loss[...]
    gd[me_m] = gdh[...]
    swap.wait()

    def rows(f, g, k):
        block = (k * side + g) if f == 0 else (g * side + k)
        return pl.ds(pl.multiple_of(block * share, share), share)

    def product(f, g, k):
        return jnp.dot(sgt[rows(f, g, k), :], gd[f], preferred_element_type=f32)

    copies = []

    def send(src, dst, number, where):
        copy = remote(src, dst, ss.at[number], rs.at[number], dp=where)
        copy.start()
        copies.append(copy)
        return copy

    first = {}
    for f in (0, 1):
        far = (places[f] + 2) % side

        @pl.loop(0, 2)
        def _(k):
            part[f, 1, k] = product(f, far, k).astype(bf16)

        first[f, 0] = send(part.at[f, 1, 0:2], got.at[f, 0, 0], f * 6 + 0, rings[f][0])

        @pl.loop(2, 4)
        def _(k):
            part[f, 1, k] = product(f, far, k).astype(bf16)

        first[f, 1] = send(part.at[f, 1, 2:4], got.at[f, 1, 0], f * 6 + 3, rings[f][1])
    second = {}
    for f in (0, 1):
        for way in (0, 1):
            near = (places[f] + (1, side - 1)[way]) % side
            low = 2 - 2 * way

            @pl.loop(low, low + 2)
            def _(k):
                part[f, 2 * way, k] = product(f, near, k).astype(bf16)

            second[f, way] = send(part.at[f, 2 * way, low : low + 2], got.at[f, way, 1], f * 6 + 3 * way + 1, rings[f][way])
    third = {}
    for f in (0, 1):
        for way in (0, 1):
            near = (places[f] + (1, side - 1)[way]) % side
            low = 2 * way
            first[f, way].wait_recv()

            @pl.loop(low, low + 2)
            def _(k):
                part[f, 2 * way, k] = (product(f, near, k) + got[f, way, 0, k - low].astype(f32)).astype(bf16)

            third[f, way] = send(part.at[f, 2 * way, low : low + 2], got.at[f, way, 2], f * 6 + 3 * way + 2, rings[f][way])
    for f in (0, 1):

        @pl.loop(0, 4)
        def _(k):
            own[f, k] = product(f, places[f], k)

    first2 = {}
    second2 = {}
    third2 = {}
    for f in (0, 1):
        second[f, 0].wait_recv()
        second[f, 1].wait_recv()

        @pl.loop(0, 2)
        def _(k):
            own[f, k] += got[f, 1, 1, k].astype(f32)
            own[f, k + 2] += got[f, 0, 1, k].astype(f32)

    for f in (0, 1):
        third[f, 0].wait_recv()
        third[f, 1].wait_recv()

        @pl.loop(0, 2)
        def _(k):
            own[f, k] += got[f, 0, 2, k].astype(f32)
            own[f, k + 2] += got[f, 1, 2, k].astype(f32)

        g = 1 - f
        far = (places[g] + 2) % side
        part2[f, 1] = own[f, far].astype(bf16)
        base = 12 + f * 6
        first2[f, 0] = send(part2.at[f, 1, 0:part_rows], got2.at[f, 0, 0], base, rings[g][0])
        first2[f, 1] = send(part2.at[f, 1, part_rows:share], got2.at[f, 1, 0], base + 3, rings[g][1])
        for way in (0, 1):
            near = (places[g] + (1, side - 1)[way]) % side
            low = (1 - way) * part_rows
            part2[f, 2 * way, low : low + part_rows] = own[f, near, low : low + part_rows].astype(bf16)
            second2[f, way] = send(part2.at[f, 2 * way, low : low + part_rows], got2.at[f, way, 1], base + 3 * way + 1, rings[g][way])
    for f in (0, 1):
        g = 1 - f
        base = 12 + f * 6
        for way in (0, 1):
            near = (places[g] + (1, side - 1)[way]) % side
            low = way * part_rows
            first2[f, way].wait_recv()
            part2[f, 2 * way, low : low + part_rows] = (
                own[f, near, low : low + part_rows] + got2[f, way, 0].astype(f32)
            ).astype(bf16)
            third2[f, way] = send(part2.at[f, 2 * way, low : low + part_rows], got2.at[f, way, 2], base + 3 * way + 2, rings[g][way])
    for tell in tells:
        tell.wait()
    total = losses[0]
    for n in range(1, 2 * n_seg):
        total = total + losses[n]
    loss_out[...] = total * (1.0 / S)
    for f in (0, 1):
        g = 1 - f
        for way in (0, 1):
            second2[f, way].wait_recv()
        for way in (0, 1):
            third2[f, way].wait_recv()
        span = slice(f * half, (f + 1) * half)
        top = slice(0, part_rows)
        end = slice(part_rows, share)
        out[top, span] = own[f, places[g], top] + got2[f, 0, 2].astype(f32) + got2[f, 1, 1].astype(f32)
        out[end, span] = own[f, places[g], end] + got2[f, 0, 1].astype(f32) + got2[f, 1, 2].astype(f32)
    for copy in copies:
        copy.wait_send()


def back(sgt, grad_half, loss_part):
    n_seg = lax.axis_size("segment")
    n_dp = lax.axis_size("dp")
    side = 4
    share = sgt.shape[0] // n_dp
    slots, half = grad_half.shape
    half_rows = share // 2
    vmem = pl.BlockSpec(memory_space=pltpu.VMEM)
    flops = 2 * sgt.shape[0] * slots * 2 * half
    return pl.pallas_call(
        functools.partial(back_kernel, n_seg, side),
        out_shape=(
            jax.ShapeDtypeStruct((share, 2 * half), f32),
            jax.ShapeDtypeStruct((1, slots), f32),
        ),
        in_specs=[vmem] * 3,
        out_specs=(vmem, vmem),
        scratch_shapes=[
            pltpu.VMEM((2, slots, half), bf16),
            pltpu.VMEM((2, 3, 4, share, half), bf16),
            pltpu.VMEM((2, 4, share, half), f32),
            pltpu.VMEM((2, 2, 3, 2, share, half), bf16),
            pltpu.VMEM((2, 3, share, half), bf16),
            pltpu.VMEM((2, 2, 3, half_rows, half), bf16),
            pltpu.VMEM((2 * n_seg, 1, slots), f32),
            pltpu.SemaphoreType.DMA((25,)),
            pltpu.SemaphoreType.DMA((25,)),
            pltpu.SemaphoreType.DMA((2 * n_seg - 1,)),
            pltpu.SemaphoreType.DMA((2 * n_seg - 1,)),
        ],
        compiler_params=pltpu.CompilerParams(
            collective_id=1, has_side_effects=True, vmem_limit_bytes=56 * 2**20
        ),
        cost_estimate=pl.CostEstimate(flops=flops, bytes_accessed=8 * 2**20, transcendentals=0),
    )(sgt, grad_half, loss_part)


def local(
    teacher_hidden,
    teacher_id,
    destination,
    row_counts,
    section_gain,
    adapter_down,
    adapter_up,
    student_in,
    student_gain,
    student_weight,
    projector,
):
    h = teacher_hidden
    tok = h.shape[0]
    half = h.shape[1]
    n_seg = lax.axis_size("segment")
    n_dp = lax.axis_size("dp")
    i = lax.axis_index("dp")
    up = adapter_up[0]
    down = adapter_down[0]
    q = RANK // n_dp
    slots = student_in.shape[0]
    cap = slots // n_dp
    cols = projector.shape[1]
    mine = lax.dynamic_index_in_dim(up.reshape(TEACH, n_dp, q, half), i, 1, keepdims=False)
    u_all = lax.all_gather(mine.reshape(TEACH * q, half), "segment").reshape(n_seg * TEACH * q, half)
    scaled_down = (section_gain[0].astype(f32)[:, None] * down.astype(f32)).astype(bf16)
    up_t = up.T
    hp_part = dot(h, projector).astype(bf16)
    mg = jnp.stack([dot(u_all, scaled_down), dot(u_all, up_t)], axis=1)
    mg = mg.reshape(n_seg, TEACH, q, 2, TEACH, RANK)
    mg = jnp.stack([mg[:, k, :, :, k] for k in range(TEACH)], axis=1)
    mg = mg.reshape(n_seg * TEACH * q, 2 * RANK)
    ids = teacher_id
    pick = (ids[:, None] == jnp.arange(TEACH, dtype=jnp.int32)[None, :]).astype(f32)
    ab = jnp.stack([dot(h, scaled_down), dot(h, up_t)], axis=1).reshape(tok, 2, TEACH, RANK)
    ab = jnp.sum(ab * pick[:, None, :, None], axis=2).reshape(tok, 2 * RANK)
    wide = h.astype(f32)
    sq_part = jnp.sum(wide * wide, axis=1)
    x = student_in.astype(f32)
    sx_part = jnp.sum(x * x, axis=1)
    mg, ab, sq, sx = lax.psum((mg, ab, sq_part, sx_part), "mp")
    upp = lax.psum_scatter(dot(u_all, projector).astype(bf16), "mp", scatter_dimension=1, tiled=True)
    upp = lax.all_gather(upp, "dp")
    mg = lax.all_gather(lax.all_gather(mg.astype(bf16), "segment"), "dp")
    mg = mg.reshape(n_dp, n_seg, n_seg, TEACH * q, 2 * RANK)
    hp = lax.psum_scatter(hp_part, "mp", scatter_dimension=1, tiled=True)
    onehot = (destination[:, None] == jnp.arange(n_dp, dtype=jnp.int32)[None, :]).astype(jnp.int32)
    earlier = jnp.cumsum(onehot, axis=0) - onehot
    position = destination * cap + jnp.sum(earlier * onehot, axis=1)
    sel = (position[None, :] == jnp.arange(slots, dtype=jnp.int32)[:, None]).astype(bf16)
    sq_hi = sq.astype(bf16)
    sq_lo = (sq - sq_hi.astype(f32)).astype(bf16)
    meta = jnp.concatenate(
        [ab.astype(bf16), jnp.stack([ids.astype(bf16), sq_hi, sq_lo], axis=1), jnp.zeros((tok, 125), bf16)], axis=1
    )
    send = dot(sel, meta).astype(bf16).reshape(n_dp, cap, -1)
    meta = lax.all_to_all(send, "dp", split_axis=0, concat_axis=0, tiled=True).reshape(slots, -1)
    send = dot(sel, hp).astype(bf16).reshape(n_dp, cap, -1)
    hp = lax.all_to_all(send, "dp", split_axis=0, concat_axis=0, tiled=True).reshape(slots, -1)
    ab = lax.all_gather(meta[:, : 2 * RANK], "segment").astype(f32)
    sid = meta[:, 2 * RANK].astype(f32)
    norm = meta[:, 2 * RANK + 1].astype(f32) + meta[:, 2 * RANK + 2].astype(f32)
    cidx = jnp.arange(n_dp * TEACH * q, dtype=jnp.int32)
    src = (cidx // (TEACH * q)) * q + cidx % q
    spread = (jnp.arange(RANK, dtype=jnp.int32)[:, None] == src[None, :]).astype(bf16)
    keep = ((cidx // q) % TEACH).astype(f32)[None, :] == sid[:, None]
    chosen = []
    for s in range(n_seg):
        a_s, b_s = ab[s, :, :RANK], ab[s, :, RANK:]
        lat = a_s
        cross = 2.0 * b_s
        for t in range(s):
            table = mg[:, s, t].reshape(n_dp * TEACH * q, 2 * RANK)
            both = dot(chosen[t], table)
            lat = lat + both[:, :RANK]
            cross = cross + 2.0 * both[:, RANK:]
        lat = (lat * lax.rsqrt(jnp.maximum(norm, 0.0) / D + 1e-06)[:, None]).astype(bf16)
        wide_c = jnp.where(keep, dot(lat, spread), 0.0).astype(bf16)
        table = mg[:, s, s, :, RANK:].reshape(n_dp * TEACH * q, RANK)
        cross = cross + dot(wide_c, table)
        norm = norm + jnp.sum(cross * lat.astype(f32), axis=1)
        chosen.append(wide_c)
    c_all = jnp.stack(chosen, axis=1).reshape(slots, n_seg, n_dp, TEACH * q)
    c_all = c_all.transpose(0, 2, 1, 3).reshape(slots, -1)
    target = hp.astype(f32) + dot(c_all, upp.reshape(-1, cols // 2))
    recip = lax.rsqrt(sx / S + 1e-06)
    sgated = (x * student_gain[None, :]).astype(bf16)
    so = lax.psum_scatter(dot(sgated, student_weight).astype(bf16), "mp", scatter_dimension=1, tiled=True).astype(f32)
    valid = (jnp.arange(cap, dtype=jnp.int32)[None, :] < row_counts[0][:, None]).reshape(slots)
    diff = jnp.where(valid[:, None], so * recip[:, None] - target, 0.0)
    loss_part = jnp.sum(diff * diff, axis=1).reshape(1, slots)
    grad_half = (diff * (recip / TOK_DEV)[:, None]).astype(bf16)
    weight_grad, row_loss = back(sgated.T, grad_half, loss_part)
    share = weight_grad.shape[0]
    row_loss = row_loss.reshape(slots)
    return (weight_grad.reshape(1, share, cols), row_loss)


def solution(mesh):
    placed = (
        P("dp", "mp"),
        P("dp"),
        P("dp"),
        P("dp", None),
        P("segment", "mp"),
        P("segment", "mp", None),
        P("segment", None, "mp"),
        P("dp", "mp"),
        P("mp"),
        P("mp", "segment"),
        P("mp", "segment"),
    )
    return jax.shard_map(
        local,
        mesh=mesh,
        in_specs=placed,
        out_specs=(P("mp", "dp", "segment"), P("dp")),
        check_vma=False,
    )
```

```python
import functools

import jax
import jax.numpy as jnp
import numpy as np
from jax import lax
from jax.experimental import pallas as pl
from jax.experimental.pallas import tpu as pltpu
from jax.sharding import PartitionSpec as P

D = 8192
S = 5120
RANK = 64
TOK_DEV = 256
TEACH = 3
LANES = 128
bf16 = jnp.bfloat16
f32 = jnp.float32


def dot(a, b):
    return jnp.dot(a, b, preferred_element_type=f32)


def remote(src, dst, send, recv, **where):
    return pltpu.make_async_remote_copy(
        src_ref=src,
        dst_ref=dst,
        send_sem=send,
        recv_sem=recv,
        device_id=where,
        device_id_type=pl.DeviceIdType.MESH,
    )


def back_kernel(n_seg, side, sgt, gdh, loss, out, loss_out, gd, part, own, got, part2, got2, losses, ss, rs, ls, lr):
    share = out.shape[0]
    half = gdh.shape[1]
    part_rows = share // 2
    me_s = lax.axis_index("segment")
    me_m = lax.axis_index("mp")
    me_d = lax.axis_index("dp")
    z = me_d // side
    y = me_d % side
    other = 1 - me_m
    y_next = [z * side + (y + step) % side for step in (1, side - 1)]
    z_next = [((z + step) % side) * side + y for step in (1, side - 1)]
    rings = (y_next, z_next)
    places = (y, z)

    barrier = pltpu.get_barrier_semaphore()
    for where in y_next + z_next:
        pl.semaphore_signal(barrier, inc=1, device_id={"dp": where}, device_id_type=pl.DeviceIdType.MESH)
    peers = []
    for ds in range(n_seg):
        for dm in range(2):
            if ds or dm:
                peers.append({"segment": (me_s + ds) % n_seg, "mp": (me_m + dm) % 2})
    for where in peers:
        pl.semaphore_signal(barrier, inc=1, device_id=where, device_id_type=pl.DeviceIdType.MESH)
    pl.semaphore_wait(barrier, 4 + len(peers))

    swap = remote(gdh, gd.at[me_m], ss.at[24], rs.at[24], mp=other)
    swap.start()
    mine = me_s * 2 + me_m
    tells = []
    for n, where in enumerate(peers):
        tell = remote(loss, losses.at[mine], ls.at[n], lr.at[n], **where)
        tell.start()
        tells.append(tell)
    losses[mine] = loss[...]
    gd[me_m] = gdh[...]
    swap.wait()

    def rows(f, g, k):
        block = (k * side + g) if f == 0 else (g * side + k)
        return pl.ds(pl.multiple_of(block * share, share), share)

    def product(f, g, k):
        return jnp.dot(sgt[rows(f, g, k), :], gd[f], preferred_element_type=f32)

    copies = []

    def send(src, dst, number, where):
        copy = remote(src, dst, ss.at[number], rs.at[number], dp=where)
        copy.start()
        copies.append(copy)
        return copy

    first = {}
    for f in (0, 1):
        far = (places[f] + 2) % side

        @pl.loop(0, 2)
        def _(k):
            part[f, 1, k] = product(f, far, k).astype(bf16)

        first[f, 0] = send(part.at[f, 1, 0:2], got.at[f, 0, 0], f * 6 + 0, rings[f][0])

        @pl.loop(2, 4)
        def _(k):
            part[f, 1, k] = product(f, far, k).astype(bf16)

        first[f, 1] = send(part.at[f, 1, 2:4], got.at[f, 1, 0], f * 6 + 3, rings[f][1])
    second = {}
    for f in (0, 1):
        for way in (0, 1):
            near = (places[f] + (1, side - 1)[way]) % side
            low = 2 - 2 * way

            @pl.loop(low, low + 2)
            def _(k):
                part[f, 2 * way, k] = product(f, near, k).astype(bf16)

            second[f, way] = send(part.at[f, 2 * way, low : low + 2], got.at[f, way, 1], f * 6 + 3 * way + 1, rings[f][way])
    third = {}
    for f in (0, 1):
        for way in (0, 1):
            near = (places[f] + (1, side - 1)[way]) % side
            low = 2 * way
            first[f, way].wait_recv()

            @pl.loop(low, low + 2)
            def _(k):
                part[f, 2 * way, k] = (product(f, near, k) + got[f, way, 0, k - low].astype(f32)).astype(bf16)

            third[f, way] = send(part.at[f, 2 * way, low : low + 2], got.at[f, way, 2], f * 6 + 3 * way + 2, rings[f][way])
    for f in (0, 1):

        @pl.loop(0, 4)
        def _(k):
            own[f, k] = product(f, places[f], k)

    first2 = {}
    second2 = {}
    third2 = {}
    for f in (0, 1):
        second[f, 0].wait_recv()
        second[f, 1].wait_recv()

        @pl.loop(0, 2)
        def _(k):
            own[f, k] += got[f, 1, 1, k].astype(f32)
            own[f, k + 2] += got[f, 0, 1, k].astype(f32)

    for f in (0, 1):
        third[f, 0].wait_recv()
        third[f, 1].wait_recv()

        @pl.loop(0, 2)
        def _(k):
            own[f, k] += got[f, 0, 2, k].astype(f32)
            own[f, k + 2] += got[f, 1, 2, k].astype(f32)

        g = 1 - f
        far = (places[g] + 2) % side
        part2[f, 1] = own[f, far].astype(bf16)
        base = 12 + f * 6
        first2[f, 0] = send(part2.at[f, 1, 0:part_rows], got2.at[f, 0, 0], base, rings[g][0])
        first2[f, 1] = send(part2.at[f, 1, part_rows:share], got2.at[f, 1, 0], base + 3, rings[g][1])
        for way in (0, 1):
            near = (places[g] + (1, side - 1)[way]) % side
            low = (1 - way) * part_rows
            part2[f, 2 * way, low : low + part_rows] = own[f, near, low : low + part_rows].astype(bf16)
            second2[f, way] = send(part2.at[f, 2 * way, low : low + part_rows], got2.at[f, way, 1], base + 3 * way + 1, rings[g][way])
    for f in (0, 1):
        g = 1 - f
        base = 12 + f * 6
        for way in (0, 1):
            near = (places[g] + (1, side - 1)[way]) % side
            low = way * part_rows
            first2[f, way].wait_recv()
            part2[f, 2 * way, low : low + part_rows] = (
                own[f, near, low : low + part_rows] + got2[f, way, 0].astype(f32)
            ).astype(bf16)
            third2[f, way] = send(part2.at[f, 2 * way, low : low + part_rows], got2.at[f, way, 2], base + 3 * way + 2, rings[g][way])
    for tell in tells:
        tell.wait()
    total = losses[0]
    for n in range(1, 2 * n_seg):
        total = total + losses[n]
    loss_out[...] = total * (1.0 / S)
    for f in (0, 1):
        g = 1 - f
        for way in (0, 1):
            second2[f, way].wait_recv()
        for way in (0, 1):
            third2[f, way].wait_recv()
        span = slice(f * half, (f + 1) * half)
        top = slice(0, part_rows)
        end = slice(part_rows, share)
        out[top, span] = own[f, places[g], top] + got2[f, 0, 2].astype(f32) + got2[f, 1, 1].astype(f32)
        out[end, span] = own[f, places[g], end] + got2[f, 0, 1].astype(f32) + got2[f, 1, 2].astype(f32)
    for copy in copies:
        copy.wait_send()


def back(sgt, grad_half, loss_part):
    n_seg = lax.axis_size("segment")
    n_dp = lax.axis_size("dp")
    side = 4
    share = sgt.shape[0] // n_dp
    slots, half = grad_half.shape
    half_rows = share // 2
    vmem = pl.BlockSpec(memory_space=pltpu.VMEM)
    flops = 2 * sgt.shape[0] * slots * 2 * half
    return pl.pallas_call(
        functools.partial(back_kernel, n_seg, side),
        out_shape=(
            jax.ShapeDtypeStruct((share, 2 * half), f32),
            jax.ShapeDtypeStruct((1, slots), f32),
        ),
        in_specs=[vmem] * 3,
        out_specs=(vmem, vmem),
        scratch_shapes=[
            pltpu.VMEM((2, slots, half), bf16),
            pltpu.VMEM((2, 3, 4, share, half), bf16),
            pltpu.VMEM((2, 4, share, half), f32),
            pltpu.VMEM((2, 2, 3, 2, share, half), bf16),
            pltpu.VMEM((2, 3, share, half), bf16),
            pltpu.VMEM((2, 2, 3, half_rows, half), bf16),
            pltpu.VMEM((2 * n_seg, 1, slots), f32),
            pltpu.SemaphoreType.DMA((25,)),
            pltpu.SemaphoreType.DMA((25,)),
            pltpu.SemaphoreType.DMA((2 * n_seg - 1,)),
            pltpu.SemaphoreType.DMA((2 * n_seg - 1,)),
        ],
        compiler_params=pltpu.CompilerParams(
            collective_id=1, has_side_effects=True, vmem_limit_bytes=56 * 2**20
        ),
        cost_estimate=pl.CostEstimate(flops=flops, bytes_accessed=8 * 2**20, transcendentals=0),
    )(sgt, grad_half, loss_part)


def iota(shape, dim):
    return lax.broadcasted_iota(jnp.int32, shape, dim)


def ones_where(mask):
    return jnp.where(mask, 1.0, 0.0).astype(bf16)


def dot_nt(a, b):
    return lax.dot_general(a, b, (((1,), (1,)), ((), ())), preferred_element_type=f32)


def turned(row):
    return jnp.broadcast_to(row, (LANES, row.shape[1])).T


def fold(wide, keep):
    kept = jnp.where(keep, wide, 0.0)
    both = kept[:, :LANES] + kept[:, LANES:]
    return both + pltpu.roll(both, RANK, 1)


def front_kernel(
    n_seg, n_dp, cap,
    h_hbm, down_hbm, up_hbm, x_hbm, w_hbm, p_hbm, xmap_hbm,
    ids, dest, counts, gain, sgain, kcol,
    gd_out, loss_out, sgt_out,
    h, down, up, x, w, p, xmap,
    usend, ugot, ucat, wide_a, wide_b, abx, abgot, sel, pay, aslots, agot, aall,
    mgx, mggot, mgs, mgall, upx, upgot, upall,
    hpx, hpsend, hpgot, hslots, hgot,
    sg, sox, sosend, sogot, sxx, sxgot, ctil,
    lsem, s_m, r_m, s_x, r_x, s_d, r_d,
):
    me_s = lax.axis_index("segment")
    me_m = lax.axis_index("mp")
    me_d = lax.axis_index("dp")
    other = 1 - me_m
    tok, half = h.shape
    slots = x.shape[0]
    cols = p.shape[1]
    out_half = cols // 2
    rows_u = mgx.shape[0]
    per = rows_u // n_seg
    q = per // TEACH
    part = half // n_seg

    loads = []
    for n, (src, dst) in enumerate(
        ((up_hbm, up), (h_hbm, h), (down_hbm, down), (p_hbm, p), (xmap_hbm, xmap), (x_hbm, x), (w_hbm, w))
    ):
        copy = pltpu.make_async_copy(src, dst, lsem.at[n])
        copy.start()
        loads.append(copy)
    up_in, h_in, down_in, p_in, xmap_in, x_in, w_in = loads

    barrier = pltpu.get_barrier_semaphore()
    mesh_id = pl.DeviceIdType.MESH
    pl.semaphore_signal(barrier, inc=1, device_id={"mp": other}, device_id_type=mesh_id)
    for n in range(1, n_seg):
        pl.semaphore_signal(barrier, inc=1, device_id={"segment": (me_s + n) % n_seg}, device_id_type=mesh_id)

    @pl.loop(1, n_dp)
    def _(n):
        pl.semaphore_signal(barrier, inc=1, device_id={"dp": (me_d + n) % n_dp}, device_id_type=mesh_id)

    def to_peer(n, src, dst):
        return remote(src, dst, s_m.at[n], r_m.at[n], mp=other)

    def to_seg(kind, n, src, dst):
        number = kind * (n_seg - 1) + n - 1
        return remote(src, dst, s_x.at[number], r_x.at[number], segment=(me_s + n) % n_seg)

    def to_dp(kind, n, src, dst):
        number = kind * (n_dp - 1) + n - 1
        return remote(src, dst, s_d.at[number], r_d.at[number], dp=(me_d + n) % n_dp)

    packed = n_seg * per
    row = iota((packed, up.shape[0]), 0)
    col = iota((packed, up.shape[0]), 1)
    quad = row >> 2
    block = (quad >= 3).astype(jnp.int32) + (quad >= 6).astype(jnp.int32) + (quad >= 9).astype(jnp.int32)
    teacher = quad - 3 * block
    hit = ((col >> 6) == teacher) & (((col & 63) >> 2) == me_d) & ((col & 3) == (row & 3))
    up_in.wait()
    mine = jnp.zeros((packed, part), f32)
    for g in range(n_seg):
        mine = mine + dot(ones_where(hit & (block == g)), up[:, g * part : (g + 1) * part])
    usend[...] = mine.astype(bf16)
    ugot[me_s] = usend[...]
    pl.semaphore_wait(barrier, 1 + (n_seg - 1) + (n_dp - 1))
    u_sent = [to_seg(0, n, usend, ugot.at[me_s]) for n in range(1, n_seg)]
    for copy in u_sent:
        copy.start()

    h_in.wait()
    down_in.wait()
    wide_a[...] = jnp.zeros(wide_a.shape, f32)
    wide_b[...] = jnp.zeros(wide_b.shape, f32)
    abx[...] = jnp.zeros(abx.shape, f32)
    rank_all = down.shape[1]

    @pl.loop(0, n_seg)
    def _(g):
        span = pl.ds(pl.multiple_of(g * part, part), part)
        here = h[:, span]
        wide = here.astype(f32)
        scaled = (wide * gain[:, span].astype(f32)).astype(bf16)
        wide_a[:, :rank_all] += dot(scaled, down[span, :])
        wide_b[:, :rank_all] += dot_nt(here, up[:, span])
        abx[:, LANES:] += jnp.broadcast_to(jnp.sum(wide * wide, axis=1, keepdims=True), (tok, LANES))

    id_col = turned(ids[...].astype(f32))
    lane2 = iota((tok, 2 * LANES), 1)
    own = (lane2 >> 6).astype(f32) == jnp.concatenate([id_col, id_col], axis=1)
    lane = iota((tok, LANES), 1)
    abx[:, :LANES] = jnp.where(lane < RANK, fold(wide_a[...], own), fold(wide_b[...], own))
    ab_sent = to_peer(0, abx, abgot)
    ab_sent.start()

    dest_f = dest[...].astype(f32)
    onehot = jnp.where(iota((n_dp, tok), 0).astype(f32) == dest_f, 1.0, 0.0)
    before = ones_where(iota((tok, tok), 0) < iota((tok, tok), 1))
    earlier = dot(onehot.astype(bf16), before)
    position = dest_f * cap + jnp.sum(earlier * onehot, axis=0, keepdims=True)
    sel[...] = ones_where(iota((slots, tok), 0).astype(f32) == position)

    ab_sent.wait_recv()
    total = abx[...] + abgot[...]
    sq = total[:, LANES:]
    sq_hi = sq.astype(bf16).astype(f32)
    extra = jnp.where(lane == 0, id_col, jnp.where(lane == 1, sq_hi, jnp.where(lane == 2, sq - sq_hi, 0.0)))
    pay[:, :LANES] = total[:, :LANES].astype(bf16)
    pay[:, LANES:] = extra.astype(bf16)
    aslots[...] = dot(sel[...], pay[...]).astype(bf16).reshape(aslots.shape)
    agot[me_d] = aslots[me_d]

    def a_copy(n):
        return to_dp(0, n, aslots.at[(me_d + n) % n_dp], agot.at[me_d])

    @pl.loop(1, n_dp)
    def _(n):
        a_copy(n).start()

    for copy in u_sent:
        copy.wait_recv()
    row = iota((packed, n_seg * packed), 0)
    col = iota((packed, n_seg * packed), 1)
    quad = row >> 2
    block = (quad >= 3).astype(jnp.int32) + (quad >= 6).astype(jnp.int32) + (quad >= 9).astype(jnp.int32)
    got_u = ugot[...].reshape(n_seg * packed, part)
    for g in range(n_seg):
        take = ones_where(col == row + (packed - per) * block + per * g)
        ucat[:, g * part : (g + 1) * part] = dot(take, got_u).astype(bf16)
    u = ucat[...]
    u_scaled = (u.astype(f32) * gain[...].astype(f32)).astype(bf16)
    wide_a[:rows_u, :rank_all] = dot(u_scaled, down[...])
    wide_b[:rows_u, :rank_all] = dot_nt(u, up[...])
    row = iota((rows_u, 2 * LANES), 0)
    quad = row >> 2
    block = (quad >= 3).astype(jnp.int32) + (quad >= 6).astype(jnp.int32) + (quad >= 9).astype(jnp.int32)
    same = (quad - 3 * block) == (iota((rows_u, 2 * LANES), 1) >> 6)
    lane_u = iota((rows_u, LANES), 1)
    mgx[...] = jnp.where(lane_u < RANK, fold(wide_a[:rows_u, :], same), fold(wide_b[:rows_u, :], same))
    mg_sent = to_peer(1, mgx, mggot)
    mg_sent.start()
    p_in.wait()
    tile = 2 * LANES

    @pl.loop(0, cols // tile)
    def _(n):
        span = pl.ds(pl.multiple_of(n * tile, tile), tile)
        upx[:, span] = dot(ucat[...], p[:, span])

    away = pl.ds(pl.multiple_of(other * out_half, LANES), out_half)
    kept = pl.ds(pl.multiple_of(me_m * out_half, LANES), out_half)
    up_sent = to_peer(2, upx.at[:, away], upgot)
    up_sent.start()
    mg_sent.wait_recv()
    mgs[me_s] = (mgx[...] + mggot[...]).astype(bf16)
    mg_x = [to_seg(1, n, mgs.at[me_s], mgs.at[me_s]) for n in range(1, n_seg)]
    for copy in mg_x:
        copy.start()
    up_sent.wait_recv()
    upall[me_d] = (upx[:, kept] + upgot[...]).astype(bf16)

    def u_copy(n):
        return to_dp(1, n, upall.at[me_d], upall.at[me_d])

    @pl.loop(1, n_dp)
    def _(n):
        u_copy(n).start()

    @pl.loop(0, cols // tile)
    def _(n):
        span = pl.ds(pl.multiple_of(n * tile, tile), tile)
        hpx[:, span] = dot(h[...], p[:, span])

    hpsend[...] = hpx[:, away].astype(bf16)
    hp_sent = to_peer(3, hpsend, hpgot)
    hp_sent.start()
    for copy in mg_x:
        copy.wait_recv()
    pair = n_seg // 2
    mgall[me_m, me_d] = mgs[pl.ds(me_m * pair, pair)]

    def m_copy(n):
        return to_dp(2, n, mgall.at[me_m, me_d], mgall.at[me_m, me_d])

    @pl.loop(1, n_dp)
    def _(n):
        m_copy(n).start()

    @pl.loop(1, n_dp)
    def _(n):
        a_copy(n).wait_recv()

    aall[me_s] = agot[:, :, :LANES].reshape(slots, LANES)
    a_x = [to_seg(2, n, aall.at[me_s], aall.at[me_s]) for n in range(1, n_seg)]
    for copy in a_x:
        copy.start()
    hp_sent.wait_recv()
    hp = (hpx[:, kept] + hpgot[...].astype(f32)).astype(bf16)
    hslots[...] = dot(sel[...], hp).astype(bf16).reshape(hslots.shape)
    hgot[me_d] = hslots[me_d]

    def h_copy(n):
        return to_dp(3, n, hslots.at[(me_d + n) % n_dp], hgot.at[me_d])

    @pl.loop(1, n_dp)
    def _(n):
        h_copy(n).start()

    x_in.wait()
    chunk = 128

    @pl.loop(0, slots // chunk)
    def _(n):
        span = pl.ds(pl.multiple_of(n * chunk, chunk), chunk)
        wide = x[span, :].astype(f32)
        sxx[span, :] = jnp.broadcast_to(jnp.sum(wide * wide, axis=1, keepdims=True), (chunk, LANES))
        sg[span, :] = (wide * sgain[...]).astype(bf16)

    sx_sent = to_peer(4, sxx, sxgot)
    sx_sent.start()
    w_in.wait()

    @pl.loop(0, cols // tile)
    def _(n):
        span = pl.ds(pl.multiple_of(n * tile, tile), tile)
        sox[:, span] = dot(sg[...], w[:, span])

    sosend[...] = sox[:, away].astype(bf16)
    so_sent = to_peer(5, sosend, sogot)
    so_sent.start()

    @pl.loop(0, x.shape[1] // chunk)
    def _(n):
        span = pl.ds(pl.multiple_of(n * chunk, chunk), chunk)
        sgt_out[span, :] = sg[:, span].T

    xmap_in.wait()

    @pl.loop(1, n_dp)
    def _(n):
        m_copy(n).wait_recv()

    mg_swap = to_peer(6, mgall.at[me_m], mgall.at[me_m])
    mg_swap.start()
    extra = agot[:, :, LANES:].reshape(slots, LANES).astype(f32)
    id_slot = extra[:, 0:1]
    norm = extra[:, 1:2] + extra[:, 2:3]
    keep = kcol[...] == id_slot
    lane = iota((slots, LANES), 1)
    for copy in a_x:
        copy.wait_recv()
    mg_swap.wait_recv()
    known = rows_u * n_dp
    both = jnp.zeros((slots, LANES), f32)
    for s in range(n_seg):
        ab = aall[s].astype(f32)
        lat = (ab + both) * lax.rsqrt(jnp.maximum(norm, 0.0) * (1.0 / D) + 1e-06)
        lat = lat.astype(bf16)
        lat_low = jnp.where(lane < RANK, lat.astype(f32), 0.0)
        wide_c = jnp.where(keep, dot(lat_low.astype(bf16), xmap[s]), 0.0).astype(bf16)
        if s == 0:
            ctil[...] = wide_c
        else:
            ctil[...] += wide_c
        if s + 1 < n_seg:
            here = mgall[s // pair, :, s % pair].reshape(known, LANES)
            after = mgall[(s + 1) // pair, :, (s + 1) % pair].reshape(known, LANES)
            self_part = dot(ctil[...], here)
            lat_high = pltpu.roll(lat_low, RANK, 1)
            norm = norm + jnp.sum(lat_high * (2.0 * ab + both + self_part), axis=1, keepdims=True)
            both = dot(ctil[...], after)

    @pl.loop(1, n_dp)
    def _(n):
        u_copy(n).wait_recv()
        h_copy(n).wait_recv()

    sx_sent.wait_recv()
    so_sent.wait_recv()
    table = upall[...].reshape(known, out_half)
    slot = iota((slots, n_dp), 0)
    source = iota((slots, n_dp), 1)
    room = slot - source * cap
    valid = jnp.sum(
        jnp.where((room >= 0) & (room < cap) & (room < counts[...]), 1.0, 0.0), axis=1, keepdims=True
    )
    recip = lax.rsqrt((sxx[:, 0:1] + sxgot[:, 0:1]) * (1.0 / S) + 1e-06)
    target = dot(ctil[...], table) + hgot[...].reshape(slots, out_half).astype(f32)
    out = (sox[:, kept] + sogot[...].astype(f32)) * recip
    diff = jnp.where(valid > 0.0, out - target, 0.0)
    loss = jnp.sum(diff * diff, axis=1, keepdims=True)
    loss_out[...] = jnp.broadcast_to(loss, (slots, LANES)).T[0:1, :]
    gd_out[...] = (diff * (recip * (1.0 / TOK_DEV))).astype(bf16)

    for copy in u_sent + mg_x + a_x + [ab_sent, mg_sent, up_sent, hp_sent, sx_sent, so_sent, mg_swap]:
        copy.wait_send()

    @pl.loop(1, n_dp)
    def _(n):
        a_copy(n).wait_send()
        u_copy(n).wait_send()
        m_copy(n).wait_send()
        h_copy(n).wait_send()


def front(h, ids, dest, counts, gain, down, up, x, sgain, w, p):
    n_seg = lax.axis_size("segment")
    n_dp = lax.axis_size("dp")
    tok, half = h.shape
    slots, width = x.shape
    cols = p.shape[1]
    out_half = cols // 2
    cap = slots // n_dp
    q = RANK // n_dp
    per = TEACH * q
    rows_u = n_seg * per
    known = rows_u * n_dp
    c = np.arange(known)
    c_i, c_t, c_k, c_q = c // rows_u, c % rows_u // per, c % per // q, c % q
    spot = np.arange(LANES)[None, :, None]
    xmap = (np.arange(n_seg)[:, None, None] == c_t) & (spot == c_i * q + c_q)
    xmap = jnp.asarray(xmap.astype(np.float32), dtype=bf16)
    kcol = jnp.asarray(c_k[None, :].astype(np.float32))
    vmem = pl.BlockSpec(memory_space=pltpu.VMEM)
    hbm = pl.BlockSpec(memory_space=pl.ANY)
    flops = 2 * (tok * half * cols + slots * width * cols)
    scratch = [
        (h.shape, bf16), (down.shape, bf16), (up.shape, bf16), (x.shape, bf16), (w.shape, bf16), (p.shape, bf16),
        (xmap.shape, bf16),
        ((rows_u, half // n_seg), bf16), ((n_seg, rows_u, half // n_seg), bf16), ((rows_u, half), bf16),
        ((tok, 2 * LANES), f32), ((tok, 2 * LANES), f32), ((tok, 2 * LANES), f32), ((tok, 2 * LANES), f32),
        ((slots, tok), bf16), ((tok, 2 * LANES), bf16),
        ((n_dp, cap, 2 * LANES), bf16), ((n_dp, cap, 2 * LANES), bf16), ((n_seg, slots, LANES), bf16),
        ((rows_u, LANES), f32), ((rows_u, LANES), f32), ((n_seg, rows_u, LANES), bf16),
        ((2, n_dp, n_seg // 2, rows_u, LANES), bf16),
        ((rows_u, cols), f32), ((rows_u, out_half), f32), ((n_dp, rows_u, out_half), bf16),
        ((tok, cols), f32), ((tok, out_half), bf16), ((tok, out_half), bf16),
        ((n_dp, cap, out_half), bf16), ((n_dp, cap, out_half), bf16),
        (x.shape, bf16), ((slots, cols), f32), ((slots, out_half), bf16), ((slots, out_half), bf16),
        ((slots, LANES), f32), ((slots, LANES), f32), ((slots, known), bf16),
    ]
    sems = [7, 7, 7, 3 * (n_seg - 1), 3 * (n_seg - 1), 4 * (n_dp - 1), 4 * (n_dp - 1)]
    return pl.pallas_call(
        functools.partial(front_kernel, n_seg, n_dp, cap),
        out_shape=(
            jax.ShapeDtypeStruct((slots, out_half), bf16),
            jax.ShapeDtypeStruct((1, slots), f32),
            jax.ShapeDtypeStruct((width, slots), bf16),
        ),
        in_specs=[hbm] * 7 + [vmem] * 6,
        out_specs=(vmem, vmem, vmem),
        scratch_shapes=[pltpu.VMEM(*s) for s in scratch] + [pltpu.SemaphoreType.DMA((n,)) for n in sems],
        compiler_params=pltpu.CompilerParams(
            collective_id=0, has_side_effects=True, vmem_limit_bytes=60 * 2**20
        ),
        cost_estimate=pl.CostEstimate(flops=flops, bytes_accessed=25 * 2**20, transcendentals=0),
    )(
        h, down, up, x, w, p, xmap,
        ids.reshape(1, tok), dest.reshape(1, tok), counts, gain, sgain.reshape(1, width), kcol,
    )


def local(
    teacher_hidden,
    teacher_id,
    destination,
    row_counts,
    section_gain,
    adapter_down,
    adapter_up,
    student_in,
    student_gain,
    student_weight,
    projector,
):
    grad_half, loss_part, sgt = front(
        teacher_hidden,
        teacher_id,
        destination,
        row_counts,
        section_gain,
        adapter_down[0],
        adapter_up[0],
        student_in,
        student_gain,
        student_weight,
        projector,
    )
    weight_grad, row_loss = back(sgt, grad_half, loss_part)
    share, cols = weight_grad.shape
    return (weight_grad.reshape(1, share, cols), row_loss.reshape(student_in.shape[0]))


def solution(mesh):
    placed = (
        P("dp", "mp"),
        P("dp"),
        P("dp"),
        P("dp", None),
        P("segment", "mp"),
        P("segment", "mp", None),
        P("segment", None, "mp"),
        P("dp", "mp"),
        P("mp"),
        P("mp", "segment"),
        P("mp", "segment"),
    )
    return jax.shard_map(
        local,
        mesh=mesh,
        in_specs=placed,
        out_specs=(P("mp", "dp", "segment"), P("dp")),
        check_vma=False,
    )
```

```python
import functools

import jax
import jax.numpy as jnp
import numpy as np
from jax import lax
from jax.experimental import pallas as pl
from jax.experimental.pallas import tpu as pltpu
from jax.sharding import PartitionSpec as P

D = 8192
S = 5120
RANK = 64
TOK_DEV = 256
TEACH = 3
LANES = 128
bf16 = jnp.bfloat16
f32 = jnp.float32


def dot(a, b):
    return jnp.dot(a, b, preferred_element_type=f32)


def remote(src, dst, send, recv, **where):
    return pltpu.make_async_remote_copy(
        src_ref=src,
        dst_ref=dst,
        send_sem=send,
        recv_sem=recv,
        device_id=where,
        device_id_type=pl.DeviceIdType.MESH,
    )


def back_kernel(n_seg, side, sgt, gdh, loss, out, loss_out, gd, part, own, got, part2, got2, losses, ss, rs, ls, lr):
    share = out.shape[0]
    half = gdh.shape[1]
    part_rows = share // 2
    me_s = lax.axis_index("segment")
    me_m = lax.axis_index("mp")
    me_d = lax.axis_index("dp")
    z = me_d // side
    y = me_d % side
    other = 1 - me_m
    y_next = [z * side + (y + step) % side for step in (1, side - 1)]
    z_next = [((z + step) % side) * side + y for step in (1, side - 1)]
    rings = (y_next, z_next)
    places = (y, z)

    barrier = pltpu.get_barrier_semaphore()
    for where in y_next + z_next:
        pl.semaphore_signal(barrier, inc=1, device_id={"dp": where}, device_id_type=pl.DeviceIdType.MESH)
    peers = []
    for ds in range(n_seg):
        for dm in range(2):
            if ds or dm:
                peers.append({"segment": (me_s + ds) % n_seg, "mp": (me_m + dm) % 2})
    for where in peers:
        pl.semaphore_signal(barrier, inc=1, device_id=where, device_id_type=pl.DeviceIdType.MESH)
    pl.semaphore_wait(barrier, 4 + len(peers))

    swap = remote(gdh, gd.at[me_m], ss.at[24], rs.at[24], mp=other)
    swap.start()
    mine = me_s * 2 + me_m
    tells = []
    for n, where in enumerate(peers):
        tell = remote(loss, losses.at[mine], ls.at[n], lr.at[n], **where)
        tell.start()
        tells.append(tell)
    losses[mine] = loss[...]
    gd[me_m] = gdh[...]
    swap.wait()

    def rows(f, g, k):
        block = (k * side + g) if f == 0 else (g * side + k)
        return pl.ds(pl.multiple_of(block * share, share), share)

    def product(f, g, k):
        return jnp.dot(sgt[rows(f, g, k), :], gd[f], preferred_element_type=f32)

    copies = []

    def send(src, dst, number, where):
        copy = remote(src, dst, ss.at[number], rs.at[number], dp=where)
        copy.start()
        copies.append(copy)
        return copy

    first = {}
    for f in (0, 1):
        far = (places[f] + 2) % side

        @pl.loop(0, 2)
        def _(k):
            part[f, 1, k] = product(f, far, k).astype(bf16)

        first[f, 0] = send(part.at[f, 1, 0:2], got.at[f, 0, 0], f * 6 + 0, rings[f][0])

        @pl.loop(2, 4)
        def _(k):
            part[f, 1, k] = product(f, far, k).astype(bf16)

        first[f, 1] = send(part.at[f, 1, 2:4], got.at[f, 1, 0], f * 6 + 3, rings[f][1])
    second = {}
    for f in (0, 1):
        for way in (0, 1):
            near = (places[f] + (1, side - 1)[way]) % side
            low = 2 - 2 * way

            @pl.loop(low, low + 2)
            def _(k):
                part[f, 2 * way, k] = product(f, near, k).astype(bf16)

            second[f, way] = send(part.at[f, 2 * way, low : low + 2], got.at[f, way, 1], f * 6 + 3 * way + 1, rings[f][way])
    third = {}
    for f in (0, 1):
        for way in (0, 1):
            near = (places[f] + (1, side - 1)[way]) % side
            low = 2 * way
            first[f, way].wait_recv()

            @pl.loop(low, low + 2)
            def _(k):
                part[f, 2 * way, k] = (product(f, near, k) + got[f, way, 0, k - low].astype(f32)).astype(bf16)

            third[f, way] = send(part.at[f, 2 * way, low : low + 2], got.at[f, way, 2], f * 6 + 3 * way + 2, rings[f][way])
    for f in (0, 1):

        @pl.loop(0, 4)
        def _(k):
            own[f, k] = product(f, places[f], k)

    first2 = {}
    second2 = {}
    third2 = {}
    for f in (0, 1):
        second[f, 0].wait_recv()
        second[f, 1].wait_recv()

        @pl.loop(0, 2)
        def _(k):
            own[f, k] += got[f, 1, 1, k].astype(f32)
            own[f, k + 2] += got[f, 0, 1, k].astype(f32)

    for f in (0, 1):
        third[f, 0].wait_recv()
        third[f, 1].wait_recv()

        @pl.loop(0, 2)
        def _(k):
            own[f, k] += got[f, 0, 2, k].astype(f32)
            own[f, k + 2] += got[f, 1, 2, k].astype(f32)

        g = 1 - f
        far = (places[g] + 2) % side
        part2[f, 1] = own[f, far].astype(bf16)
        base = 12 + f * 6
        first2[f, 0] = send(part2.at[f, 1, 0:part_rows], got2.at[f, 0, 0], base, rings[g][0])
        first2[f, 1] = send(part2.at[f, 1, part_rows:share], got2.at[f, 1, 0], base + 3, rings[g][1])
        for way in (0, 1):
            near = (places[g] + (1, side - 1)[way]) % side
            low = (1 - way) * part_rows
            part2[f, 2 * way, low : low + part_rows] = own[f, near, low : low + part_rows].astype(bf16)
            second2[f, way] = send(part2.at[f, 2 * way, low : low + part_rows], got2.at[f, way, 1], base + 3 * way + 1, rings[g][way])
    for f in (0, 1):
        g = 1 - f
        base = 12 + f * 6
        for way in (0, 1):
            near = (places[g] + (1, side - 1)[way]) % side
            low = way * part_rows
            first2[f, way].wait_recv()
            part2[f, 2 * way, low : low + part_rows] = (
                own[f, near, low : low + part_rows] + got2[f, way, 0].astype(f32)
            ).astype(bf16)
            third2[f, way] = send(part2.at[f, 2 * way, low : low + part_rows], got2.at[f, way, 2], base + 3 * way + 2, rings[g][way])
    for tell in tells:
        tell.wait()
    total = losses[0]
    for n in range(1, 2 * n_seg):
        total = total + losses[n]
    loss_out[...] = total * (1.0 / S)
    for f in (0, 1):
        g = 1 - f
        for way in (0, 1):
            second2[f, way].wait_recv()
        for way in (0, 1):
            third2[f, way].wait_recv()
        span = slice(f * half, (f + 1) * half)
        top = slice(0, part_rows)
        end = slice(part_rows, share)
        out[top, span] = own[f, places[g], top] + got2[f, 0, 2].astype(f32) + got2[f, 1, 1].astype(f32)
        out[end, span] = own[f, places[g], end] + got2[f, 0, 1].astype(f32) + got2[f, 1, 2].astype(f32)
    for copy in copies:
        copy.wait_send()


def back(sgt, grad_half, loss_part):
    n_seg = lax.axis_size("segment")
    n_dp = lax.axis_size("dp")
    side = 4
    share = sgt.shape[0] // n_dp
    slots, half = grad_half.shape
    half_rows = share // 2
    vmem = pl.BlockSpec(memory_space=pltpu.VMEM)
    flops = 2 * sgt.shape[0] * slots * 2 * half
    return pl.pallas_call(
        functools.partial(back_kernel, n_seg, side),
        out_shape=(
            jax.ShapeDtypeStruct((share, 2 * half), f32),
            jax.ShapeDtypeStruct((1, slots), f32),
        ),
        in_specs=[vmem] * 3,
        out_specs=(vmem, vmem),
        scratch_shapes=[
            pltpu.VMEM((2, slots, half), bf16),
            pltpu.VMEM((2, 3, 4, share, half), bf16),
            pltpu.VMEM((2, 4, share, half), f32),
            pltpu.VMEM((2, 2, 3, 2, share, half), bf16),
            pltpu.VMEM((2, 3, share, half), bf16),
            pltpu.VMEM((2, 2, 3, half_rows, half), bf16),
            pltpu.VMEM((2 * n_seg, 1, slots), f32),
            pltpu.SemaphoreType.DMA((25,)),
            pltpu.SemaphoreType.DMA((25,)),
            pltpu.SemaphoreType.DMA((2 * n_seg - 1,)),
            pltpu.SemaphoreType.DMA((2 * n_seg - 1,)),
        ],
        compiler_params=pltpu.CompilerParams(
            collective_id=1, has_side_effects=True, vmem_limit_bytes=56 * 2**20
        ),
        cost_estimate=pl.CostEstimate(flops=flops, bytes_accessed=8 * 2**20, transcendentals=0),
    )(sgt, grad_half, loss_part)


def iota(shape, dim):
    return lax.broadcasted_iota(jnp.int32, shape, dim)


def ones_where(mask):
    return jnp.where(mask, 1.0, 0.0).astype(bf16)


def dot_nt(a, b):
    return lax.dot_general(a, b, (((1,), (1,)), ((), ())), preferred_element_type=f32)


def turned(row):
    return jnp.broadcast_to(row, (LANES, row.shape[1])).T


def fold(wide, keep):
    kept = jnp.where(keep, wide, 0.0)
    both = kept[:, :LANES] + kept[:, LANES:]
    return both + pltpu.roll(both, RANK, 1)


def front_kernel(
    n_seg, side, cap,
    h_hbm, down_hbm, up_hbm, x_hbm, w_hbm, p_hbm, xmap_hbm,
    ids, dest, counts, gain, sgain, kcol,
    gd_out, loss_out, sgt_out,
    h, down, up, x, w, p, xmap,
    usend, ugot, ucat, wide_a, wide_b, abx, abgot, sel, pay, aslots, agot, aall,
    mgx, mggot, mgs, upx, upgot, blocks, tables,
    hpx, hpsend, hpgot, hslots, hgot,
    sg, sox, sosend, sogot, sxx, sxgot, ctil,
    lsem, s_m, r_m, s_x, r_x, s_d, r_d,
):
    me_s = lax.axis_index("segment")
    me_m = lax.axis_index("mp")
    me_d = lax.axis_index("dp")
    other = 1 - me_m
    n_dp = side * side
    tok, half = h.shape
    slots = x.shape[0]
    cols = p.shape[1]
    out_half = cols // 2
    rows_u = mgx.shape[0]
    per = rows_u // n_seg
    part = half // n_seg
    tile = 2 * LANES
    tiles = cols // tile
    pair = n_seg // 2

    def load(n, src, dst):
        copy = pltpu.make_async_copy(src, dst, lsem.at[n])
        copy.start()
        return copy

    def p_copy(n):
        span = pl.ds(pl.multiple_of(n * tile, tile), tile)
        return pltpu.make_async_copy(p_hbm.at[:, span], p.at[:, span], lsem.at[5 + n])

    def w_copy(n):
        span = pl.ds(pl.multiple_of(n * tile, tile), tile)
        return pltpu.make_async_copy(w_hbm.at[:, span], w.at[:, span], lsem.at[5 + tiles + n])

    up_in = load(0, up_hbm, up)
    h_in = load(1, h_hbm, h)
    for n in range(tiles):
        p_copy(n).start()
    down_in = load(2, down_hbm, down)
    x_in = load(3, x_hbm, x)
    for n in range(tiles):
        w_copy(n).start()
    xmap_in = load(4, xmap_hbm, xmap)

    barrier = pltpu.get_barrier_semaphore()
    mesh_id = pl.DeviceIdType.MESH
    pl.semaphore_signal(barrier, inc=1, device_id={"mp": other}, device_id_type=mesh_id)
    for n in range(1, n_seg):
        pl.semaphore_signal(barrier, inc=1, device_id={"segment": (me_s + n) % n_seg}, device_id_type=mesh_id)

    @pl.loop(1, n_dp)
    def _(n):
        pl.semaphore_signal(barrier, inc=1, device_id={"dp": (me_d + n) % n_dp}, device_id_type=mesh_id)

    def to_peer(n, src, dst):
        return remote(src, dst, s_m.at[n], r_m.at[n], mp=other)

    def to_seg(kind, n, src, dst):
        number = kind * (n_seg - 1) + n - 1
        return remote(src, dst, s_x.at[number], r_x.at[number], segment=(me_s + n) % n_seg)

    def to_dp(kind, n, src, dst):
        number = kind * (n_dp - 1) + n - 1
        return remote(src, dst, s_d.at[number], r_d.at[number], dp=(me_d + n) % n_dp)

    z = me_d // side
    y = me_d % side

    def place(first, second):
        a = ((z * other + y * me_m) + second) % side
        b = ((y * other + z * me_m) + first) % side
        return (a * other + b * me_m) * side + b * other + a * me_m

    def gather_first(n):
        return remote(blocks.at[me_d], blocks.at[me_d], s_d.at[n + 29], r_d.at[n + 29], dp=place(n, 0))

    def gather_second(k, n):
        source = place(side - k, 0)
        number = 33 + k * (side - 1) + n - 1
        return remote(blocks.at[source], blocks.at[source], s_d.at[number], r_d.at[number], dp=place(0, n))

    packed = n_seg * per
    row = iota((packed, up.shape[0]), 0)
    col = iota((packed, up.shape[0]), 1)
    quad = row >> 2
    block = (quad >= 3).astype(jnp.int32) + (quad >= 6).astype(jnp.int32) + (quad >= 9).astype(jnp.int32)
    teacher = quad - 3 * block
    hit = ((col >> 6) == teacher) & (((col & 63) >> 2) == me_d) & ((col & 3) == (row & 3))
    up_in.wait()
    mine = jnp.zeros((packed, part), f32)
    for g in range(n_seg):
        mine = mine + dot(ones_where(hit & (block == g)), up[:, g * part : (g + 1) * part])
    usend[...] = mine.astype(bf16)
    ugot[me_s] = usend[...]
    pl.semaphore_wait(barrier, 1 + (n_seg - 1) + (n_dp - 1))
    u_sent = [to_seg(0, n, usend, ugot.at[me_s]) for n in range(1, n_seg)]
    for copy in u_sent:
        copy.start()

    dest_f = dest[...].astype(f32)
    onehot = jnp.where(iota((n_dp, tok), 0).astype(f32) == dest_f, 1.0, 0.0)
    before = ones_where(iota((tok, tok), 0) < iota((tok, tok), 1))
    earlier = dot(onehot.astype(bf16), before)
    position = dest_f * cap + jnp.sum(earlier * onehot, axis=0, keepdims=True)
    sel[...] = ones_where(iota((slots, tok), 0).astype(f32) == position)
    wide_a[...] = jnp.zeros(wide_a.shape, f32)
    wide_b[...] = jnp.zeros(wide_b.shape, f32)
    abx[...] = jnp.zeros(abx.shape, f32)

    away = pl.ds(pl.multiple_of(other * out_half, LANES), out_half)
    kept = pl.ds(pl.multiple_of(me_m * out_half, LANES), out_half)
    h_in.wait()

    @pl.loop(0, tiles)
    def _(n):
        span = pl.ds(pl.multiple_of(n * tile, tile), tile)
        p_copy(n).wait()
        hpx[:, span] = dot(h[...], p[:, span])

    hpsend[...] = hpx[:, away].astype(bf16)
    hp_sent = to_peer(3, hpsend, hpgot)
    hp_sent.start()

    for copy in u_sent:
        copy.wait_recv()
    row = iota((packed, n_seg * packed), 0)
    col = iota((packed, n_seg * packed), 1)
    quad = row >> 2
    block = (quad >= 3).astype(jnp.int32) + (quad >= 6).astype(jnp.int32) + (quad >= 9).astype(jnp.int32)
    got_u = ugot[...].reshape(n_seg * packed, part)
    for g in range(n_seg):
        take = ones_where(col == row + (packed - per) * block + per * g)
        ucat[:, g * part : (g + 1) * part] = dot(take, got_u).astype(bf16)
    down_in.wait()
    rank_all = down.shape[0]
    u = ucat[...]
    u_scaled = (u.astype(f32) * gain[...].astype(f32)).astype(bf16)
    wide_a[:rows_u, :rank_all] = dot_nt(u_scaled, down[...])
    wide_b[:rows_u, :rank_all] = dot_nt(u, up[...])
    row = iota((rows_u, 2 * LANES), 0)
    quad = row >> 2
    block = (quad >= 3).astype(jnp.int32) + (quad >= 6).astype(jnp.int32) + (quad >= 9).astype(jnp.int32)
    same = (quad - 3 * block) == (iota((rows_u, 2 * LANES), 1) >> 6)
    lane_u = iota((rows_u, LANES), 1)
    mgx[...] = jnp.where(lane_u < RANK, fold(wide_a[:rows_u, :], same), fold(wide_b[:rows_u, :], same))
    mg_sent = to_peer(1, mgx, mggot)
    mg_sent.start()

    @pl.loop(0, tiles)
    def _(n):
        span = pl.ds(pl.multiple_of(n * tile, tile), tile)
        upx[:, span] = dot(ucat[...], p[:, span])

    up_sent = to_peer(2, upx.at[:, away], upgot)
    up_sent.start()
    mg_sent.wait_recv()
    mgs[me_s] = (mgx[...] + mggot[...]).astype(bf16)
    mg_x = [to_seg(1, n, mgs.at[me_s], mgs.at[me_s]) for n in range(1, n_seg)]
    for copy in mg_x:
        copy.start()

    hp_sent.wait_recv()
    hp = (hpx[:, kept] + hpgot[...].astype(f32)).astype(bf16)
    hslots[...] = dot(sel[...], hp).astype(bf16).reshape(hslots.shape)
    hgot[me_d] = hslots[me_d]

    def h_copy(n):
        return to_dp(1, n, hslots.at[(me_d + n) % n_dp], hgot.at[me_d])

    @pl.loop(1, n_dp)
    def _(n):
        h_copy(n).start()

    wide_a[:rows_u, :] = jnp.zeros((rows_u, 2 * LANES), f32)
    wide_b[:rows_u, :] = jnp.zeros((rows_u, 2 * LANES), f32)

    @pl.loop(0, n_seg)
    def _(g):
        span = pl.ds(pl.multiple_of(g * part, part), part)
        here = h[:, span]
        wide = here.astype(f32)
        scaled = (wide * gain[:, span].astype(f32)).astype(bf16)
        wide_a[:, :rank_all] += dot_nt(scaled, down[:, span])
        wide_b[:, :rank_all] += dot_nt(here, up[:, span])
        abx[:, LANES:] += jnp.broadcast_to(jnp.sum(wide * wide, axis=1, keepdims=True), (tok, LANES))

    id_col = turned(ids[...].astype(f32))
    lane2 = iota((tok, 2 * LANES), 1)
    own = (lane2 >> 6).astype(f32) == jnp.concatenate([id_col, id_col], axis=1)
    lane = iota((tok, LANES), 1)
    abx[:, :LANES] = jnp.where(lane < RANK, fold(wide_a[...], own), fold(wide_b[...], own))
    ab_sent = to_peer(0, abx, abgot)
    ab_sent.start()

    up_sent.wait_recv()
    blocks[me_d, :, :out_half] = (upx[:, kept] + upgot[...]).astype(bf16)
    for copy in mg_x:
        copy.wait_recv()
    for n in range(pair):
        low = out_half + n * LANES
        blocks[me_d, :, low : low + LANES] = mgs[me_m * pair + n]
    firsts = [gather_first(n) for n in range(1, side)]
    for copy in firsts:
        copy.start()
    seconds = [gather_second(0, n) for n in range(1, side)]
    for copy in seconds:
        copy.start()

    ab_sent.wait_recv()
    total = abx[...] + abgot[...]
    sq = total[:, LANES:]
    sq_hi = sq.astype(bf16).astype(f32)
    extra = jnp.where(lane == 0, id_col, jnp.where(lane == 1, sq_hi, jnp.where(lane == 2, sq - sq_hi, 0.0)))
    pay[:, :LANES] = total[:, :LANES].astype(bf16)
    pay[:, LANES:] = extra.astype(bf16)
    lanes_here = pl.ds(pl.multiple_of(me_m * LANES, LANES), LANES)
    aslots[...] = dot(sel[...], pay[:, lanes_here]).astype(bf16).reshape(aslots.shape)
    agot[me_m, me_d] = aslots[me_d]

    def a_copy(n):
        return to_dp(0, n, aslots.at[(me_d + n) % n_dp], agot.at[me_m, me_d])

    @pl.loop(1, n_dp)
    def _(n):
        a_copy(n).start()

    x_in.wait()
    sxx[...] = jnp.zeros(sxx.shape, f32)

    @pl.loop(0, x.shape[1] // LANES)
    def _(n):
        span = pl.ds(pl.multiple_of(n * LANES, LANES), LANES)
        wide = x[:, span].astype(f32)
        sxx[...] += wide * wide
        sg[:, span] = (wide * sgain[pl.ds(n, 1), :]).astype(bf16)

    sx_sent = to_peer(4, sxx, sxgot)
    sx_sent.start()
    for k in range(1, side):
        firsts[k - 1].wait_recv()
        for n in range(1, side):
            copy = gather_second(k, n)
            copy.start()
            seconds.append(copy)

    def student(n):
        span = pl.ds(pl.multiple_of(n * tile, tile), tile)
        w_copy(n).wait()
        sox[:, span] = dot(sg[...], w[:, span])

    pl.loop(0, tiles // 2)(student)

    @pl.loop(1, n_dp)
    def _(n):
        a_copy(n).wait_recv()

    a_x = [to_seg(2, n, aall.at[me_s], aall.at[me_s]) for n in range(1, n_seg)]
    extra_swap = to_peer(6, agot.at[1], agot.at[1])

    @pl.when(me_m == 0)
    def _():
        aall[me_s] = agot[0].reshape(slots, LANES)
        for copy in a_x:
            copy.start()

    @pl.when(me_m == 1)
    def _():
        extra_swap.start()

    pl.loop(tiles // 2, tiles)(student)
    sosend[...] = sox[:, away].astype(bf16)
    so_sent = to_peer(5, sosend, sogot)
    so_sent.start()
    a_swap = to_peer(7, aall, aall)

    @pl.when(me_m == 0)
    def _():
        for copy in a_x:
            copy.wait_recv()
        a_swap.start()

    @pl.loop(0, x.shape[1] // LANES)
    def _(n):
        span = pl.ds(pl.multiple_of(n * LANES, LANES), LANES)
        sgt_out[span, :] = sg[:, span].T

    for copy in seconds:
        copy.wait_recv()
    tables[me_m] = blocks[:, :, out_half:]
    table_swap = to_peer(8, tables.at[me_m], tables.at[me_m])
    table_swap.start()

    @pl.when(me_m == 0)
    def _():
        extra_swap.wait_recv()

    @pl.when(me_m == 1)
    def _():
        a_swap.wait_recv()

    xmap_in.wait()
    extra = agot[1].reshape(slots, LANES).astype(f32)
    id_slot = extra[:, 0:1]
    norm = extra[:, 1:2] + extra[:, 2:3]
    keep = kcol[...] == id_slot
    lane = iota((slots, LANES), 1)
    known = rows_u * n_dp
    both = jnp.zeros((slots, LANES), f32)
    table_swap.wait_recv()
    for s in range(n_seg):
        ab = aall[s].astype(f32)
        lat = (ab + both) * lax.rsqrt(jnp.maximum(norm, 0.0) * (1.0 / D) + 1e-06)
        lat = lat.astype(bf16)
        lat_low = jnp.where(lane < RANK, lat.astype(f32), 0.0)
        wide_c = jnp.where(keep, dot(lat_low.astype(bf16), xmap[s]), 0.0).astype(bf16)
        if s == 0:
            ctil[...] = wide_c
        else:
            ctil[...] += wide_c
        if s + 1 < n_seg:
            low, high = (s % pair) * LANES, ((s + 1) % pair) * LANES
            here = tables[s // pair, :, :, low : low + LANES].reshape(known, LANES)
            after = tables[(s + 1) // pair, :, :, high : high + LANES].reshape(known, LANES)
            self_part = dot(ctil[...], here)
            lat_high = pltpu.roll(lat_low, RANK, 1)
            norm = norm + jnp.sum(lat_high * (2.0 * ab + both + self_part), axis=1, keepdims=True)
            both = dot(ctil[...], after)

    @pl.loop(1, n_dp)
    def _(n):
        h_copy(n).wait_recv()

    sx_sent.wait_recv()
    so_sent.wait_recv()
    table = blocks[:, :, :out_half].reshape(known, out_half)
    slot = iota((slots, n_dp), 0)
    source = iota((slots, n_dp), 1)
    room = slot - source * cap
    valid = jnp.sum(
        jnp.where((room >= 0) & (room < cap) & (room < counts[...]), 1.0, 0.0), axis=1, keepdims=True
    )
    square = jnp.sum(sxx[...] + sxgot[...], axis=1, keepdims=True)
    recip = lax.rsqrt(square * (1.0 / S) + 1e-06)
    target = dot(ctil[...], table) + hgot[...].reshape(slots, out_half).astype(f32)
    out = (sox[:, kept] + sogot[...].astype(f32)) * recip
    diff = jnp.where(valid > 0.0, out - target, 0.0)
    loss = jnp.sum(diff * diff, axis=1, keepdims=True)
    loss_out[...] = jnp.broadcast_to(loss, (slots, LANES)).T[0:1, :]
    gd_out[...] = (diff * (recip * (1.0 / TOK_DEV))).astype(bf16)

    for copy in u_sent + mg_x + firsts + seconds + [ab_sent, mg_sent, up_sent, hp_sent, sx_sent, so_sent, table_swap]:
        copy.wait_send()

    @pl.when(me_m == 0)
    def _():
        for copy in a_x + [a_swap]:
            copy.wait_send()

    @pl.when(me_m == 1)
    def _():
        extra_swap.wait_send()

    @pl.loop(1, n_dp)
    def _(n):
        a_copy(n).wait_send()
        h_copy(n).wait_send()


def front(h, ids, dest, counts, gain, down, up, x, sgain, w, p):
    side = 4
    n_seg = lax.axis_size("segment")
    n_dp = lax.axis_size("dp")
    tok, half = h.shape
    slots, width = x.shape
    cols = p.shape[1]
    out_half = cols // 2
    cap = slots // n_dp
    q = RANK // n_dp
    per = TEACH * q
    rows_u = n_seg * per
    known = rows_u * n_dp
    c = np.arange(known)
    c_i, c_t, c_k, c_q = c // rows_u, c % rows_u // per, c % per // q, c % q
    spot = np.arange(LANES)[None, :, None]
    xmap = (np.arange(n_seg)[:, None, None] == c_t) & (spot == c_i * q + c_q)
    xmap = jnp.asarray(xmap.astype(np.float32), dtype=bf16)
    kcol = jnp.asarray(c_k[None, :].astype(np.float32))
    vmem = pl.BlockSpec(memory_space=pltpu.VMEM)
    hbm = pl.BlockSpec(memory_space=pl.ANY)
    flops = 2 * (tok * half * cols + slots * width * cols)
    scratch = [
        (h.shape, bf16), (down.shape, bf16), (up.shape, bf16), (x.shape, bf16), (w.shape, bf16), (p.shape, bf16),
        (xmap.shape, bf16),
        ((rows_u, half // n_seg), bf16), ((n_seg, rows_u, half // n_seg), bf16), ((rows_u, half), bf16),
        ((tok, 2 * LANES), f32), ((tok, 2 * LANES), f32), ((tok, 2 * LANES), f32), ((tok, 2 * LANES), f32),
        ((slots, tok), bf16), ((tok, 2 * LANES), bf16),
        ((n_dp, cap, LANES), bf16), ((2, n_dp, cap, LANES), bf16), ((n_seg, slots, LANES), bf16),
        ((rows_u, LANES), f32), ((rows_u, LANES), f32), ((n_seg, rows_u, LANES), bf16),
        ((rows_u, cols), f32), ((rows_u, out_half), f32),
        ((n_dp, rows_u, out_half + n_seg // 2 * LANES), bf16), ((2, n_dp, rows_u, n_seg // 2 * LANES), bf16),
        ((tok, cols), f32), ((tok, out_half), bf16), ((tok, out_half), bf16),
        ((n_dp, cap, out_half), bf16), ((n_dp, cap, out_half), bf16),
        (x.shape, bf16), ((slots, cols), f32), ((slots, out_half), bf16), ((slots, out_half), bf16),
        ((slots, LANES), f32), ((slots, LANES), f32), ((slots, known), bf16),
    ]
    sems = [5 + cols // LANES, 9, 9, 3 * (n_seg - 1), 3 * (n_seg - 1), 3 * (n_dp - 1), 3 * (n_dp - 1)]
    return pl.pallas_call(
        functools.partial(front_kernel, n_seg, side, cap),
        out_shape=(
            jax.ShapeDtypeStruct((slots, out_half), bf16),
            jax.ShapeDtypeStruct((1, slots), f32),
            jax.ShapeDtypeStruct((width, slots), bf16),
        ),
        in_specs=[hbm] * 7 + [vmem] * 6,
        out_specs=(vmem, vmem, vmem),
        scratch_shapes=[pltpu.VMEM(*s) for s in scratch] + [pltpu.SemaphoreType.DMA((n,)) for n in sems],
        compiler_params=pltpu.CompilerParams(
            collective_id=0, has_side_effects=True, vmem_limit_bytes=60 * 2**20
        ),
        cost_estimate=pl.CostEstimate(flops=flops, bytes_accessed=25 * 2**20, transcendentals=0),
    )(
        h, down, up, x, w, p, xmap,
        ids.reshape(1, tok), dest.reshape(1, tok), counts, gain, sgain.reshape(width // LANES, LANES), kcol,
    )


def local(
    teacher_hidden,
    teacher_id,
    destination,
    row_counts,
    section_gain,
    adapter_down,
    adapter_up,
    student_in,
    student_gain,
    student_weight,
    projector,
):
    grad_half, loss_part, sgt = front(
        teacher_hidden,
        teacher_id,
        destination,
        row_counts,
        section_gain,
        adapter_down[0].T,
        adapter_up[0],
        student_in,
        student_gain,
        student_weight,
        projector,
    )
    weight_grad, row_loss = back(sgt, grad_half, loss_part)
    share, cols = weight_grad.shape
    return (weight_grad.reshape(1, share, cols), row_loss.reshape(student_in.shape[0]))


def solution(mesh):
    placed = (
        P("dp", "mp"),
        P("dp"),
        P("dp"),
        P("dp", None),
        P("segment", "mp"),
        P("segment", "mp", None),
        P("segment", None, "mp"),
        P("dp", "mp"),
        P("mp"),
        P("mp", "segment"),
        P("mp", "segment"),
    )
    return jax.shard_map(
        local,
        mesh=mesh,
        in_specs=placed,
        out_specs=(P("mp", "dp", "segment"), P("dp")),
        check_vma=False,
    )
```

```python
import functools

import jax
import jax.numpy as jnp
import numpy as np
from jax import lax
from jax.experimental import pallas as pl
from jax.experimental.pallas import tpu as pltpu
from jax.sharding import PartitionSpec as P

D = 8192
S = 5120
RANK = 64
TOK_DEV = 256
TEACH = 3
LANES = 128
bf16 = jnp.bfloat16
f32 = jnp.float32


def dot(a, b):
    return jnp.dot(a, b, preferred_element_type=f32)


def remote(src, dst, send, recv, **where):
    return pltpu.make_async_remote_copy(
        src_ref=src,
        dst_ref=dst,
        send_sem=send,
        recv_sem=recv,
        device_id=where,
        device_id_type=pl.DeviceIdType.MESH,
    )


def iota(shape, dim):
    return lax.broadcasted_iota(jnp.int32, shape, dim)


def ones_where(mask):
    return jnp.where(mask, 1.0, 0.0).astype(bf16)


def dot_nt(a, b):
    return lax.dot_general(a, b, (((1,), (1,)), ((), ())), preferred_element_type=f32)


def turned(row):
    return jnp.broadcast_to(row, (LANES, row.shape[1])).T


def fold(wide, keep):
    kept = jnp.where(keep, wide, 0.0)
    both = kept[:, :LANES] + kept[:, LANES:]
    return both + pltpu.roll(both, RANK, 1)


def step_kernel(
    n_seg, side, cap,
    h_hbm, down_hbm, up_hbm, x_hbm, w_hbm, p_hbm, xmap_hbm,
    ids, dest, counts, gain, sgain, kcol,
    out, loss_out,
    h, down, up, x, w, p, xmap,
    usend, ugot, ucat, wide_a, wide_b, abx, abgot, sel, pay, aslots, agot, aall,
    mgx, mggot, mgs, upx, upgot, blocks, tables,
    hpx, hpsend, hpgot, hslots, hgot,
    sg, sox, sosend, sogot, sxx, sxgot, ctil,
    sgt, gd, held, part2, got2, losspart, lossgot, losses,
    lsem, s_m, r_m, s_x, r_x, s_d, r_d, s_r, r_r,
):
    me_s = lax.axis_index("segment")
    me_m = lax.axis_index("mp")
    me_d = lax.axis_index("dp")
    other = 1 - me_m
    n_dp = side * side
    tok, half = h.shape
    slots = x.shape[0]
    cols = p.shape[1]
    out_half = cols // 2
    rows_u = mgx.shape[0]
    per = rows_u // n_seg
    part = half // n_seg
    tile = 2 * LANES
    tiles = cols // tile
    pair = n_seg // 2

    def load(n, src, dst):
        copy = pltpu.make_async_copy(src, dst, lsem.at[n])
        copy.start()
        return copy

    def p_copy(n):
        span = pl.ds(pl.multiple_of(n * tile, tile), tile)
        return pltpu.make_async_copy(p_hbm.at[:, span], p.at[:, span], lsem.at[5 + n])

    def w_copy(n):
        span = pl.ds(pl.multiple_of(n * tile, tile), tile)
        return pltpu.make_async_copy(w_hbm.at[:, span], w.at[:, span], lsem.at[5 + tiles + n])

    up_in = load(0, up_hbm, up)
    h_in = load(1, h_hbm, h)
    for n in range(tiles):
        p_copy(n).start()
    down_in = load(2, down_hbm, down)
    x_in = load(3, x_hbm, x)
    for n in range(tiles):
        w_copy(n).start()
    xmap_in = load(4, xmap_hbm, xmap)

    barrier = pltpu.get_barrier_semaphore()
    mesh_id = pl.DeviceIdType.MESH
    pl.semaphore_signal(barrier, inc=1, device_id={"mp": other}, device_id_type=mesh_id)
    for n in range(1, n_seg):
        pl.semaphore_signal(barrier, inc=1, device_id={"segment": (me_s + n) % n_seg}, device_id_type=mesh_id)

    @pl.loop(1, n_dp)
    def _(n):
        pl.semaphore_signal(barrier, inc=1, device_id={"dp": (me_d + n) % n_dp}, device_id_type=mesh_id)

    def to_peer(n, src, dst):
        return remote(src, dst, s_m.at[n], r_m.at[n], mp=other)

    def to_seg(kind, n, src, dst):
        number = kind * (n_seg - 1) + n - 1
        return remote(src, dst, s_x.at[number], r_x.at[number], segment=(me_s + n) % n_seg)

    def to_dp(kind, n, src, dst):
        number = kind * (n_dp - 1) + n - 1
        return remote(src, dst, s_d.at[number], r_d.at[number], dp=(me_d + n) % n_dp)

    z = me_d // side
    y = me_d % side

    def place(first, second):
        a = ((z * other + y * me_m) + second) % side
        b = ((y * other + z * me_m) + first) % side
        return (a * other + b * me_m) * side + b * other + a * me_m

    def gather_first(n):
        return remote(blocks.at[me_d], blocks.at[me_d], s_d.at[n + 29], r_d.at[n + 29], dp=place(n, 0))

    def gather_second(k, n):
        source = place(side - k, 0)
        number = 33 + k * (side - 1) + n - 1
        return remote(blocks.at[source], blocks.at[source], s_d.at[number], r_d.at[number], dp=place(0, n))

    packed = n_seg * per
    row = iota((packed, up.shape[0]), 0)
    col = iota((packed, up.shape[0]), 1)
    quad = row >> 2
    block = (quad >= 3).astype(jnp.int32) + (quad >= 6).astype(jnp.int32) + (quad >= 9).astype(jnp.int32)
    teacher = quad - 3 * block
    hit = ((col >> 6) == teacher) & (((col & 63) >> 2) == me_d) & ((col & 3) == (row & 3))
    up_in.wait()
    mine = jnp.zeros((packed, part), f32)
    for g in range(n_seg):
        mine = mine + dot(ones_where(hit & (block == g)), up[:, g * part : (g + 1) * part])
    usend[...] = mine.astype(bf16)
    ugot[me_s] = usend[...]
    dest_f = dest[...].astype(f32)
    onehot = jnp.where(iota((n_dp, tok), 0).astype(f32) == dest_f, 1.0, 0.0)
    before = ones_where(iota((tok, tok), 0) < iota((tok, tok), 1))
    earlier = dot(onehot.astype(bf16), before)
    position = dest_f * cap + jnp.sum(earlier * onehot, axis=0, keepdims=True)
    sel[...] = ones_where(iota((slots, tok), 0).astype(f32) == position)
    wide_a[...] = jnp.zeros(wide_a.shape, f32)
    wide_b[...] = jnp.zeros(wide_b.shape, f32)
    abx[...] = jnp.zeros(abx.shape, f32)

    pl.semaphore_wait(barrier, 1 + (n_seg - 1) + (n_dp - 1))
    u_sent = [to_seg(0, n, usend, ugot.at[me_s]) for n in range(1, n_seg)]
    for copy in u_sent:
        copy.start()

    away = pl.ds(pl.multiple_of(other * out_half, LANES), out_half)
    kept = pl.ds(pl.multiple_of(me_m * out_half, LANES), out_half)
    h_in.wait()

    @pl.loop(0, tiles)
    def _(n):
        span = pl.ds(pl.multiple_of(n * tile, tile), tile)
        p_copy(n).wait()
        hpx[:, span] = dot(h[...], p[:, span])

    hpsend[...] = hpx[:, away].astype(bf16)
    hp_sent = to_peer(3, hpsend, hpgot)
    hp_sent.start()

    down_in.wait()
    rank_all = down.shape[0]

    @pl.loop(0, n_seg)
    def _(g):
        span = pl.ds(pl.multiple_of(g * part, part), part)
        here = h[:, span]
        wide = here.astype(f32)
        scaled = (wide * gain[:, span].astype(f32)).astype(bf16)
        wide_a[:, :rank_all] += dot_nt(scaled, down[:, span])
        wide_b[:, :rank_all] += dot_nt(here, up[:, span])
        abx[:, LANES:] += jnp.broadcast_to(jnp.sum(wide * wide, axis=1, keepdims=True), (tok, LANES))

    id_col = turned(ids[...].astype(f32))
    lane2 = iota((tok, 2 * LANES), 1)
    own = (lane2 >> 6).astype(f32) == jnp.concatenate([id_col, id_col], axis=1)
    lane = iota((tok, LANES), 1)
    abx[:, :LANES] = jnp.where(lane < RANK, fold(wide_a[...], own), fold(wide_b[...], own))
    ab_sent = to_peer(0, abx, abgot)
    ab_sent.start()

    hp_sent.wait_recv()
    hp = (hpx[:, kept] + hpgot[...].astype(f32)).astype(bf16)
    hslots[...] = dot(sel[...], hp).astype(bf16).reshape(hslots.shape)
    hgot[me_d] = hslots[me_d]

    def h_copy(n):
        return to_dp(1, n, hslots.at[(me_d + n) % n_dp], hgot.at[me_d])

    @pl.loop(1, n_dp)
    def _(n):
        h_copy(n).start()

    for copy in u_sent:
        copy.wait_recv()
    row = iota((packed, n_seg * packed), 0)
    col = iota((packed, n_seg * packed), 1)
    quad = row >> 2
    block = (quad >= 3).astype(jnp.int32) + (quad >= 6).astype(jnp.int32) + (quad >= 9).astype(jnp.int32)
    got_u = ugot[...].reshape(n_seg * packed, part)
    for g in range(n_seg):
        take = ones_where(col == row + (packed - per) * block + per * g)
        ucat[:, g * part : (g + 1) * part] = dot(take, got_u).astype(bf16)
    u = ucat[...]
    u_scaled = (u.astype(f32) * gain[...].astype(f32)).astype(bf16)
    wide_a[:rows_u, :rank_all] = dot_nt(u_scaled, down[...])
    wide_b[:rows_u, :rank_all] = dot_nt(u, up[...])
    row = iota((rows_u, 2 * LANES), 0)
    quad = row >> 2
    block = (quad >= 3).astype(jnp.int32) + (quad >= 6).astype(jnp.int32) + (quad >= 9).astype(jnp.int32)
    same = (quad - 3 * block) == (iota((rows_u, 2 * LANES), 1) >> 6)
    lane_u = iota((rows_u, LANES), 1)
    mgx[...] = jnp.where(lane_u < RANK, fold(wide_a[:rows_u, :], same), fold(wide_b[:rows_u, :], same))
    mg_sent = to_peer(1, mgx, mggot)
    mg_sent.start()

    ab_sent.wait_recv()
    total = abx[...] + abgot[...]
    sq = total[:, LANES:]
    sq_hi = sq.astype(bf16).astype(f32)
    extra = jnp.where(lane == 0, id_col, jnp.where(lane == 1, sq_hi, jnp.where(lane == 2, sq - sq_hi, 0.0)))
    pay[:, :LANES] = total[:, :LANES].astype(bf16)
    pay[:, LANES:] = extra.astype(bf16)
    lanes_here = pl.ds(pl.multiple_of(me_m * LANES, LANES), LANES)
    aslots[...] = dot(sel[...], pay[:, lanes_here]).astype(bf16).reshape(aslots.shape)
    agot[me_m, me_d] = aslots[me_d]

    def a_copy(n):
        return to_dp(0, n, aslots.at[(me_d + n) % n_dp], agot.at[me_m, me_d])

    @pl.loop(1, n_dp)
    def _(n):
        a_copy(n).start()

    mg_sent.wait_recv()
    mgs[me_s] = (mgx[...] + mggot[...]).astype(bf16)
    mg_x = [to_seg(1, n, mgs.at[me_s], mgs.at[me_s]) for n in range(1, n_seg)]
    for copy in mg_x:
        copy.start()

    @pl.loop(0, tiles)
    def _(n):
        span = pl.ds(pl.multiple_of(n * tile, tile), tile)
        upx[:, span] = dot(ucat[...], p[:, span])

    up_sent = to_peer(2, upx.at[:, away], upgot)
    up_sent.start()
    x_in.wait()
    sxx[...] = jnp.zeros(sxx.shape, f32)

    @pl.loop(0, x.shape[1] // LANES)
    def _(n):
        span = pl.ds(pl.multiple_of(n * LANES, LANES), LANES)
        wide = x[:, span].astype(f32)
        sxx[...] += wide * wide
        sg[:, span] = (wide * sgain[pl.ds(n, 1), :]).astype(bf16)

    sx_sent = to_peer(4, sxx, sxgot)
    sx_sent.start()
    up_sent.wait_recv()
    blocks[me_d, :, :out_half] = (upx[:, kept] + upgot[...]).astype(bf16)
    for copy in mg_x:
        copy.wait_recv()
    for n in range(pair):
        low = out_half + n * LANES
        blocks[me_d, :, low : low + LANES] = mgs[me_m * pair + n]
    firsts = [gather_first(n) for n in range(1, side)]
    for copy in firsts:
        copy.start()
    seconds = [gather_second(0, n) for n in range(1, side)]
    for copy in seconds:
        copy.start()

    def student(n):
        span = pl.ds(pl.multiple_of(n * tile, tile), tile)
        w_copy(n).wait()
        sox[:, span] = dot(sg[...], w[:, span])

    pl.loop(0, 2)(student)

    @pl.loop(1, n_dp)
    def _(n):
        a_copy(n).wait_recv()

    a_x = [to_seg(2, n, aall.at[me_s], aall.at[me_s]) for n in range(1, n_seg)]
    extra_swap = to_peer(6, agot.at[1], agot.at[1])

    @pl.when(me_m == 0)
    def _():
        aall[me_s] = agot[0].reshape(slots, LANES)
        for copy in a_x:
            copy.start()

    @pl.when(me_m == 1)
    def _():
        extra_swap.start()

    pl.loop(2, 3)(student)
    for k in range(1, side):
        firsts[k - 1].wait_recv()
        for n in range(1, side):
            copy = gather_second(k, n)
            copy.start()
            seconds.append(copy)


    pl.loop(3, tiles)(student)
    sosend[...] = sox[:, away].astype(bf16)
    so_sent = to_peer(5, sosend, sogot)
    so_sent.start()
    a_swap = to_peer(7, aall, aall)

    @pl.when(me_m == 0)
    def _():
        for copy in a_x:
            copy.wait_recv()
        a_swap.start()

    @pl.loop(0, x.shape[1] // LANES)
    def _(n):
        span = pl.ds(pl.multiple_of(n * LANES, LANES), LANES)
        sgt[span, :] = sg[:, span].T

    for copy in seconds:
        copy.wait_recv()
    tables[me_m] = blocks[:, :, out_half:]
    table_swap = to_peer(8, tables.at[me_m], tables.at[me_m])
    table_swap.start()

    @pl.when(me_m == 0)
    def _():
        extra_swap.wait_recv()

    @pl.when(me_m == 1)
    def _():
        a_swap.wait_recv()

    xmap_in.wait()
    extra = agot[1].reshape(slots, LANES).astype(f32)
    id_slot = extra[:, 0:1]
    norm = extra[:, 1:2] + extra[:, 2:3]
    keep = kcol[...] == id_slot
    lane = iota((slots, LANES), 1)
    known = rows_u * n_dp
    both = jnp.zeros((slots, LANES), f32)
    table_swap.wait_recv()
    for s in range(n_seg):
        ab = aall[s].astype(f32)
        lat = (ab + both) * lax.rsqrt(jnp.maximum(norm, 0.0) * (1.0 / D) + 1e-06)
        lat = lat.astype(bf16)
        lat_low = jnp.where(lane < RANK, lat.astype(f32), 0.0)
        wide_c = jnp.where(keep, dot(lat_low.astype(bf16), xmap[s]), 0.0).astype(bf16)
        if s == 0:
            ctil[...] = wide_c
        else:
            ctil[...] += wide_c
        if s + 1 < n_seg:
            low, high = (s % pair) * LANES, ((s + 1) % pair) * LANES
            here = tables[s // pair, :, :, low : low + LANES].reshape(known, LANES)
            after = tables[(s + 1) // pair, :, :, high : high + LANES].reshape(known, LANES)
            self_part = dot(ctil[...], here)
            lat_high = pltpu.roll(lat_low, RANK, 1)
            norm = norm + jnp.sum(lat_high * (2.0 * ab + both + self_part), axis=1, keepdims=True)
            both = dot(ctil[...], after)

    @pl.loop(1, n_dp)
    def _(n):
        h_copy(n).wait_recv()

    sx_sent.wait_recv()
    so_sent.wait_recv()
    table = blocks[:, :, :out_half].reshape(known, out_half)
    slot = iota((slots, n_dp), 0)
    source = iota((slots, n_dp), 1)
    room = slot - source * cap
    valid = jnp.sum(
        jnp.where((room >= 0) & (room < cap) & (room < counts[...]), 1.0, 0.0), axis=1, keepdims=True
    )
    square = jnp.sum(sxx[...] + sxgot[...], axis=1, keepdims=True)
    recip = lax.rsqrt(square * (1.0 / S) + 1e-06)
    target = dot(ctil[...], table) + hgot[...].reshape(slots, out_half).astype(f32)
    student_out = (sox[:, kept] + sogot[...].astype(f32)) * recip
    diff = jnp.where(valid > 0.0, student_out - target, 0.0)
    loss = jnp.sum(diff * diff, axis=1, keepdims=True)
    gd[me_m] = (diff * (recip * (1.0 / TOK_DEV))).astype(bf16)
    gd_swap = to_peer(9, gd.at[me_m], gd.at[me_m])
    gd_swap.start()
    losspart[...] = jnp.broadcast_to(loss, (slots, LANES)).T[0:1, :]
    loss_swap = to_peer(10, losspart, lossgot)
    loss_swap.start()

    share = out.shape[0]
    edge = share // 2
    wide_out = gd.shape[2]

    def step(way):
        return 1 + way * (side - 2)

    def ring(f, way):
        ahead = step(way)
        return (1 - f) * (z * side + (y + ahead) % side) + f * (((z + ahead) % side) * side + y)

    def product(f, ahead, mid, b):
        first = ((1 - f) * y + f * z + ahead) % side
        second = ((1 - f) * z + f * y + (1 - mid) * (2 - 2 * b) + mid * (1 + 2 * b)) % side
        owner = (1 - f) * (second * side + first) + f * (first * side + second)
        return jnp.dot(
            sgt[pl.ds(pl.multiple_of(owner * share, share), share), :], gd[f], preferred_element_type=f32
        )

    def sent(f, slot, row, count):
        low = pl.multiple_of(((f * 3 + slot) * 4 + row) * share, share)
        return p.at[pl.ds(low, count * share), wide_out:]

    def landed(f, way, row, count):
        low = pl.multiple_of(((f * 2 + way) * 6 + row) * share, share)
        return p.at[pl.ds(low, count * share), :wide_out]

    def first_copy(f, way, msg):
        number = (f * 2 + way) * 4 + msg
        if msg == 0:
            src, dst = sent(f, 0, 2 * way, 2), landed(f, way, 0, 2)
        elif msg == 1:
            src, dst = sent(f, 1 + way, 2 - 2 * way, 2), landed(f, way, 2, 2)
        else:
            src, dst = sent(f, 1 + way, 2 * way + msg - 2, 1), landed(f, way, 2 + msg, 1)
        return remote(src, dst, s_r.at[number], r_r.at[number], dp=ring(f, way))

    def second_copy(f, way, msg):
        number = 16 + (f * 2 + way) * 3 + msg
        slot = 0 if msg == 0 else 1 + way
        low = (1 - way) * edge if msg == 1 else way * edge
        src = part2.at[f, slot, pl.ds(pl.multiple_of(low, edge), edge)]
        return remote(src, got2.at[f, way, msg], s_r.at[number], r_r.at[number], dp=ring(1 - f, way))

    def flow(n):
        return me_m + n * (1 - 2 * me_m)

    for n in range(2):
        if n == 1:
            gd_swap.wait_recv()

        @pl.loop(0, 2)
        def _(way):
            @pl.loop(0, 2)
            def _(b):
                sent(flow(n), 0, 2 * way + b, 1)[...] = product(flow(n), 2, way, b).astype(bf16)

            first_copy(flow(n), way, 0).start()

    @pl.loop(0, 2)
    def _(n):
        @pl.loop(0, 2)
        def _(way):
            @pl.loop(0, 2)
            def _(b):
                blk = product(flow(n), step(way), 1 - way, b)
                sent(flow(n), 1 + way, 2 - 2 * way + b, 1)[...] = blk.astype(bf16)

            first_copy(flow(n), way, 1).start()

    loss_swap.wait_recv()
    losses[me_s] = losspart[...] + lossgot[...]
    tells = [to_seg(3, n, losses.at[me_s], losses.at[me_s]) for n in range(1, n_seg)]
    for copy in tells:
        copy.start()

    @pl.loop(0, 2)
    def _(n):
        @pl.loop(0, 2)
        def _(mid):
            @pl.loop(0, 2)
            def _(b):
                held[flow(n), 2 * mid + b] = product(flow(n), 0, mid, b)

    for b in range(2):

        @pl.loop(0, 2)
        def _(n):
            @pl.loop(0, 2)
            def _(way):
                f = flow(n)
                if b == 0:
                    first_copy(f, way, 0).wait_recv()
                blk = product(f, step(way), way, b) + landed(f, way, b, 1)[...].astype(f32)
                sent(f, 1 + way, 2 * way + b, 1)[...] = blk.astype(bf16)
                first_copy(f, way, 2 + b).start()

    for copy in tells:
        copy.wait_recv()
    total = losses[0]
    for n in range(1, n_seg):
        total = total + losses[n]
    loss_out[...] = total * (1.0 / S)

    @pl.loop(0, 2)
    def _(n):
        f = flow(n)

        @pl.loop(0, 2)
        def _(way):
            first_copy(f, way, 1).wait_recv()
            for b in range(2):
                held[f, 2 - 2 * way + b] += landed(f, way, 2 + b, 1)[...].astype(f32)

    for b in range(2):

        @pl.loop(0, 2)
        def _(n):
            f = flow(n)

            @pl.loop(0, 2)
            def _(way):
                first_copy(f, way, 2 + b).wait_recv()
                held[f, 2 * way + b] += landed(f, way, 4 + b, 1)[...].astype(f32)

            if b == 0:
                part2[f, 0] = held[f, 0].astype(bf16)
                for way in range(2):
                    second_copy(f, way, 0).start()
                part2[f, 1, edge:] = held[f, 2, edge:].astype(bf16)
                second_copy(f, 0, 1).start()
            else:
                part2[f, 2, :edge] = held[f, 3, :edge].astype(bf16)
                second_copy(f, 1, 1).start()

    @pl.loop(0, 2)
    def _(n):
        f = flow(n)
        for way in range(2):
            second_copy(f, way, 0).wait_recv()
            rows = slice(way * edge, (way + 1) * edge)
            part2[f, 1 + way, rows] = (held[f, 2 + way, rows] + got2[f, way, 0].astype(f32)).astype(bf16)
            second_copy(f, way, 2).start()

    @pl.loop(0, 2)
    def _(n):
        f = flow(n)
        for msg in (1, 2):
            for way in range(2):
                second_copy(f, way, msg).wait_recv()
        span = pl.ds(pl.multiple_of(f * wide_out, LANES), wide_out)
        out[:edge, span] = held[f, 1, :edge] + got2[f, 0, 2].astype(f32) + got2[f, 1, 1].astype(f32)
        out[edge:, span] = held[f, 1, edge:] + got2[f, 0, 1].astype(f32) + got2[f, 1, 2].astype(f32)

    @pl.loop(0, 2)
    def _(f):
        @pl.loop(0, 2)
        def _(way):
            for msg in range(4):
                first_copy(f, way, msg).wait_send()

        for way in range(2):
            for msg in range(3):
                second_copy(f, way, msg).wait_send()

    for copy in u_sent + mg_x + firsts + seconds + [ab_sent, mg_sent, up_sent, hp_sent, sx_sent, so_sent, table_swap, gd_swap, loss_swap] + tells:
        copy.wait_send()

    @pl.when(me_m == 0)
    def _():
        for copy in a_x + [a_swap]:
            copy.wait_send()

    @pl.when(me_m == 1)
    def _():
        extra_swap.wait_send()

    @pl.loop(1, n_dp)
    def _(n):
        a_copy(n).wait_send()
        h_copy(n).wait_send()


def run_step(h, ids, dest, counts, gain, down, up, x, sgain, w, p):
    side = 4
    n_seg = lax.axis_size("segment")
    n_dp = lax.axis_size("dp")
    tok, half = h.shape
    slots, width = x.shape
    cols = p.shape[1]
    out_half = cols // 2
    cap = slots // n_dp
    q = RANK // n_dp
    per = TEACH * q
    rows_u = n_seg * per
    known = rows_u * n_dp
    share = width // n_dp
    c = np.arange(known)
    c_i, c_t, c_k, c_q = c // rows_u, c % rows_u // per, c % per // q, c % q
    spot = np.arange(LANES)[None, :, None]
    xmap = (np.arange(n_seg)[:, None, None] == c_t) & (spot == c_i * q + c_q)
    xmap = jnp.asarray(xmap.astype(np.float32), dtype=bf16)
    kcol = jnp.asarray(c_k[None, :].astype(np.float32))
    vmem = pl.BlockSpec(memory_space=pltpu.VMEM)
    hbm = pl.BlockSpec(memory_space=pl.ANY)
    flops = 2 * (tok * half * cols + 2 * slots * width * cols)
    scratch = [
        (h.shape, bf16), (down.shape, bf16), (up.shape, bf16), (x.shape, bf16), (w.shape, bf16), (p.shape, bf16),
        (xmap.shape, bf16),
        ((rows_u, half // n_seg), bf16), ((n_seg, rows_u, half // n_seg), bf16), ((rows_u, half), bf16),
        ((tok, 2 * LANES), f32), ((tok, 2 * LANES), f32), ((tok, 2 * LANES), f32), ((tok, 2 * LANES), f32),
        ((slots, tok), bf16), ((tok, 2 * LANES), bf16),
        ((n_dp, cap, LANES), bf16), ((2, n_dp, cap, LANES), bf16), ((n_seg, slots, LANES), bf16),
        ((rows_u, LANES), f32), ((rows_u, LANES), f32), ((n_seg, rows_u, LANES), bf16),
        ((rows_u, cols), f32), ((rows_u, out_half), f32),
        ((n_dp, rows_u, out_half + n_seg // 2 * LANES), bf16), ((2, n_dp, rows_u, n_seg // 2 * LANES), bf16),
        ((tok, cols), f32), ((tok, out_half), bf16), ((tok, out_half), bf16),
        ((n_dp, cap, out_half), bf16), ((n_dp, cap, out_half), bf16),
        (x.shape, bf16), ((slots, cols), f32), ((slots, out_half), bf16), ((slots, out_half), bf16),
        ((slots, LANES), f32), ((slots, LANES), f32), ((slots, known), bf16),
        ((width, slots), bf16), ((2, slots, out_half), bf16), ((2, 4, share, out_half), f32),
        ((2, 3, share, out_half), bf16), ((2, 2, 3, share // 2, out_half), bf16),
        ((1, slots), f32), ((1, slots), f32), ((n_seg, 1, slots), f32),
    ]
    sems = [5 + cols // LANES, 11, 11, 4 * (n_seg - 1), 4 * (n_seg - 1), 3 * (n_dp - 1), 3 * (n_dp - 1), 28, 28]
    return pl.pallas_call(
        functools.partial(step_kernel, n_seg, side, cap),
        out_shape=(
            jax.ShapeDtypeStruct((share, cols), f32),
            jax.ShapeDtypeStruct((1, slots), f32),
        ),
        in_specs=[hbm] * 7 + [vmem] * 6,
        out_specs=(vmem, vmem),
        scratch_shapes=[pltpu.VMEM(*s) for s in scratch] + [pltpu.SemaphoreType.DMA((n,)) for n in sems],
        compiler_params=pltpu.CompilerParams(
            collective_id=0, has_side_effects=True, vmem_limit_bytes=60 * 2**20
        ),
        cost_estimate=pl.CostEstimate(flops=flops, bytes_accessed=25 * 2**20, transcendentals=0),
    )(
        h, down, up, x, w, p, xmap,
        ids.reshape(1, tok), dest.reshape(1, tok), counts, gain, sgain.reshape(width // LANES, LANES), kcol,
    )


def local(
    teacher_hidden,
    teacher_id,
    destination,
    row_counts,
    section_gain,
    adapter_down,
    adapter_up,
    student_in,
    student_gain,
    student_weight,
    projector,
):
    weight_grad, row_loss = run_step(
        teacher_hidden,
        teacher_id,
        destination,
        row_counts,
        section_gain,
        adapter_down[0].T,
        adapter_up[0],
        student_in,
        student_gain,
        student_weight,
        projector,
    )
    share, cols = weight_grad.shape
    return (weight_grad.reshape(1, share, cols), row_loss.reshape(student_in.shape[0]))


def solution(mesh):
    placed = (
        P("dp", "mp"),
        P("dp"),
        P("dp"),
        P("dp", None),
        P("segment", "mp"),
        P("segment", "mp", None),
        P("segment", None, "mp"),
        P("dp", "mp"),
        P("mp"),
        P("mp", "segment"),
        P("mp", "segment"),
    )
    return jax.shard_map(
        local,
        mesh=mesh,
        in_specs=placed,
        out_specs=(P("mp", "dp", "segment"), P("dp")),
        check_vma=False,
    )
```

```python
import functools

import jax
import jax.numpy as jnp
import numpy as np
from jax import lax
from jax.experimental import pallas as pl
from jax.experimental.pallas import tpu as pltpu
from jax.sharding import PartitionSpec as P

D = 8192
S = 5120
RANK = 64
TOK_DEV = 256
TEACH = 3
LANES = 128
bf16 = jnp.bfloat16
f32 = jnp.float32


def dot(a, b):
    return jnp.dot(a, b, preferred_element_type=f32)


def remote(src, dst, send, recv, **where):
    return pltpu.make_async_remote_copy(
        src_ref=src,
        dst_ref=dst,
        send_sem=send,
        recv_sem=recv,
        device_id=where,
        device_id_type=pl.DeviceIdType.MESH,
    )


def iota(shape, dim):
    return lax.broadcasted_iota(jnp.int32, shape, dim)


def ones_where(mask):
    return jnp.where(mask, 1.0, 0.0).astype(bf16)


def dot_nt(a, b):
    return lax.dot_general(a, b, (((1,), (1,)), ((), ())), preferred_element_type=f32)


def turned(row):
    return jnp.broadcast_to(row, (LANES, row.shape[1])).T


def fold(wide, keep):
    kept = jnp.where(keep, wide, 0.0)
    both = kept[:, :LANES] + kept[:, LANES:]
    return both + pltpu.roll(both, RANK, 1)


def step_kernel(
    n_seg, side, cap,
    h_hbm, down_hbm, up_hbm, x_hbm, w_hbm, p_hbm, xmap_hbm,
    ids, dest, counts, gain, sgain, kcol,
    out, loss_out,
    h, down, up, x, w, p, xmap,
    usend, ugot, ucat, wide_a, wide_b, abx, abgot, sel, pay, aslots, agot, aall,
    mgx, mggot, mgs, upx, upgot, blocks, tables,
    hpx, hpsend, hpgot, hslots, hgot,
    sg, sox, sosend, sogot, sxx, sxgot, ctil,
    sgt, nb, held, finsend, fingot, losspart, lossgot, losses,
    lsem, s_m, r_m, s_x, r_x, s_d, r_d, s_n, r_n, s_r, r_r,
):
    me_s = lax.axis_index("segment")
    me_m = lax.axis_index("mp")
    me_d = lax.axis_index("dp")
    other = 1 - me_m
    n_dp = side * side
    tok, half = h.shape
    slots = x.shape[0]
    cols = p.shape[1]
    out_half = cols // 2
    rows_u = mgx.shape[0]
    per = rows_u // n_seg
    part = half // n_seg
    tile = 2 * LANES
    tiles = cols // tile
    pair = n_seg // 2

    def load(n, src, dst):
        copy = pltpu.make_async_copy(src, dst, lsem.at[n])
        copy.start()
        return copy

    def p_copy(n):
        span = pl.ds(pl.multiple_of(n * tile, tile), tile)
        return pltpu.make_async_copy(p_hbm.at[:, span], p.at[:, span], lsem.at[5 + n])

    def w_copy(n):
        span = pl.ds(pl.multiple_of(n * tile, tile), tile)
        return pltpu.make_async_copy(w_hbm.at[:, span], w.at[:, span], lsem.at[5 + tiles + n])

    up_in = load(0, up_hbm, up)
    x_in = load(3, x_hbm, x)
    h_in = load(1, h_hbm, h)
    for n in range(tiles):
        p_copy(n).start()
    down_in = load(2, down_hbm, down)
    for n in range(tiles):
        w_copy(n).start()
    xmap_in = load(4, xmap_hbm, xmap)

    z = me_d // side
    y = me_d % side

    def place(first, second):
        a = ((z * other + y * me_m) + second) % side
        b = ((y * other + z * me_m) + first) % side
        return (a * other + b * me_m) * side + b * other + a * me_m

    barrier = pltpu.get_barrier_semaphore()
    mesh_id = pl.DeviceIdType.MESH
    pl.semaphore_signal(barrier, inc=1, device_id={"mp": other}, device_id_type=mesh_id)
    for n in range(1, n_seg):
        pl.semaphore_signal(barrier, inc=1, device_id={"segment": (me_s + n) % n_seg}, device_id_type=mesh_id)

    @pl.loop(1, n_dp)
    def _(n):
        pl.semaphore_signal(barrier, inc=1, device_id={"dp": (me_d + n) % n_dp}, device_id_type=mesh_id)

    for n in range(1, side):
        pl.semaphore_signal(barrier, inc=1, device_id={"dp": place(n, 0), "mp": other}, device_id_type=mesh_id)

    def to_peer(n, src, dst):
        return remote(src, dst, s_m.at[n], r_m.at[n], mp=other)

    def to_seg(kind, n, src, dst):
        number = kind * (n_seg - 1) + n - 1
        return remote(src, dst, s_x.at[number], r_x.at[number], segment=(me_s + n) % n_seg)

    def to_dp(kind, n, src, dst):
        number = kind * (n_dp - 1) + n - 1
        return remote(src, dst, s_d.at[number], r_d.at[number], dp=(me_d + n) % n_dp)

    def gather_first(n):
        return remote(blocks.at[me_d], blocks.at[me_d], s_d.at[n + 29], r_d.at[n + 29], dp=place(n, 0))

    def gather_second(k, n):
        source = place(side - k, 0)
        number = 33 + k * (side - 1) + n - 1
        return remote(blocks.at[source], blocks.at[source], s_d.at[number], r_d.at[number], dp=place(0, n))

    packed = n_seg * per
    row = iota((packed, up.shape[0]), 0)
    col = iota((packed, up.shape[0]), 1)
    quad = row >> 2
    block = (quad >= 3).astype(jnp.int32) + (quad >= 6).astype(jnp.int32) + (quad >= 9).astype(jnp.int32)
    teacher = quad - 3 * block
    hit = ((col >> 6) == teacher) & (((col & 63) >> 2) == me_d) & ((col & 3) == (row & 3))
    up_in.wait()
    mine = jnp.zeros((packed, part), f32)
    for g in range(n_seg):
        mine = mine + dot(ones_where(hit & (block == g)), up[:, g * part : (g + 1) * part])
    usend[...] = mine.astype(bf16)
    ugot[me_s] = usend[...]
    dest_f = dest[...].astype(f32)
    onehot = jnp.where(iota((n_dp, tok), 0).astype(f32) == dest_f, 1.0, 0.0)
    before = ones_where(iota((tok, tok), 0) < iota((tok, tok), 1))
    earlier = dot(onehot.astype(bf16), before)
    position = dest_f * cap + jnp.sum(earlier * onehot, axis=0, keepdims=True)
    sel[...] = ones_where(iota((slots, tok), 0).astype(f32) == position)
    wide_a[...] = jnp.zeros(wide_a.shape, f32)
    wide_b[...] = jnp.zeros(wide_b.shape, f32)
    abx[...] = jnp.zeros(abx.shape, f32)

    x_in.wait()
    sxx[...] = jnp.zeros(sxx.shape, f32)

    @pl.loop(0, x.shape[1] // LANES)
    def _(n):
        span = pl.ds(pl.multiple_of(n * LANES, LANES), LANES)
        wide = x[:, span].astype(f32)
        sxx[...] += wide * wide
        scaled = (wide * sgain[pl.ds(n, 1), :]).astype(bf16)
        sg[:, span] = scaled
        sgt[span, :] = scaled.T

    pl.semaphore_wait(barrier, 1 + (n_seg - 1) + (n_dp - 1) + (side - 1))
    u_sent = [to_seg(0, n, usend, ugot.at[me_s]) for n in range(1, n_seg)]
    for copy in u_sent:
        copy.start()

    share = out.shape[0]

    def rows_of(owner):
        return sgt.at[pl.ds(pl.multiple_of(owner * share, share), share)]

    def owner_of(f, other_ring):
        return (1 - f) * (other_ring * side + y) + f * (z * side + other_ring)

    def block_copy(f, n):
        if f == 0:
            where = z * side + (y + n) % side
            owner = me_s * side + (y + n) % side
        else:
            where = ((z + n) % side) * side + y
            owner = ((z + n) % side) * side + me_s
        number = f * (side - 1) + n - 1
        return remote(
            rows_of(owner), nb.at[me_s, me_m, side - n], s_n.at[number], r_n.at[(n - 1) * 2 + me_m], dp=where, mp=f
        )

    def block_landed(m, n):
        where = nb.at[me_s, m, side - n]
        return remote(where, where, s_n.at[0], r_n.at[(n - 1) * 2 + m], mp=other)

    def chip_copy(n):
        return remote(rows_of(owner_of(other, n)), nb.at[n, me_m, 0], s_n.at[6 + n], r_n.at[6 + n], mp=other)

    def plane_copy(way, m):
        number = 10 + way * 2 + m
        block = nb.at[me_s, m, 1:side]
        return remote(block, block, s_n.at[number], r_n.at[number], segment=(me_s + 1 + way * (n_seg - 2)) % n_seg)

    def plane_forward(way):
        block = nb.at[(me_s + n_seg - 1 + 2 * way) % n_seg, way, 1:side]
        return remote(block, block, s_n.at[14 + way], r_n.at[14 + way], segment=(me_s + 1 + way * (n_seg - 2)) % n_seg)

    for n in range(1, side):
        for f in (0, 1):
            block_copy(f, n).start()
    for n in range(side):
        chip_copy(n).start()
    sx_sent = to_peer(4, sxx, sxgot)
    sx_sent.start()
    for n in range(side):
        nb[n, me_m, 0] = rows_of(owner_of(me_m, n))[...]

    away = pl.ds(pl.multiple_of(other * out_half, LANES), out_half)
    kept = pl.ds(pl.multiple_of(me_m * out_half, LANES), out_half)
    h_in.wait()
    down_in.wait()
    rank_all = down.shape[0]

    @pl.loop(0, n_seg)
    def _(g):
        span = pl.ds(pl.multiple_of(g * part, part), part)
        here = h[:, span]
        wide = here.astype(f32)
        scaled = (wide * gain[:, span].astype(f32)).astype(bf16)
        wide_a[:, :rank_all] += dot_nt(scaled, down[:, span])
        wide_b[:, :rank_all] += dot_nt(here, up[:, span])
        abx[:, LANES:] += jnp.broadcast_to(jnp.sum(wide * wide, axis=1, keepdims=True), (tok, LANES))

    id_col = turned(ids[...].astype(f32))
    lane2 = iota((tok, 2 * LANES), 1)
    own = (lane2 >> 6).astype(f32) == jnp.concatenate([id_col, id_col], axis=1)
    lane = iota((tok, LANES), 1)
    abx[:, :LANES] = jnp.where(lane < RANK, fold(wide_a[...], own), fold(wide_b[...], own))
    ab_sent = to_peer(0, abx, abgot)
    ab_sent.start()


    @pl.loop(0, tiles)
    def _(n):
        span = pl.ds(pl.multiple_of(n * tile, tile), tile)
        p_copy(n).wait()
        hpx[:, span] = dot(h[...], p[:, span])

    hpsend[...] = hpx[:, away].astype(bf16)
    hp_sent = to_peer(3, hpsend, hpgot)
    hp_sent.start()

    ab_sent.wait_recv()
    total = abx[...] + abgot[...]
    sq = total[:, LANES:]
    sq_hi = sq.astype(bf16).astype(f32)
    extra = jnp.where(lane == 0, id_col, jnp.where(lane == 1, sq_hi, jnp.where(lane == 2, sq - sq_hi, 0.0)))
    pay[:, :LANES] = total[:, :LANES].astype(bf16)
    pay[:, LANES:] = extra.astype(bf16)
    lanes_here = pl.ds(pl.multiple_of(me_m * LANES, LANES), LANES)
    aslots[...] = dot(sel[...], pay[:, lanes_here]).astype(bf16).reshape(aslots.shape)
    agot[me_m, me_d] = aslots[me_d]

    def a_copy(n):
        return to_dp(0, n, aslots.at[(me_d + n) % n_dp], agot.at[me_m, me_d])

    @pl.loop(1, n_dp)
    def _(n):
        a_copy(n).start()

    hp_sent.wait_recv()
    hp = (hpx[:, kept] + hpgot[...].astype(f32)).astype(bf16)
    hslots[...] = dot(sel[...], hp).astype(bf16).reshape(hslots.shape)
    hgot[me_d] = hslots[me_d]

    def h_copy(n):
        return to_dp(1, n, hslots.at[(me_d + n) % n_dp], hgot.at[me_d])

    @pl.loop(1, n_dp)
    def _(n):
        h_copy(n).start()

    for copy in u_sent:
        copy.wait_recv()
    row = iota((packed, n_seg * packed), 0)
    col = iota((packed, n_seg * packed), 1)
    quad = row >> 2
    block = (quad >= 3).astype(jnp.int32) + (quad >= 6).astype(jnp.int32) + (quad >= 9).astype(jnp.int32)
    got_u = ugot[...].reshape(n_seg * packed, part)
    for g in range(n_seg):
        take = ones_where(col == row + (packed - per) * block + per * g)
        ucat[:, g * part : (g + 1) * part] = dot(take, got_u).astype(bf16)
    u = ucat[...]
    u_scaled = (u.astype(f32) * gain[...].astype(f32)).astype(bf16)
    wide_a[:rows_u, :rank_all] = dot_nt(u_scaled, down[...])
    wide_b[:rows_u, :rank_all] = dot_nt(u, up[...])
    row = iota((rows_u, 2 * LANES), 0)
    quad = row >> 2
    block = (quad >= 3).astype(jnp.int32) + (quad >= 6).astype(jnp.int32) + (quad >= 9).astype(jnp.int32)
    same = (quad - 3 * block) == (iota((rows_u, 2 * LANES), 1) >> 6)
    lane_u = iota((rows_u, LANES), 1)
    mgx[...] = jnp.where(lane_u < RANK, fold(wide_a[:rows_u, :], same), fold(wide_b[:rows_u, :], same))
    mg_sent = to_peer(1, mgx, mggot)
    mg_sent.start()

    @pl.loop(0, tiles)
    def _(n):
        span = pl.ds(pl.multiple_of(n * tile, tile), tile)
        upx[:, span] = dot(ucat[...], p[:, span])

    up_sent = to_peer(2, upx.at[:, away], upgot)
    up_sent.start()
    mg_sent.wait_recv()
    mgs[me_s] = (mgx[...] + mggot[...]).astype(bf16)
    mg_x = [to_seg(1, n, mgs.at[me_s], mgs.at[me_s]) for n in range(1, n_seg)]
    for copy in mg_x:
        copy.start()

    def student(n):
        span = pl.ds(pl.multiple_of(n * tile, tile), tile)
        w_copy(n).wait()
        sox[:, span] = dot(sg[...], w[:, span])

    @pl.loop(1, n_dp)
    def _(n):
        a_copy(n).wait_recv()

    a_x = [to_seg(2, n, aall.at[me_s], aall.at[me_s]) for n in range(1, n_seg)]
    extra_swap = to_peer(6, agot.at[1], agot.at[1])

    @pl.when(me_m == 0)
    def _():
        aall[me_s] = agot[0].reshape(slots, LANES)
        for copy in a_x:
            copy.start()

    @pl.when(me_m == 1)
    def _():
        extra_swap.start()

    for n in range(1, side):
        for m in (0, 1):
            block_landed(m, n).wait_recv()
    for way in (0, 1):
        for m in (way, 1 - way):
            plane_copy(way, m).start()
    pl.loop(0, 2)(student)

    up_sent.wait_recv()
    blocks[me_d, :, :out_half] = (upx[:, kept] + upgot[...]).astype(bf16)
    for copy in mg_x:
        copy.wait_recv()
    for n in range(pair):
        low = out_half + n * LANES
        blocks[me_d, :, low : low + LANES] = mgs[me_m * pair + n]
    firsts = [gather_first(n) for n in range(1, side)]
    for copy in firsts:
        copy.start()
    seconds = [gather_second(0, n) for n in range(1, side)]
    for copy in seconds:
        copy.start()

    pl.loop(2, 3)(student)
    for k in range(1, side):
        firsts[k - 1].wait_recv()
        for n in range(1, side):
            copy = gather_second(k, n)
            copy.start()
            seconds.append(copy)


    pl.loop(3, tiles)(student)
    sosend[...] = sox[:, away].astype(bf16)
    so_sent = to_peer(5, sosend, sogot)
    so_sent.start()
    a_swap = to_peer(7, aall, aall)

    @pl.when(me_m == 0)
    def _():
        for copy in a_x:
            copy.wait_recv()
        a_swap.start()

    for copy in seconds:
        copy.wait_recv()
    tables[me_m] = blocks[:, :, out_half:]
    table_swap = to_peer(8, tables.at[me_m], tables.at[me_m])
    table_swap.start()

    @pl.when(me_m == 0)
    def _():
        extra_swap.wait_recv()

    @pl.when(me_m == 1)
    def _():
        a_swap.wait_recv()

    xmap_in.wait()
    extra = agot[1].reshape(slots, LANES).astype(f32)
    id_slot = extra[:, 0:1]
    norm = extra[:, 1:2] + extra[:, 2:3]
    keep = kcol[...] == id_slot
    lane = iota((slots, LANES), 1)
    known = rows_u * n_dp
    both = jnp.zeros((slots, LANES), f32)
    table_swap.wait_recv()
    for s in range(n_seg):
        ab = aall[s].astype(f32)
        lat = (ab + both) * lax.rsqrt(jnp.maximum(norm, 0.0) * (1.0 / D) + 1e-06)
        lat = lat.astype(bf16)
        lat_low = jnp.where(lane < RANK, lat.astype(f32), 0.0)
        wide_c = jnp.where(keep, dot(lat_low.astype(bf16), xmap[s]), 0.0).astype(bf16)
        if s == 0:
            ctil[...] = wide_c
        else:
            ctil[...] += wide_c
        if s + 1 < n_seg:
            low, high = (s % pair) * LANES, ((s + 1) % pair) * LANES
            here = tables[s // pair, :, :, low : low + LANES].reshape(known, LANES)
            after = tables[(s + 1) // pair, :, :, high : high + LANES].reshape(known, LANES)
            self_part = dot(ctil[...], here)
            lat_high = pltpu.roll(lat_low, RANK, 1)
            norm = norm + jnp.sum(lat_high * (2.0 * ab + both + self_part), axis=1, keepdims=True)
            both = dot(ctil[...], after)

    @pl.loop(1, n_dp)
    def _(n):
        h_copy(n).wait_recv()

    sx_sent.wait_recv()
    so_sent.wait_recv()
    table = blocks[:, :, :out_half].reshape(known, out_half)
    slot = iota((slots, n_dp), 0)
    source = iota((slots, n_dp), 1)
    room = slot - source * cap
    valid = jnp.sum(
        jnp.where((room >= 0) & (room < cap) & (room < counts[...]), 1.0, 0.0), axis=1, keepdims=True
    )
    square = jnp.sum(sxx[...] + sxgot[...], axis=1, keepdims=True)
    recip = lax.rsqrt(square * (1.0 / S) + 1e-06)
    target = dot(ctil[...], table) + hgot[...].reshape(slots, out_half).astype(f32)
    student_out = (sox[:, kept] + sogot[...].astype(f32)) * recip
    diff = jnp.where(valid > 0.0, student_out - target, 0.0)
    loss = jnp.sum(diff * diff, axis=1, keepdims=True)
    edge = slots // 2

    def gathered(ahead, low=0, count=slots):
        return p.at[pl.ds(ahead * slots + low, count), :out_half]

    def diff_copy(way, part):
        ahead = (side - 1, 1)[way]
        number = way * 2 + part
        return remote(
            gathered(0, part * edge, edge), gathered(ahead, part * edge, edge),
            s_r.at[number], r_r.at[number], dp=place(1 + way * (side - 2), 0),
        )

    def diff_forward(way):
        ahead = (side - 1, 1)[way]
        return remote(
            gathered(ahead, way * edge, edge), gathered(2, way * edge, edge),
            s_r.at[4 + way], r_r.at[4 + way], dp=place(1 + way * (side - 2), 0),
        )

    gathered(0)[...] = (diff * (recip * (1.0 / TOK_DEV))).astype(bf16)
    for way in (0, 1):
        diff_copy(way, way).start()
    for way in (0, 1):
        diff_copy(way, 1 - way).start()
    losspart[...] = jnp.broadcast_to(loss, (slots, LANES)).T[0:1, :]
    loss_swap = to_peer(9, losspart, lossgot)
    loss_swap.start()
    for way in (0, 1):
        plane_copy(way, way).wait_recv()
        plane_forward(way).start()

    def product(owner, m, ahead):
        return dot(nb[owner, m, ahead], gathered(ahead)[...])

    for n in range(side):
        chip_copy(n).wait_recv()

    @pl.loop(0, side)
    def _(n):
        @pl.loop(0, 2)
        def _(m):
            held[n, m] = product(n, m, 0)

    for way in (0, 1):
        diff_copy(way, way).wait_recv()
        diff_forward(way).start()
    loss_swap.wait_recv()
    losses[me_s] = losspart[...] + lossgot[...]
    tells = [to_seg(3, n, losses.at[me_s], losses.at[me_s]) for n in range(1, n_seg)]
    for copy in tells:
        copy.start()
    for way in (0, 1):
        plane_copy(way, 1 - way).wait_recv()
        plane_forward(way).wait_recv()
    for way in (0, 1):
        diff_copy(way, 1 - way).wait_recv()

    @pl.loop(0, side)
    def _(n):
        @pl.loop(0, 2)
        def _(m):
            held[n, m] += product(n, m, 1) + product(n, m, 3)

    for copy in tells:
        copy.wait_recv()
    total = losses[0]
    for n in range(1, n_seg):
        total = total + losses[n]
    loss_out[...] = total * (1.0 / S)

    ring_at = z * other + y * me_m
    base = side * slots

    def sent(slot, m):
        return p.at[pl.ds(base + (slot * 2 + m) * share, share), :out_half]

    def landed(way, msg):
        return p.at[pl.ds(pl.multiple_of(base + (way * 3 + msg) * share, 16), share), out_half:]

    def sum_copy(way, msg):
        slot = 0 if msg == 0 else 1 + way
        m = 1 - way if msg == 1 else way
        number = 6 + way * 3 + msg
        return remote(
            sent(slot, m), landed(way, msg), s_r.at[number], r_r.at[number], dp=place(0, 1 + way * (side - 2))
        )

    for way in (0, 1):
        diff_forward(way).wait_recv()
    far = (ring_at + 2) % side
    nears = [(ring_at + 1) % side, (ring_at + side - 1) % side]
    for way in (0, 1):
        sent(0, way)[...] = (held[far, way] + product(far, way, 2)).astype(bf16)
        sum_copy(way, 0).start()
    for way in (0, 1):
        sent(1 + way, 1 - way)[...] = (held[nears[way], 1 - way] + product(nears[way], 1 - way, 2)).astype(bf16)
        sum_copy(way, 1).start()
    for way in (0, 1):
        held[nears[way], way] += product(nears[way], way, 2)

    @pl.loop(0, 2)
    def _(m):
        held[ring_at, m] += product(ring_at, m, 2)

    for way in (0, 1):
        sum_copy(way, 0).wait_recv()
        sent(1 + way, way)[...] = (held[nears[way], way] + landed(way, 0)[...].astype(f32)).astype(bf16)
        sum_copy(way, 2).start()
    for msg in (1, 2):
        for way in (0, 1):
            sum_copy(way, msg).wait_recv()

    def summed(m):
        return held[ring_at, m] + landed(0, 2 - m)[...].astype(f32) + landed(1, 1 + m)[...].astype(f32)

    finsend[...] = summed(other)
    last_swap = to_peer(10, finsend, fingot)
    last_swap.start()
    out[:, kept] = summed(me_m)
    last_swap.wait_recv()
    out[:, away] = fingot[...]

    for n in range(1, side):
        for f in (0, 1):
            block_copy(f, n).wait_send()
    for n in range(side):
        chip_copy(n).wait_send()
    for way in (0, 1):
        for m in (0, 1):
            plane_copy(way, m).wait_send()
            diff_copy(way, m).wait_send()
        plane_forward(way).wait_send()
        diff_forward(way).wait_send()
        for msg in range(3):
            sum_copy(way, msg).wait_send()
    for copy in u_sent + mg_x + firsts + seconds + [ab_sent, mg_sent, up_sent, hp_sent, sx_sent, so_sent, table_swap, loss_swap, last_swap] + tells:
        copy.wait_send()

    @pl.when(me_m == 0)
    def _():
        for copy in a_x + [a_swap]:
            copy.wait_send()

    @pl.when(me_m == 1)
    def _():
        extra_swap.wait_send()

    @pl.loop(1, n_dp)
    def _(n):
        a_copy(n).wait_send()
        h_copy(n).wait_send()


def run_step(h, ids, dest, counts, gain, down, up, x, sgain, w, p):
    side = 4
    n_seg = lax.axis_size("segment")
    n_dp = lax.axis_size("dp")
    tok, half = h.shape
    slots, width = x.shape
    cols = p.shape[1]
    out_half = cols // 2
    cap = slots // n_dp
    q = RANK // n_dp
    per = TEACH * q
    rows_u = n_seg * per
    known = rows_u * n_dp
    share = width // n_dp
    c = np.arange(known)
    c_i, c_t, c_k, c_q = c // rows_u, c % rows_u // per, c % per // q, c % q
    spot = np.arange(LANES)[None, :, None]
    xmap = (np.arange(n_seg)[:, None, None] == c_t) & (spot == c_i * q + c_q)
    xmap = jnp.asarray(xmap.astype(np.float32), dtype=bf16)
    kcol = jnp.asarray(c_k[None, :].astype(np.float32))
    vmem = pl.BlockSpec(memory_space=pltpu.VMEM)
    hbm = pl.BlockSpec(memory_space=pl.ANY)
    flops = 2 * (tok * half * cols + 2 * slots * width * cols)
    scratch = [
        (h.shape, bf16), (down.shape, bf16), (up.shape, bf16), (x.shape, bf16), (w.shape, bf16), (p.shape, bf16),
        (xmap.shape, bf16),
        ((rows_u, half // n_seg), bf16), ((n_seg, rows_u, half // n_seg), bf16), ((rows_u, half), bf16),
        ((tok, 2 * LANES), f32), ((tok, 2 * LANES), f32), ((tok, 2 * LANES), f32), ((tok, 2 * LANES), f32),
        ((slots, tok), bf16), ((tok, 2 * LANES), bf16),
        ((n_dp, cap, LANES), bf16), ((2, n_dp, cap, LANES), bf16), ((n_seg, slots, LANES), bf16),
        ((rows_u, LANES), f32), ((rows_u, LANES), f32), ((n_seg, rows_u, LANES), bf16),
        ((rows_u, cols), f32), ((rows_u, out_half), f32),
        ((n_dp, rows_u, out_half + n_seg // 2 * LANES), bf16), ((2, n_dp, rows_u, n_seg // 2 * LANES), bf16),
        ((tok, cols), f32), ((tok, out_half), bf16), ((tok, out_half), bf16),
        ((n_dp, cap, out_half), bf16), ((n_dp, cap, out_half), bf16),
        (x.shape, bf16), ((slots, cols), f32), ((slots, out_half), bf16), ((slots, out_half), bf16),
        ((slots, LANES), f32), ((slots, LANES), f32), ((slots, known), bf16),
        ((width, slots), bf16), ((n_seg, 2, side, share, slots), bf16), ((side, 2, share, out_half), f32),
        ((share, out_half), f32), ((share, out_half), f32),
        ((1, slots), f32), ((1, slots), f32), ((n_seg, 1, slots), f32),
    ]
    sems = [5 + cols // LANES, 11, 11, 4 * (n_seg - 1), 4 * (n_seg - 1), 3 * (n_dp - 1), 3 * (n_dp - 1), 16, 16, 12, 12]
    return pl.pallas_call(
        functools.partial(step_kernel, n_seg, side, cap),
        out_shape=(
            jax.ShapeDtypeStruct((share, cols), f32),
            jax.ShapeDtypeStruct((1, slots), f32),
        ),
        in_specs=[hbm] * 7 + [vmem] * 6,
        out_specs=(vmem, vmem),
        scratch_shapes=[pltpu.VMEM(*s) for s in scratch] + [pltpu.SemaphoreType.DMA((n,)) for n in sems],
        compiler_params=pltpu.CompilerParams(
            collective_id=0, has_side_effects=True, vmem_limit_bytes=60 * 2**20
        ),
        cost_estimate=pl.CostEstimate(flops=flops, bytes_accessed=25 * 2**20, transcendentals=0),
    )(
        h, down, up, x, w, p, xmap,
        ids.reshape(1, tok), dest.reshape(1, tok), counts, gain, sgain.reshape(width // LANES, LANES), kcol,
    )


def local(
    teacher_hidden,
    teacher_id,
    destination,
    row_counts,
    section_gain,
    adapter_down,
    adapter_up,
    student_in,
    student_gain,
    student_weight,
    projector,
):
    weight_grad, row_loss = run_step(
        teacher_hidden,
        teacher_id,
        destination,
        row_counts,
        section_gain,
        adapter_down[0].T,
        adapter_up[0],
        student_in,
        student_gain,
        student_weight,
        projector,
    )
    share, cols = weight_grad.shape
    return (weight_grad.reshape(1, share, cols), row_loss.reshape(student_in.shape[0]))


def solution(mesh):
    placed = (
        P("dp", "mp"),
        P("dp"),
        P("dp"),
        P("dp", None),
        P("segment", "mp"),
        P("segment", "mp", None),
        P("segment", None, "mp"),
        P("dp", "mp"),
        P("mp"),
        P("mp", "segment"),
        P("mp", "segment"),
    )
    return jax.shard_map(
        local,
        mesh=mesh,
        in_specs=placed,
        out_specs=(P("mp", "dp", "segment"), P("dp")),
        check_vma=False,
    )
```

```python
import functools

import jax
import jax.numpy as jnp
import numpy as np
from jax import lax
from jax.experimental import pallas as pl
from jax.experimental.pallas import tpu as pltpu
from jax.sharding import PartitionSpec as P

D = 8192
S = 5120
RANK = 64
TOK_DEV = 256
TEACH = 3
LANES = 128
bf16 = jnp.bfloat16
f32 = jnp.float32


def dot(a, b):
    return jnp.dot(a, b, preferred_element_type=f32)


def remote(src, dst, send, recv, **where):
    return pltpu.make_async_remote_copy(
        src_ref=src,
        dst_ref=dst,
        send_sem=send,
        recv_sem=recv,
        device_id=where,
        device_id_type=pl.DeviceIdType.MESH,
    )


def iota(shape, dim):
    return lax.broadcasted_iota(jnp.int32, shape, dim)


def ones_where(mask):
    return jnp.where(mask, 1.0, 0.0).astype(bf16)


def dot_nt(a, b):
    return lax.dot_general(a, b, (((1,), (1,)), ((), ())), preferred_element_type=f32)


def turned(row):
    return jnp.broadcast_to(row, (LANES, row.shape[1])).T


def fold(wide, keep):
    kept = jnp.where(keep, wide, 0.0)
    both = kept[:, :LANES] + kept[:, LANES:]
    return both + pltpu.roll(both, RANK, 1)


def step_kernel(
    n_seg, side, cap,
    h_hbm, down_hbm, up_hbm, x_hbm, w_hbm, p_hbm, xmap_hbm,
    ids, dest, counts, gain, sgain, kcol,
    out, loss_out,
    h, down, up, x, w, p, xmap,
    usend, ugot, ucat, wide_a, wide_b, abx, abgot, sel, pay, aslots, agot, aall,
    mgx, mggot, mgs, upx, upgot, blocks, tables,
    hpx, hpsend, hpgot, hslots, hgot,
    sg, sox, sosend, sogot, sxx, sxgot, ctil, base,
    sgt, nb, held, finsend, fingot, losspart, lossgot, losses,
    lsem, s_m, r_m, s_x, r_x, s_d, r_d, s_n, r_n, s_r, r_r,
):
    me_s = lax.axis_index("segment")
    me_m = lax.axis_index("mp")
    me_d = lax.axis_index("dp")
    other = 1 - me_m
    n_dp = side * side
    tok, half = h.shape
    slots = x.shape[0]
    cols = p.shape[1]
    out_half = cols // 2
    rows_u = mgx.shape[0]
    per = rows_u // n_seg
    part = half // n_seg
    tile = 2 * LANES
    tiles = cols // tile
    pair = n_seg // 2

    def load(n, src, dst):
        copy = pltpu.make_async_copy(src, dst, lsem.at[n])
        copy.start()
        return copy

    def p_copy(n):
        span = pl.ds(pl.multiple_of(n * tile, tile), tile)
        return pltpu.make_async_copy(p_hbm.at[:, span], p.at[:, span], lsem.at[5 + n])

    def w_copy(n):
        span = pl.ds(pl.multiple_of(n * tile, tile), tile)
        return pltpu.make_async_copy(w_hbm.at[:, span], w.at[:, span], lsem.at[5 + tiles + n])

    up_in = load(0, up_hbm, up)
    x_in = load(3, x_hbm, x)
    h_in = load(1, h_hbm, h)
    for n in range(tiles):
        p_copy(n).start()
    down_in = load(2, down_hbm, down)
    for n in range(tiles):
        w_copy(n).start()
    xmap_in = load(4, xmap_hbm, xmap)

    z = me_d // side
    y = me_d % side

    def place(first, second):
        a = ((z * other + y * me_m) + second) % side
        b = ((y * other + z * me_m) + first) % side
        return (a * other + b * me_m) * side + b * other + a * me_m

    barrier = pltpu.get_barrier_semaphore()
    mesh_id = pl.DeviceIdType.MESH
    pl.semaphore_signal(barrier, inc=1, device_id={"mp": other}, device_id_type=mesh_id)
    for n in range(1, n_seg):
        pl.semaphore_signal(barrier, inc=1, device_id={"segment": (me_s + n) % n_seg}, device_id_type=mesh_id)

    @pl.loop(1, n_dp)
    def _(n):
        pl.semaphore_signal(barrier, inc=1, device_id={"dp": (me_d + n) % n_dp}, device_id_type=mesh_id)

    for n in range(1, side):
        pl.semaphore_signal(barrier, inc=1, device_id={"dp": place(n, 0), "mp": other}, device_id_type=mesh_id)

    def to_peer(n, src, dst):
        return remote(src, dst, s_m.at[n], r_m.at[n], mp=other)

    def to_seg(kind, n, src, dst):
        number = kind * (n_seg - 1) + n - 1
        return remote(src, dst, s_x.at[number], r_x.at[number], segment=(me_s + n) % n_seg)

    def to_dp(kind, n, src, dst):
        number = kind * (n_dp - 1) + n - 1
        return remote(src, dst, s_d.at[number], r_d.at[number], dp=(me_d + n) % n_dp)

    def gather_first(n):
        return remote(blocks.at[me_d], blocks.at[me_d], s_d.at[n + 44], r_d.at[n + 44], dp=place(n, 0))

    def gather_second(k, n):
        source = place(side - k, 0)
        number = 48 + k * (side - 1) + n - 1
        return remote(blocks.at[source], blocks.at[source], s_d.at[number], r_d.at[number], dp=place(0, n))

    packed = n_seg * per
    row = iota((packed, up.shape[0]), 0)
    col = iota((packed, up.shape[0]), 1)
    quad = row >> 2
    block = (quad >= 3).astype(jnp.int32) + (quad >= 6).astype(jnp.int32) + (quad >= 9).astype(jnp.int32)
    teacher = quad - 3 * block
    hit = ((col >> 6) == teacher) & (((col & 63) >> 2) == me_d) & ((col & 3) == (row & 3))
    up_in.wait()
    mine = jnp.zeros((packed, part), f32)
    for g in range(n_seg):
        mine = mine + dot(ones_where(hit & (block == g)), up[:, g * part : (g + 1) * part])
    usend[...] = mine.astype(bf16)
    ugot[me_s] = usend[...]
    wide_a[...] = jnp.zeros(wide_a.shape, f32)
    wide_b[...] = jnp.zeros(wide_b.shape, f32)
    abx[...] = jnp.zeros(abx.shape, f32)

    x_in.wait()
    sxx[...] = jnp.zeros(sxx.shape, f32)

    @pl.loop(0, x.shape[1] // LANES)
    def _(n):
        span = pl.ds(pl.multiple_of(n * LANES, LANES), LANES)
        wide = x[:, span].astype(f32)
        sxx[...] += wide * wide
        scaled = (wide * sgain[pl.ds(n, 1), :]).astype(bf16)
        sg[:, span] = scaled
        sgt[span, :] = scaled.T

    pl.semaphore_wait(barrier, 1 + (n_seg - 1) + (n_dp - 1) + (side - 1))
    u_sent = [to_seg(0, n, usend, ugot.at[me_s]) for n in range(1, n_seg)]
    for copy in u_sent:
        copy.start()

    share = out.shape[0]

    def rows_of(owner):
        return sgt.at[pl.ds(pl.multiple_of(owner * share, share), share)]

    def owner_of(f, other_ring):
        return (1 - f) * (other_ring * side + y) + f * (z * side + other_ring)

    def block_copy(f, n):
        if f == 0:
            where = z * side + (y + n) % side
            owner = me_s * side + (y + n) % side
        else:
            where = ((z + n) % side) * side + y
            owner = ((z + n) % side) * side + me_s
        number = f * (side - 1) + n - 1
        return remote(
            rows_of(owner), nb.at[me_s, me_m, side - n], s_n.at[number], r_n.at[(n - 1) * 2 + me_m], dp=where, mp=f
        )

    def block_landed(m, n):
        where = nb.at[me_s, m, side - n]
        return remote(where, where, s_n.at[0], r_n.at[(n - 1) * 2 + m], mp=other)

    def chip_copy(n):
        return remote(rows_of(owner_of(other, n)), nb.at[n, me_m, 0], s_n.at[6 + n], r_n.at[6 + n], mp=other)

    def plane_copy(way, m):
        number = 10 + way * 2 + m
        block = nb.at[me_s, m, 1:side]
        return remote(block, block, s_n.at[number], r_n.at[number], segment=(me_s + 1 + way * (n_seg - 2)) % n_seg)

    def plane_forward(way):
        block = nb.at[(me_s + n_seg - 1 + 2 * way) % n_seg, way, 1:side]
        return remote(block, block, s_n.at[14 + way], r_n.at[14 + way], segment=(me_s + 1 + way * (n_seg - 2)) % n_seg)

    for n in range(1, side):
        for f in (0, 1):
            block_copy(f, n).start()
    for n in range(side):
        chip_copy(n).start()
    sx_sent = to_peer(4, sxx, sxgot)
    sx_sent.start()
    for n in range(side):
        nb[n, me_m, 0] = rows_of(owner_of(me_m, n))[...]

    away = pl.ds(pl.multiple_of(other * out_half, LANES), out_half)
    kept = pl.ds(pl.multiple_of(me_m * out_half, LANES), out_half)
    h_in.wait()
    down_in.wait()
    rank_all = down.shape[0]

    @pl.loop(0, n_seg)
    def _(g):
        span = pl.ds(pl.multiple_of(g * part, part), part)
        here = h[:, span]
        wide = here.astype(f32)
        scaled = (wide * gain[:, span].astype(f32)).astype(bf16)
        wide_a[:, :rank_all] += dot_nt(scaled, down[:, span])
        wide_b[:, :rank_all] += dot_nt(here, up[:, span])
        abx[:, LANES:] += jnp.broadcast_to(jnp.sum(wide * wide, axis=1, keepdims=True), (tok, LANES))

    id_col = turned(ids[...].astype(f32))
    lane2 = iota((tok, 2 * LANES), 1)
    own = (lane2 >> 6).astype(f32) == jnp.concatenate([id_col, id_col], axis=1)
    lane = iota((tok, LANES), 1)
    abx[:, :LANES] = jnp.where(lane < RANK, fold(wide_a[...], own), fold(wide_b[...], own))
    ab_sent = to_peer(0, abx, abgot)
    ab_sent.start()


    @pl.loop(0, tiles)
    def _(n):
        span = pl.ds(pl.multiple_of(n * tile, tile), tile)
        p_copy(n).wait()
        hpx[:, span] = dot(h[...], p[:, span])

    hpsend[...] = hpx[:, away].astype(bf16)
    hp_sent = to_peer(3, hpsend, hpgot)
    hp_sent.start()

    dest_f = dest[...].astype(f32)
    onehot = jnp.where(iota((n_dp, tok), 0).astype(f32) == dest_f, 1.0, 0.0)
    before = ones_where(iota((tok, tok), 0) < iota((tok, tok), 1))
    earlier = dot(onehot.astype(bf16), before)
    position = dest_f * cap + jnp.sum(earlier * onehot, axis=0, keepdims=True)
    sel[...] = ones_where(iota((slots, tok), 0).astype(f32) == position)
    ab_sent.wait_recv()
    total = abx[...] + abgot[...]
    sq = total[:, LANES:]
    sq_hi = sq.astype(bf16).astype(f32)
    extra = jnp.where(lane == 0, id_col, jnp.where(lane == 1, sq_hi, jnp.where(lane == 2, sq - sq_hi, 0.0)))
    pay[:, :LANES] = total[:, :LANES].astype(bf16)
    pay[:, LANES:] = extra.astype(bf16)
    lanes_here = pl.ds(pl.multiple_of(me_m * LANES, LANES), LANES)
    aslots[...] = dot(sel[...], pay[:, lanes_here]).astype(bf16).reshape(aslots.shape)
    agot[me_m, me_d] = aslots[me_d]

    def a_copy(n):
        return to_dp(0, n, aslots.at[(me_d + n) % n_dp], agot.at[me_m, me_d])

    @pl.loop(1, n_dp)
    def _(n):
        a_copy(n).start()

    hp_sent.wait_recv()
    hp = (hpx[:, kept] + hpgot[...].astype(f32)).astype(bf16)
    hslots[...] = dot(sel[...], hp).astype(bf16).reshape(hslots.shape)
    hgot[me_d] = hslots[me_d]

    def h_copy(n):
        return to_dp(1, n, hslots.at[(me_d + n) % n_dp], hgot.at[me_d])

    @pl.loop(1, n_dp)
    def _(n):
        h_copy(n).start()

    for copy in u_sent:
        copy.wait_recv()
    row = iota((packed, n_seg * packed), 0)
    col = iota((packed, n_seg * packed), 1)
    quad = row >> 2
    block = (quad >= 3).astype(jnp.int32) + (quad >= 6).astype(jnp.int32) + (quad >= 9).astype(jnp.int32)
    got_u = ugot[...].reshape(n_seg * packed, part)
    for g in range(n_seg):
        take = ones_where(col == row + (packed - per) * block + per * g)
        ucat[:, g * part : (g + 1) * part] = dot(take, got_u).astype(bf16)
    u = ucat[...]
    u_scaled = (u.astype(f32) * gain[...].astype(f32)).astype(bf16)
    wide_a[:rows_u, :rank_all] = dot_nt(u_scaled, down[...])
    wide_b[:rows_u, :rank_all] = dot_nt(u, up[...])
    row = iota((rows_u, 2 * LANES), 0)
    quad = row >> 2
    block = (quad >= 3).astype(jnp.int32) + (quad >= 6).astype(jnp.int32) + (quad >= 9).astype(jnp.int32)
    same = (quad - 3 * block) == (iota((rows_u, 2 * LANES), 1) >> 6)
    lane_u = iota((rows_u, LANES), 1)
    mgx[...] = jnp.where(lane_u < RANK, fold(wide_a[:rows_u, :], same), fold(wide_b[:rows_u, :], same))
    mg_sent = to_peer(1, mgx, mggot)
    mg_sent.start()

    def up_tile(n):
        span = pl.ds(pl.multiple_of(n * tile, tile), tile)
        upx[:, span] = dot(ucat[...], p[:, span])

    pl.loop(0, 2)(up_tile)
    mg_sent.wait_recv()
    mgs[me_s] = (mgx[...] + mggot[...]).astype(bf16)
    mg_x = [to_seg(1, n, mgs.at[me_s], mgs.at[me_s]) for n in range(1, n_seg)]
    for copy in mg_x:
        copy.start()

    pl.loop(2, tiles)(up_tile)
    up_sent = to_peer(2, upx.at[:, away], upgot)
    up_sent.start()

    def student(n):
        span = pl.ds(pl.multiple_of(n * tile, tile), tile)
        w_copy(n).wait()
        sox[:, span] = dot(sg[...], w[:, span])

    pl.loop(0, 1)(student)

    for copy in mg_x:
        copy.wait_recv()
    for n in range(pair):
        tables[me_m, me_d, :, n * LANES : (n + 1) * LANES] = mgs[me_m * pair + n]

    def m_copy(n):
        return to_dp(2, n, tables.at[me_m, me_d], tables.at[me_m, me_d])

    @pl.loop(1, n_dp)
    def _(n):
        m_copy(n).start()

    up_sent.wait_recv()
    blocks[me_d] = (upx[:, kept] + upgot[...]).astype(bf16)
    firsts = [gather_first(n) for n in range(1, side)]
    for copy in firsts:
        copy.start()
    seconds = [gather_second(0, n) for n in range(1, side)]
    for copy in seconds:
        copy.start()

    @pl.loop(1, n_dp)
    def _(n):
        a_copy(n).wait_recv()

    a_x = [to_seg(2, n, aall.at[me_s], aall.at[me_s]) for n in range(1, n_seg)]
    extra_swap = to_peer(6, agot.at[1], agot.at[1])

    @pl.when(me_m == 0)
    def _():
        aall[me_s] = agot[0].reshape(slots, LANES)
        for copy in a_x:
            copy.start()

    @pl.when(me_m == 1)
    def _():
        extra_swap.start()

    for n in range(1, side):
        for m in (0, 1):
            block_landed(m, n).wait_recv()
    for way in (0, 1):
        for m in (way, 1 - way):
            plane_copy(way, m).start()

    pl.loop(1, 4)(student)
    for k in range(1, side):
        firsts[k - 1].wait_recv()
        for n in range(1, side):
            copy = gather_second(k, n)
            copy.start()
            seconds.append(copy)

    pl.loop(4, tiles)(student)
    sosend[...] = sox[:, away].astype(bf16)
    so_sent = to_peer(5, sosend, sogot)
    so_sent.start()
    a_swap = to_peer(7, aall, aall)

    @pl.when(me_m == 0)
    def _():
        for copy in a_x:
            copy.wait_recv()
        a_swap.start()

    @pl.loop(1, n_dp)
    def _(n):
        m_copy(n).wait_recv()

    table_swap = to_peer(8, tables.at[me_m], tables.at[me_m])
    table_swap.start()

    @pl.when(me_m == 0)
    def _():
        extra_swap.wait_recv()

    @pl.when(me_m == 1)
    def _():
        a_swap.wait_recv()

    xmap_in.wait()
    extra = agot[1].reshape(slots, LANES).astype(f32)
    id_slot = extra[:, 0:1]
    norm = extra[:, 1:2] + extra[:, 2:3]
    keep = kcol[...] == id_slot
    lane = iota((slots, LANES), 1)
    known = rows_u * n_dp
    both = jnp.zeros((slots, LANES), f32)
    table_swap.wait_recv()
    for s in range(n_seg):
        ab = aall[s].astype(f32)
        lat = (ab + both) * lax.rsqrt(jnp.maximum(norm, 0.0) * (1.0 / D) + 1e-06)
        lat = lat.astype(bf16)
        lat_low = jnp.where(lane < RANK, lat.astype(f32), 0.0)
        wide_c = jnp.where(keep, dot(lat_low.astype(bf16), xmap[s]), 0.0).astype(bf16)
        if s == 0:
            ctil[...] = wide_c
        else:
            ctil[...] += wide_c
        if s + 1 < n_seg:
            low, high = (s % pair) * LANES, ((s + 1) % pair) * LANES
            here = tables[s // pair, :, :, low : low + LANES].reshape(known, LANES)
            after = tables[(s + 1) // pair, :, :, high : high + LANES].reshape(known, LANES)
            self_part = dot(ctil[...], here)
            lat_high = pltpu.roll(lat_low, RANK, 1)
            norm = norm + jnp.sum(lat_high * (2.0 * ab + both + self_part), axis=1, keepdims=True)
            both = dot(ctil[...], after)

    @pl.loop(1, n_dp)
    def _(n):
        h_copy(n).wait_recv()

    sx_sent.wait()
    so_sent.wait_recv()
    slot = iota((slots, n_dp), 0)
    source = iota((slots, n_dp), 1)
    room = slot - source * cap
    valid = jnp.sum(
        jnp.where((room >= 0) & (room < cap) & (room < counts[...]), 1.0, 0.0), axis=1, keepdims=True
    )
    square = jnp.sum(sxx[...] + sxgot[...], axis=1, keepdims=True)
    recip = lax.rsqrt(square * (1.0 / S) + 1e-06)
    student_out = (sox[:, kept] + sogot[...].astype(f32)) * recip
    base[...] = jnp.where(valid > 0.0, student_out - hgot[...].reshape(slots, out_half).astype(f32), 0.0)
    sxx[...] = jnp.broadcast_to(recip * (1.0 / TOK_DEV), sxx.shape)
    for copy in seconds:
        copy.wait_recv()
    table = blocks[...].reshape(known, out_half)
    edge = slots // 2

    def gathered(ahead, low=0, count=slots):
        return p.at[pl.ds(ahead * slots + low, count), :out_half]

    def diff_copy(way, part):
        ahead = (side - 1, 1)[way]
        number = way * 2 + part
        return remote(
            gathered(0, part * edge, edge), gathered(ahead, part * edge, edge),
            s_r.at[number], r_r.at[number], dp=place(1 + way * (side - 2), 0),
        )

    def diff_forward(way):
        ahead = (side - 1, 1)[way]
        return remote(
            gathered(ahead, way * edge, edge), gathered(2, way * edge, edge),
            s_r.at[4 + way], r_r.at[4 + way], dp=place(1 + way * (side - 2), 0),
        )

    def difference(part):
        rows = slice(part * edge, (part + 1) * edge)
        diff = base[rows, :] - dot(ctil[rows, :], table)
        gathered(0, part * edge, edge)[...] = (diff * sxx[rows, 0:1]).astype(bf16)
        loss = jnp.sum(diff * diff, axis=1, keepdims=True)
        losspart[:, rows] = jnp.broadcast_to(loss, (edge, LANES)).T[0:1, :]

    difference(0)
    diff_copy(0, 0).start()
    difference(1)
    diff_copy(1, 1).start()
    for way in (0, 1):
        diff_copy(way, 1 - way).start()
    loss_swap = to_peer(9, losspart, lossgot)
    loss_swap.start()
    for way in (0, 1):
        plane_copy(way, way).wait_recv()
        plane_forward(way).start()

    def product(owner, m, ahead):
        return dot(nb[owner, m, ahead], gathered(ahead)[...])

    for n in range(side):
        chip_copy(n).wait_recv()

    @pl.loop(0, side)
    def _(n):
        @pl.loop(0, 2)
        def _(m):
            held[n, m] = product(n, m, 0)

    for way in (0, 1):
        diff_copy(way, way).wait_recv()
        diff_forward(way).start()
    loss_swap.wait_recv()
    losses[me_s] = losspart[...] + lossgot[...]
    tells = [to_seg(3, n, losses.at[me_s], losses.at[me_s]) for n in range(1, n_seg)]
    for copy in tells:
        copy.start()
    for way in (0, 1):
        plane_copy(way, 1 - way).wait_recv()
        plane_forward(way).wait_recv()
    for way in (0, 1):
        diff_copy(way, 1 - way).wait_recv()

    @pl.loop(0, side)
    def _(n):
        @pl.loop(0, 2)
        def _(m):
            held[n, m] += product(n, m, 1) + product(n, m, 3)

    for copy in tells:
        copy.wait_recv()
    total = losses[0]
    for n in range(1, n_seg):
        total = total + losses[n]
    loss_out[...] = total * (1.0 / S)

    ring_at = z * other + y * me_m
    below = side * slots

    def sent(slot, m):
        return p.at[pl.ds(below + (slot * 2 + m) * share, share), :out_half]

    def landed(way, msg):
        return p.at[pl.ds(pl.multiple_of(below + (way * 3 + msg) * share, 16), share), out_half:]

    def sum_copy(way, msg):
        slot = 0 if msg == 0 else 1 + way
        m = 1 - way if msg == 1 else way
        number = 6 + way * 3 + msg
        return remote(
            sent(slot, m), landed(way, msg), s_r.at[number], r_r.at[number], dp=place(0, 1 + way * (side - 2))
        )

    for way in (0, 1):
        diff_forward(way).wait_recv()
    far = (ring_at + 2) % side
    nears = [(ring_at + 1) % side, (ring_at + side - 1) % side]
    for way in (0, 1):
        sent(0, way)[...] = (held[far, way] + product(far, way, 2)).astype(bf16)
        sum_copy(way, 0).start()
    for way in (0, 1):
        sent(1 + way, 1 - way)[...] = (held[nears[way], 1 - way] + product(nears[way], 1 - way, 2)).astype(bf16)
        sum_copy(way, 1).start()
    for way in (0, 1):
        held[nears[way], way] += product(nears[way], way, 2)

    @pl.loop(0, 2)
    def _(m):
        held[ring_at, m] += product(ring_at, m, 2)

    for way in (0, 1):
        sum_copy(way, 0).wait_recv()
        sent(1 + way, way)[...] = (held[nears[way], way] + landed(way, 0)[...].astype(f32)).astype(bf16)
        sum_copy(way, 2).start()
    for msg in (1, 2):
        for way in (0, 1):
            sum_copy(way, msg).wait_recv()

    def summed(m):
        return held[ring_at, m] + landed(0, 2 - m)[...].astype(f32) + landed(1, 1 + m)[...].astype(f32)

    finsend[...] = summed(other)
    last_swap = to_peer(10, finsend, fingot)
    last_swap.start()
    out[:, kept] = summed(me_m)
    last_swap.wait_recv()
    out[:, away] = fingot[...]

    for n in range(1, side):
        for f in (0, 1):
            block_copy(f, n).wait_send()
    for n in range(side):
        chip_copy(n).wait_send()
    for way in (0, 1):
        for m in (0, 1):
            plane_copy(way, m).wait_send()
            diff_copy(way, m).wait_send()
        plane_forward(way).wait_send()
        diff_forward(way).wait_send()
        for msg in range(3):
            sum_copy(way, msg).wait_send()
    for copy in u_sent + mg_x + firsts + seconds + [ab_sent, mg_sent, up_sent, hp_sent, so_sent, table_swap, loss_swap, last_swap] + tells:
        copy.wait_send()

    @pl.when(me_m == 0)
    def _():
        for copy in a_x + [a_swap]:
            copy.wait_send()

    @pl.when(me_m == 1)
    def _():
        extra_swap.wait_send()

    @pl.loop(1, n_dp)
    def _(n):
        a_copy(n).wait_send()
        m_copy(n).wait_send()
        h_copy(n).wait_send()


def run_step(h, ids, dest, counts, gain, down, up, x, sgain, w, p):
    side = 4
    n_seg = lax.axis_size("segment")
    n_dp = lax.axis_size("dp")
    tok, half = h.shape
    slots, width = x.shape
    cols = p.shape[1]
    out_half = cols // 2
    cap = slots // n_dp
    q = RANK // n_dp
    per = TEACH * q
    rows_u = n_seg * per
    known = rows_u * n_dp
    share = width // n_dp
    c = np.arange(known)
    c_i, c_t, c_k, c_q = c // rows_u, c % rows_u // per, c % per // q, c % q
    spot = np.arange(LANES)[None, :, None]
    xmap = (np.arange(n_seg)[:, None, None] == c_t) & (spot == c_i * q + c_q)
    xmap = jnp.asarray(xmap.astype(np.float32), dtype=bf16)
    kcol = jnp.asarray(c_k[None, :].astype(np.float32))
    vmem = pl.BlockSpec(memory_space=pltpu.VMEM)
    hbm = pl.BlockSpec(memory_space=pl.ANY)
    flops = 2 * (tok * half * cols + 2 * slots * width * cols)
    scratch = [
        (h.shape, bf16), (down.shape, bf16), (up.shape, bf16), (x.shape, bf16), (w.shape, bf16), (p.shape, bf16),
        (xmap.shape, bf16),
        ((rows_u, half // n_seg), bf16), ((n_seg, rows_u, half // n_seg), bf16), ((rows_u, half), bf16),
        ((tok, 2 * LANES), f32), ((tok, 2 * LANES), f32), ((tok, 2 * LANES), f32), ((tok, 2 * LANES), f32),
        ((slots, tok), bf16), ((tok, 2 * LANES), bf16),
        ((n_dp, cap, LANES), bf16), ((2, n_dp, cap, LANES), bf16), ((n_seg, slots, LANES), bf16),
        ((rows_u, LANES), f32), ((rows_u, LANES), f32), ((n_seg, rows_u, LANES), bf16),
        ((rows_u, cols), f32), ((rows_u, out_half), f32),
        ((n_dp, rows_u, out_half), bf16), ((2, n_dp, rows_u, n_seg // 2 * LANES), bf16),
        ((tok, cols), f32), ((tok, out_half), bf16), ((tok, out_half), bf16),
        ((n_dp, cap, out_half), bf16), ((n_dp, cap, out_half), bf16),
        (x.shape, bf16), ((slots, cols), f32), ((slots, out_half), bf16), ((slots, out_half), bf16),
        ((slots, LANES), f32), ((slots, LANES), f32), ((slots, known), bf16), ((slots, out_half), f32),
        ((width, slots), bf16), ((n_seg, 2, side, share, slots), bf16), ((side, 2, share, out_half), f32),
        ((share, out_half), f32), ((share, out_half), f32),
        ((1, slots), f32), ((1, slots), f32), ((n_seg, 1, slots), f32),
    ]
    sems = [5 + cols // LANES, 11, 11, 4 * (n_seg - 1), 4 * (n_seg - 1), 4 * (n_dp - 1), 4 * (n_dp - 1), 16, 16, 12, 12]
    return pl.pallas_call(
        functools.partial(step_kernel, n_seg, side, cap),
        out_shape=(
            jax.ShapeDtypeStruct((share, cols), f32),
            jax.ShapeDtypeStruct((1, slots), f32),
        ),
        in_specs=[hbm] * 7 + [vmem] * 6,
        out_specs=(vmem, vmem),
        scratch_shapes=[pltpu.VMEM(*s) for s in scratch] + [pltpu.SemaphoreType.DMA((n,)) for n in sems],
        compiler_params=pltpu.CompilerParams(
            collective_id=0, has_side_effects=True, vmem_limit_bytes=60 * 2**20
        ),
        cost_estimate=pl.CostEstimate(flops=flops, bytes_accessed=25 * 2**20, transcendentals=0),
    )(
        h, down, up, x, w, p, xmap,
        ids.reshape(1, tok), dest.reshape(1, tok), counts, gain, sgain.reshape(width // LANES, LANES), kcol,
    )


def local(
    teacher_hidden,
    teacher_id,
    destination,
    row_counts,
    section_gain,
    adapter_down,
    adapter_up,
    student_in,
    student_gain,
    student_weight,
    projector,
):
    weight_grad, row_loss = run_step(
        teacher_hidden,
        teacher_id,
        destination,
        row_counts,
        section_gain,
        adapter_down[0].T,
        adapter_up[0],
        student_in,
        student_gain,
        student_weight,
        projector,
    )
    share, cols = weight_grad.shape
    return (weight_grad.reshape(1, share, cols), row_loss.reshape(student_in.shape[0]))


def solution(mesh):
    placed = (
        P("dp", "mp"),
        P("dp"),
        P("dp"),
        P("dp", None),
        P("segment", "mp"),
        P("segment", "mp", None),
        P("segment", None, "mp"),
        P("dp", "mp"),
        P("mp"),
        P("mp", "segment"),
        P("mp", "segment"),
    )
    return jax.shard_map(
        local,
        mesh=mesh,
        in_specs=placed,
        out_specs=(P("mp", "dp", "segment"), P("dp")),
        check_vma=False,
    )
```

```python
import functools

import jax
import jax.numpy as jnp
import numpy as np
from jax import lax
from jax.experimental import pallas as pl
from jax.experimental.pallas import tpu as pltpu
from jax.sharding import PartitionSpec as P

D = 8192
S = 5120
RANK = 64
TOK_DEV = 256
TEACH = 3
LANES = 128
bf16 = jnp.bfloat16
f32 = jnp.float32


def dot(a, b):
    return jnp.dot(a, b, preferred_element_type=f32)


def remote(src, dst, send, recv, **where):
    return pltpu.make_async_remote_copy(
        src_ref=src,
        dst_ref=dst,
        send_sem=send,
        recv_sem=recv,
        device_id=where,
        device_id_type=pl.DeviceIdType.MESH,
    )


def iota(shape, dim):
    return lax.broadcasted_iota(jnp.int32, shape, dim)


def ones_where(mask):
    return jnp.where(mask, 1.0, 0.0).astype(bf16)


def dot_nt(a, b):
    return lax.dot_general(a, b, (((1,), (1,)), ((), ())), preferred_element_type=f32)


def turned(row):
    return jnp.broadcast_to(row, (LANES, row.shape[1])).T


def fold(wide, keep):
    kept = jnp.where(keep, wide, 0.0)
    both = kept[:, :LANES] + kept[:, LANES:]
    return both + pltpu.roll(both, RANK, 1)


def step_kernel(
    n_seg, side, cap,
    h_hbm, down_hbm, up_hbm, x_hbm, w_hbm, p_hbm, xmap_hbm,
    ids, dest, counts, gain, sgain, kcol,
    out, loss_out,
    h, down, up, x, w, p, xmap,
    usend, ugot, ucat, wide_a, wide_b, abx, abgot, sel, pay, aslots, agot, aall,
    mgx, mggot, mgs, upx, upgot, blocks, tables,
    hpx, hpsend, hpgot, hslots, hgot,
    sg, sox, sosend, sogot, sxx, sxgot, ctil, base,
    sgt, nb, held, finsend, fingot, losspart, lossgot, losses,
    lsem, s_m, r_m, s_x, r_x, s_d, r_d, s_n, r_n, s_r, r_r,
):
    me_s = lax.axis_index("segment")
    me_m = lax.axis_index("mp")
    me_d = lax.axis_index("dp")
    other = 1 - me_m
    n_dp = side * side
    tok, half = h.shape
    slots = x.shape[0]
    cols = p.shape[1]
    out_half = cols // 2
    rows_u = mgx.shape[0]
    per = rows_u // n_seg
    part = half // n_seg
    tile = 2 * LANES
    tiles = cols // tile
    pair = n_seg // 2

    def load(n, src, dst):
        copy = pltpu.make_async_copy(src, dst, lsem.at[n])
        copy.start()
        return copy

    def p_copy(n):
        span = pl.ds(pl.multiple_of(n * tile, tile), tile)
        return pltpu.make_async_copy(p_hbm.at[:, span], p.at[:, span], lsem.at[5 + n])

    def w_copy(n):
        span = pl.ds(pl.multiple_of(n * tile, tile), tile)
        return pltpu.make_async_copy(w_hbm.at[:, span], w.at[:, span], lsem.at[5 + tiles + n])

    up_in = load(0, up_hbm, up)
    x_in = load(3, x_hbm, x)
    h_in = load(1, h_hbm, h)
    for n in range(tiles):
        p_copy(n).start()
    down_in = load(2, down_hbm, down)
    for n in range(tiles):
        w_copy(n).start()
    xmap_in = load(4, xmap_hbm, xmap)

    z = me_d // side
    y = me_d % side

    def place(first, second):
        a = ((z * other + y * me_m) + second) % side
        b = ((y * other + z * me_m) + first) % side
        return (a * other + b * me_m) * side + b * other + a * me_m

    barrier = pltpu.get_barrier_semaphore()
    mesh_id = pl.DeviceIdType.MESH
    pl.semaphore_signal(barrier, inc=1, device_id={"mp": other}, device_id_type=mesh_id)
    for n in range(1, n_seg):
        pl.semaphore_signal(barrier, inc=1, device_id={"segment": (me_s + n) % n_seg}, device_id_type=mesh_id)

    @pl.loop(1, n_dp)
    def _(n):
        pl.semaphore_signal(barrier, inc=1, device_id={"dp": (me_d + n) % n_dp}, device_id_type=mesh_id)

    for n in range(1, side):
        pl.semaphore_signal(barrier, inc=1, device_id={"dp": place(n, 0), "mp": other}, device_id_type=mesh_id)

    def to_peer(n, src, dst):
        return remote(src, dst, s_m.at[n], r_m.at[n], mp=other)

    def to_seg(kind, n, src, dst):
        number = kind * (n_seg - 1) + n - 1
        return remote(src, dst, s_x.at[number], r_x.at[number], segment=(me_s + n) % n_seg)

    def to_dp(kind, n, src, dst):
        number = kind * (n_dp - 1) + n - 1
        return remote(src, dst, s_d.at[number], r_d.at[number], dp=(me_d + n) % n_dp)

    def gather_first(n):
        return remote(blocks.at[me_d], blocks.at[me_d], s_d.at[n + 44], r_d.at[n + 44], dp=place(n, 0))

    def gather_second(k, n):
        source = place(side - k, 0)
        number = 48 + k * (side - 1) + n - 1
        return remote(blocks.at[source], blocks.at[source], s_d.at[number], r_d.at[number], dp=place(0, n))

    packed = n_seg * per
    row = iota((packed, up.shape[0]), 0)
    col = iota((packed, up.shape[0]), 1)
    quad = row >> 2
    block = (quad >= 3).astype(jnp.int32) + (quad >= 6).astype(jnp.int32) + (quad >= 9).astype(jnp.int32)
    teacher = quad - 3 * block
    hit = ((col >> 6) == teacher) & (((col & 63) >> 2) == me_d) & ((col & 3) == (row & 3))
    up_in.wait()
    mine = jnp.zeros((packed, part), f32)
    for g in range(n_seg):
        mine = mine + dot(ones_where(hit & (block == g)), up[:, g * part : (g + 1) * part])
    usend[...] = mine.astype(bf16)
    ugot[me_s] = usend[...]
    wide_a[...] = jnp.zeros(wide_a.shape, f32)
    wide_b[...] = jnp.zeros(wide_b.shape, f32)
    abx[...] = jnp.zeros(abx.shape, f32)

    x_in.wait()
    sxx[...] = jnp.zeros(sxx.shape, f32)

    @pl.loop(0, x.shape[1] // LANES)
    def _(n):
        span = pl.ds(pl.multiple_of(n * LANES, LANES), LANES)
        wide = x[:, span].astype(f32)
        sxx[...] += wide * wide
        scaled = (wide * sgain[pl.ds(n, 1), :]).astype(bf16)
        sg[:, span] = scaled
        sgt[span, :] = scaled.T

    pl.semaphore_wait(barrier, 1 + (n_seg - 1) + (n_dp - 1) + (side - 1))
    u_sent = [to_seg(0, n, usend, ugot.at[me_s]) for n in range(1, n_seg)]
    for copy in u_sent:
        copy.start()

    share = out.shape[0]

    def rows_of(owner):
        return sgt.at[pl.ds(pl.multiple_of(owner * share, share), share)]

    def owner_of(f, other_ring):
        return (1 - f) * (other_ring * side + y) + f * (z * side + other_ring)

    def block_copy(f, n):
        if f == 0:
            where = z * side + (y + n) % side
            owner = me_s * side + (y + n) % side
        else:
            where = ((z + n) % side) * side + y
            owner = ((z + n) % side) * side + me_s
        number = f * (side - 1) + n - 1
        return remote(
            rows_of(owner), nb.at[me_s, side - n, me_m], s_n.at[number], r_n.at[(n - 1) * 2 + me_m], dp=where, mp=f
        )

    def block_landed(m, n):
        where = nb.at[me_s, side - n, m]
        return remote(where, where, s_n.at[0], r_n.at[(n - 1) * 2 + m], mp=other)

    def chip_copy(n):
        return remote(rows_of(owner_of(other, n)), nb.at[n, 0, me_m], s_n.at[6 + n], r_n.at[6 + n], mp=other)

    def plane_copy(way, m, k):
        number = 10 + (way * 2 + m) * (side - 1) + k - 1
        block = nb.at[me_s, k, m]
        return remote(block, block, s_n.at[number], r_n.at[number], segment=(me_s + 1 + way * (n_seg - 2)) % n_seg)

    def plane_forward(way, k):
        number = 10 + (4 + way) * (side - 1) + k - 1
        block = nb.at[(me_s + n_seg - 1 + 2 * way) % n_seg, k, way]
        return remote(block, block, s_n.at[number], r_n.at[number], segment=(me_s + 1 + way * (n_seg - 2)) % n_seg)

    for n in (1, side - 1, 2):
        for f in (0, 1):
            block_copy(f, n).start()
    for n in range(side):
        chip_copy(n).start()
    sx_sent = to_peer(4, sxx, sxgot)
    sx_sent.start()
    for n in range(side):
        nb[n, 0, me_m] = rows_of(owner_of(me_m, n))[...]

    away = pl.ds(pl.multiple_of(other * out_half, LANES), out_half)
    kept = pl.ds(pl.multiple_of(me_m * out_half, LANES), out_half)
    h_in.wait()
    down_in.wait()
    rank_all = down.shape[0]

    @pl.loop(0, n_seg)
    def _(g):
        span = pl.ds(pl.multiple_of(g * part, part), part)
        here = h[:, span]
        wide = here.astype(f32)
        scaled = (wide * gain[:, span].astype(f32)).astype(bf16)
        wide_a[:, :rank_all] += dot_nt(scaled, down[:, span])
        wide_b[:, :rank_all] += dot_nt(here, up[:, span])
        abx[:, LANES:] += jnp.broadcast_to(jnp.sum(wide * wide, axis=1, keepdims=True), (tok, LANES))

    id_col = turned(ids[...].astype(f32))
    lane2 = iota((tok, 2 * LANES), 1)
    own = (lane2 >> 6).astype(f32) == jnp.concatenate([id_col, id_col], axis=1)
    lane = iota((tok, LANES), 1)
    abx[:, :LANES] = jnp.where(lane < RANK, fold(wide_a[...], own), fold(wide_b[...], own))
    ab_sent = to_peer(0, abx, abgot)
    ab_sent.start()


    @pl.loop(0, tiles)
    def _(n):
        span = pl.ds(pl.multiple_of(n * tile, tile), tile)
        p_copy(n).wait()
        hpx[:, span] = dot(h[...], p[:, span])

    hpsend[...] = hpx[:, away].astype(bf16)
    hp_sent = to_peer(3, hpsend, hpgot)
    hp_sent.start()
    for n in (1, side - 1):
        for m in (0, 1):
            block_landed(m, n).wait_recv()
    for n in (1, side - 1):
        for way in (0, 1):
            plane_copy(way, way, n).start()

    dest_f = dest[...].astype(f32)
    onehot = jnp.where(iota((n_dp, tok), 0).astype(f32) == dest_f, 1.0, 0.0)
    before = ones_where(iota((tok, tok), 0) < iota((tok, tok), 1))
    earlier = dot(onehot.astype(bf16), before)
    position = dest_f * cap + jnp.sum(earlier * onehot, axis=0, keepdims=True)
    sel[...] = ones_where(iota((slots, tok), 0).astype(f32) == position)
    ab_sent.wait_recv()
    total = abx[...] + abgot[...]
    sq = total[:, LANES:]
    sq_hi = sq.astype(bf16).astype(f32)
    extra = jnp.where(lane == 0, id_col, jnp.where(lane == 1, sq_hi, jnp.where(lane == 2, sq - sq_hi, 0.0)))
    pay[:, :LANES] = total[:, :LANES].astype(bf16)
    pay[:, LANES:] = extra.astype(bf16)
    lanes_here = pl.ds(pl.multiple_of(me_m * LANES, LANES), LANES)
    aslots[...] = dot(sel[...], pay[:, lanes_here]).astype(bf16).reshape(aslots.shape)
    agot[me_m, me_d] = aslots[me_d]

    def a_copy(n):
        return to_dp(0, n, aslots.at[(me_d + n) % n_dp], agot.at[me_m, me_d])

    @pl.loop(1, n_dp)
    def _(n):
        a_copy(n).start()

    hp_sent.wait_recv()
    hp = (hpx[:, kept] + hpgot[...].astype(f32)).astype(bf16)
    hslots[...] = dot(sel[...], hp).astype(bf16).reshape(hslots.shape)
    hgot[me_d] = hslots[me_d]

    def h_copy(n):
        return to_dp(1, n, hslots.at[(me_d + n) % n_dp], hgot.at[me_d])

    @pl.loop(1, n_dp)
    def _(n):
        h_copy(n).start()

    for copy in u_sent:
        copy.wait_recv()
    row = iota((packed, n_seg * packed), 0)
    col = iota((packed, n_seg * packed), 1)
    quad = row >> 2
    block = (quad >= 3).astype(jnp.int32) + (quad >= 6).astype(jnp.int32) + (quad >= 9).astype(jnp.int32)
    got_u = ugot[...].reshape(n_seg * packed, part)
    for g in range(n_seg):
        take = ones_where(col == row + (packed - per) * block + per * g)
        ucat[:, g * part : (g + 1) * part] = dot(take, got_u).astype(bf16)
    u = ucat[...]
    u_scaled = (u.astype(f32) * gain[...].astype(f32)).astype(bf16)
    wide_a[:rows_u, :rank_all] = dot_nt(u_scaled, down[...])
    wide_b[:rows_u, :rank_all] = dot_nt(u, up[...])
    row = iota((rows_u, 2 * LANES), 0)
    quad = row >> 2
    block = (quad >= 3).astype(jnp.int32) + (quad >= 6).astype(jnp.int32) + (quad >= 9).astype(jnp.int32)
    same = (quad - 3 * block) == (iota((rows_u, 2 * LANES), 1) >> 6)
    lane_u = iota((rows_u, LANES), 1)
    mgx[...] = jnp.where(lane_u < RANK, fold(wide_a[:rows_u, :], same), fold(wide_b[:rows_u, :], same))
    mg_sent = to_peer(1, mgx, mggot)
    mg_sent.start()

    def up_tile(n):
        span = pl.ds(pl.multiple_of(n * tile, tile), tile)
        upx[:, span] = dot(ucat[...], p[:, span])

    pl.loop(0, 2)(up_tile)
    mg_sent.wait_recv()
    mgs[me_s] = (mgx[...] + mggot[...]).astype(bf16)
    mg_x = [to_seg(1, n, mgs.at[me_s], mgs.at[me_s]) for n in range(1, n_seg)]
    for copy in mg_x:
        copy.start()

    pl.loop(2, tiles)(up_tile)
    up_sent = to_peer(2, upx.at[:, away], upgot)
    up_sent.start()

    def student(n):
        span = pl.ds(pl.multiple_of(n * tile, tile), tile)
        w_copy(n).wait()
        sox[:, span] = dot(sg[...], w[:, span])

    pl.loop(0, 1)(student)

    for copy in mg_x:
        copy.wait_recv()
    for n in range(pair):
        tables[me_m, me_d, :, n * LANES : (n + 1) * LANES] = mgs[me_m * pair + n]

    def m_copy(n):
        return to_dp(2, n, tables.at[me_m, me_d], tables.at[me_m, me_d])

    @pl.loop(1, n_dp)
    def _(n):
        m_copy(n).start()

    up_sent.wait_recv()
    blocks[me_d] = (upx[:, kept] + upgot[...]).astype(bf16)
    firsts = [gather_first(n) for n in range(1, side)]
    for copy in firsts:
        copy.start()
    seconds = [gather_second(0, n) for n in range(1, side)]
    for copy in seconds:
        copy.start()

    @pl.loop(1, n_dp)
    def _(n):
        a_copy(n).wait_recv()

    a_x = [to_seg(2, n, aall.at[me_s], aall.at[me_s]) for n in range(1, n_seg)]
    extra_swap = to_peer(6, agot.at[1], agot.at[1])

    @pl.when(me_m == 0)
    def _():
        aall[me_s] = agot[0].reshape(slots, LANES)
        for copy in a_x:
            copy.start()

    @pl.when(me_m == 1)
    def _():
        extra_swap.start()

    for m in (0, 1):
        block_landed(m, 2).wait_recv()
    for way in (0, 1):
        plane_copy(way, way, 2).start()
    for n in (1, side - 1):
        for way in (0, 1):
            plane_copy(way, way, n).wait_recv()
            plane_forward(way, n).start()
    for n in (1, side - 1, 2):
        for way in (0, 1):
            plane_copy(way, 1 - way, n).start()

    pl.loop(1, 4)(student)
    for k in range(1, side):
        firsts[k - 1].wait_recv()
        for n in range(1, side):
            copy = gather_second(k, n)
            copy.start()
            seconds.append(copy)

    pl.loop(4, tiles)(student)
    sosend[...] = sox[:, away].astype(bf16)
    so_sent = to_peer(5, sosend, sogot)
    so_sent.start()
    a_swap = to_peer(7, aall, aall)

    @pl.when(me_m == 0)
    def _():
        for copy in a_x:
            copy.wait_recv()
        a_swap.start()

    for way in (0, 1):
        plane_copy(way, way, 2).wait_recv()
        plane_forward(way, 2).start()

    @pl.loop(1, n_dp)
    def _(n):
        m_copy(n).wait_recv()

    table_swap = to_peer(8, tables.at[me_m], tables.at[me_m])
    table_swap.start()

    @pl.when(me_m == 0)
    def _():
        extra_swap.wait_recv()

    @pl.when(me_m == 1)
    def _():
        a_swap.wait_recv()

    xmap_in.wait()
    extra = agot[1].reshape(slots, LANES).astype(f32)
    id_slot = extra[:, 0:1]
    norm = extra[:, 1:2] + extra[:, 2:3]
    keep = kcol[...] == id_slot
    lane = iota((slots, LANES), 1)
    known = rows_u * n_dp
    both = jnp.zeros((slots, LANES), f32)
    table_swap.wait_recv()
    for s in range(n_seg):
        ab = aall[s].astype(f32)
        lat = (ab + both) * lax.rsqrt(jnp.maximum(norm, 0.0) * (1.0 / D) + 1e-06)
        lat = lat.astype(bf16)
        lat_low = jnp.where(lane < RANK, lat.astype(f32), 0.0)
        wide_c = jnp.where(keep, dot(lat_low.astype(bf16), xmap[s]), 0.0).astype(bf16)
        if s == 0:
            ctil[...] = wide_c
        else:
            ctil[...] += wide_c
        if s + 1 < n_seg:
            low, high = (s % pair) * LANES, ((s + 1) % pair) * LANES
            here = tables[s // pair, :, :, low : low + LANES].reshape(known, LANES)
            after = tables[(s + 1) // pair, :, :, high : high + LANES].reshape(known, LANES)
            self_part = dot(ctil[...], here)
            lat_high = pltpu.roll(lat_low, RANK, 1)
            norm = norm + jnp.sum(lat_high * (2.0 * ab + both + self_part), axis=1, keepdims=True)
            both = dot(ctil[...], after)

    @pl.loop(1, n_dp)
    def _(n):
        h_copy(n).wait_recv()

    sx_sent.wait()
    so_sent.wait_recv()
    slot = iota((slots, n_dp), 0)
    source = iota((slots, n_dp), 1)
    room = slot - source * cap
    valid = jnp.sum(
        jnp.where((room >= 0) & (room < cap) & (room < counts[...]), 1.0, 0.0), axis=1, keepdims=True
    )
    square = jnp.sum(sxx[...] + sxgot[...], axis=1, keepdims=True)
    recip = lax.rsqrt(square * (1.0 / S) + 1e-06)
    student_out = (sox[:, kept] + sogot[...].astype(f32)) * recip
    base[...] = jnp.where(valid > 0.0, student_out - hgot[...].reshape(slots, out_half).astype(f32), 0.0)
    sxx[...] = jnp.broadcast_to(recip * (1.0 / TOK_DEV), sxx.shape)
    for copy in seconds:
        copy.wait_recv()
    table = blocks[...].reshape(known, out_half)
    edge = slots // 2

    def gathered(ahead, low=0, count=slots):
        return p.at[pl.ds(ahead * slots + low, count), :out_half]

    def diff_copy(way, part):
        ahead = (side - 1, 1)[way]
        number = way * 2 + part
        return remote(
            gathered(0, part * edge, edge), gathered(ahead, part * edge, edge),
            s_r.at[number], r_r.at[number], dp=place(1 + way * (side - 2), 0),
        )

    def diff_forward(way):
        ahead = (side - 1, 1)[way]
        return remote(
            gathered(ahead, way * edge, edge), gathered(2, way * edge, edge),
            s_r.at[4 + way], r_r.at[4 + way], dp=place(1 + way * (side - 2), 0),
        )

    def difference(part):
        rows = slice(part * edge, (part + 1) * edge)
        diff = base[rows, :] - dot(ctil[rows, :], table)
        gathered(0, part * edge, edge)[...] = (diff * sxx[rows, 0:1]).astype(bf16)
        loss = jnp.sum(diff * diff, axis=1, keepdims=True)
        losspart[:, rows] = jnp.broadcast_to(loss, (edge, LANES)).T[0:1, :]

    difference(0)
    diff_copy(0, 0).start()
    difference(1)
    diff_copy(1, 1).start()
    for way in (0, 1):
        diff_copy(way, 1 - way).start()
    loss_swap = to_peer(9, losspart, lossgot)
    loss_swap.start()
    def product(owner, ahead):
        return dot(nb[owner, ahead].reshape(2 * share, slots), gathered(ahead)[...])

    for n in range(side):
        chip_copy(n).wait_recv()

    @pl.loop(0, side)
    def _(n):
        held[n] = product(n, 0)

    for way in (0, 1):
        diff_copy(way, way).wait_recv()
        diff_forward(way).start()
    loss_swap.wait_recv()
    losses[me_s] = losspart[...] + lossgot[...]
    tells = [to_seg(3, n, losses.at[me_s], losses.at[me_s]) for n in range(1, n_seg)]
    for copy in tells:
        copy.start()
    for way in (0, 1):
        for n in range(1, side):
            plane_copy(way, 1 - way, n).wait_recv()
            plane_forward(way, n).wait_recv()
    for way in (0, 1):
        diff_copy(way, 1 - way).wait_recv()

    @pl.loop(0, side)
    def _(n):
        held[n] += product(n, 1) + product(n, 3)

    for copy in tells:
        copy.wait_recv()
    total = losses[0]
    for n in range(1, n_seg):
        total = total + losses[n]
    loss_out[...] = total * (1.0 / S)

    ring_at = z * other + y * me_m
    below = side * slots

    def sent(slot, m):
        return p.at[pl.ds(below + (slot * 2 + m) * share, share), :out_half]

    def landed(way, msg):
        return p.at[pl.ds(pl.multiple_of(below + (way * 3 + msg) * share, 16), share), out_half:]

    def sum_copy(way, msg):
        slot = 0 if msg == 0 else 1 + way
        m = 1 - way if msg == 1 else way
        number = 6 + way * 3 + msg
        return remote(
            sent(slot, m), landed(way, msg), s_r.at[number], r_r.at[number], dp=place(0, 1 + way * (side - 2))
        )

    for way in (0, 1):
        diff_forward(way).wait_recv()
    far = (ring_at + 2) % side
    nears = [(ring_at + 1) % side, (ring_at + side - 1) % side]

    def half_rows(m):
        return pl.ds(m * share, share)

    block = held[far] + product(far, 2)
    for way in (0, 1):
        sent(0, way)[...] = block[way * share : (way + 1) * share].astype(bf16)
        sum_copy(way, 0).start()
    for way in (0, 1):
        block = held[nears[way]] + product(nears[way], 2)
        sent(1 + way, 1 - way)[...] = block[(1 - way) * share : (2 - way) * share].astype(bf16)
        sum_copy(way, 1).start()
        held[nears[way], half_rows(way)] = block[way * share : (way + 1) * share]
    held[ring_at] += product(ring_at, 2)
    for way in (0, 1):
        sum_copy(way, 0).wait_recv()
        sent(1 + way, way)[...] = (held[nears[way], half_rows(way)] + landed(way, 0)[...].astype(f32)).astype(bf16)
        sum_copy(way, 2).start()
    for msg in (1, 2):
        for way in (0, 1):
            sum_copy(way, msg).wait_recv()

    def summed(m):
        mine = held[ring_at, pl.ds(pl.multiple_of(m * share, share), share)]
        return mine + landed(0, 2 - m)[...].astype(f32) + landed(1, 1 + m)[...].astype(f32)

    finsend[...] = summed(other)
    last_swap = to_peer(10, finsend, fingot)
    last_swap.start()
    out[:, kept] = summed(me_m)
    last_swap.wait_recv()
    out[:, away] = fingot[...]

    for n in range(1, side):
        for f in (0, 1):
            block_copy(f, n).wait_send()
    for n in range(side):
        chip_copy(n).wait_send()
    for way in (0, 1):
        for n in range(1, side):
            for m in (0, 1):
                plane_copy(way, m, n).wait_send()
            plane_forward(way, n).wait_send()
        for m in (0, 1):
            diff_copy(way, m).wait_send()
        diff_forward(way).wait_send()
        for msg in range(3):
            sum_copy(way, msg).wait_send()
    for copy in u_sent + mg_x + firsts + seconds + [ab_sent, mg_sent, up_sent, hp_sent, so_sent, table_swap, loss_swap, last_swap] + tells:
        copy.wait_send()

    @pl.when(me_m == 0)
    def _():
        for copy in a_x + [a_swap]:
            copy.wait_send()

    @pl.when(me_m == 1)
    def _():
        extra_swap.wait_send()

    @pl.loop(1, n_dp)
    def _(n):
        a_copy(n).wait_send()
        m_copy(n).wait_send()
        h_copy(n).wait_send()


def run_step(h, ids, dest, counts, gain, down, up, x, sgain, w, p):
    side = 4
    n_seg = lax.axis_size("segment")
    n_dp = lax.axis_size("dp")
    tok, half = h.shape
    slots, width = x.shape
    cols = p.shape[1]
    out_half = cols // 2
    cap = slots // n_dp
    q = RANK // n_dp
    per = TEACH * q
    rows_u = n_seg * per
    known = rows_u * n_dp
    share = width // n_dp
    c = np.arange(known)
    c_i, c_t, c_k, c_q = c // rows_u, c % rows_u // per, c % per // q, c % q
    spot = np.arange(LANES)[None, :, None]
    xmap = (np.arange(n_seg)[:, None, None] == c_t) & (spot == c_i * q + c_q)
    xmap = jnp.asarray(xmap.astype(np.float32), dtype=bf16)
    kcol = jnp.asarray(c_k[None, :].astype(np.float32))
    vmem = pl.BlockSpec(memory_space=pltpu.VMEM)
    hbm = pl.BlockSpec(memory_space=pl.ANY)
    flops = 2 * (tok * half * cols + 2 * slots * width * cols)
    scratch = [
        (h.shape, bf16), (down.shape, bf16), (up.shape, bf16), (x.shape, bf16), (w.shape, bf16), (p.shape, bf16),
        (xmap.shape, bf16),
        ((rows_u, half // n_seg), bf16), ((n_seg, rows_u, half // n_seg), bf16), ((rows_u, half), bf16),
        ((tok, 2 * LANES), f32), ((tok, 2 * LANES), f32), ((tok, 2 * LANES), f32), ((tok, 2 * LANES), f32),
        ((slots, tok), bf16), ((tok, 2 * LANES), bf16),
        ((n_dp, cap, LANES), bf16), ((2, n_dp, cap, LANES), bf16), ((n_seg, slots, LANES), bf16),
        ((rows_u, LANES), f32), ((rows_u, LANES), f32), ((n_seg, rows_u, LANES), bf16),
        ((rows_u, cols), f32), ((rows_u, out_half), f32),
        ((n_dp, rows_u, out_half), bf16), ((2, n_dp, rows_u, n_seg // 2 * LANES), bf16),
        ((tok, cols), f32), ((tok, out_half), bf16), ((tok, out_half), bf16),
        ((n_dp, cap, out_half), bf16), ((n_dp, cap, out_half), bf16),
        (x.shape, bf16), ((slots, cols), f32), ((slots, out_half), bf16), ((slots, out_half), bf16),
        ((slots, LANES), f32), ((slots, LANES), f32), ((slots, known), bf16), ((slots, out_half), f32),
        ((width, slots), bf16), ((n_seg, side, 2, share, slots), bf16), ((side, 2 * share, out_half), f32),
        ((share, out_half), f32), ((share, out_half), f32),
        ((1, slots), f32), ((1, slots), f32), ((n_seg, 1, slots), f32),
    ]
    sems = [5 + cols // LANES, 11, 11, 4 * (n_seg - 1), 4 * (n_seg - 1), 4 * (n_dp - 1), 4 * (n_dp - 1), 28, 28, 12, 12]
    return pl.pallas_call(
        functools.partial(step_kernel, n_seg, side, cap),
        out_shape=(
            jax.ShapeDtypeStruct((share, cols), f32),
            jax.ShapeDtypeStruct((1, slots), f32),
        ),
        in_specs=[hbm] * 7 + [vmem] * 6,
        out_specs=(vmem, vmem),
        scratch_shapes=[pltpu.VMEM(*s) for s in scratch] + [pltpu.SemaphoreType.DMA((n,)) for n in sems],
        compiler_params=pltpu.CompilerParams(
            collective_id=0, has_side_effects=True, vmem_limit_bytes=60 * 2**20
        ),
        cost_estimate=pl.CostEstimate(flops=flops, bytes_accessed=25 * 2**20, transcendentals=0),
    )(
        h, down, up, x, w, p, xmap,
        ids.reshape(1, tok), dest.reshape(1, tok), counts, gain, sgain.reshape(width // LANES, LANES), kcol,
    )


def finish_kernel(grad, loss, grad_out, loss_out, sems):
    copies = [pltpu.make_async_copy(grad, grad_out, sems.at[0]), pltpu.make_async_copy(loss, loss_out, sems.at[1])]
    for copy in copies:
        copy.start()
    for copy in copies:
        copy.wait()


def finish(grad, loss):
    hbm = pl.BlockSpec(memory_space=pl.ANY)
    return pl.pallas_call(
        finish_kernel,
        out_shape=(jax.ShapeDtypeStruct(grad.shape, f32), jax.ShapeDtypeStruct(loss.shape, f32)),
        in_specs=[hbm, hbm],
        out_specs=(hbm, hbm),
        scratch_shapes=[pltpu.SemaphoreType.DMA((2,))],
    )(grad, loss)


def local(
    teacher_hidden,
    teacher_id,
    destination,
    row_counts,
    section_gain,
    adapter_down,
    adapter_up,
    student_in,
    student_gain,
    student_weight,
    projector,
):
    weight_grad, row_loss = run_step(
        teacher_hidden,
        teacher_id,
        destination,
        row_counts,
        section_gain,
        adapter_down[0].T,
        adapter_up[0],
        student_in,
        student_gain,
        student_weight,
        projector,
    )
    weight_grad, row_loss = finish(weight_grad, row_loss)
    share, cols = weight_grad.shape
    return (weight_grad.reshape(1, share, cols), row_loss.reshape(student_in.shape[0]))


def solution(mesh):
    placed = (
        P("dp", "mp"),
        P("dp"),
        P("dp"),
        P("dp", None),
        P("segment", "mp"),
        P("segment", "mp", None),
        P("segment", None, "mp"),
        P("dp", "mp"),
        P("mp"),
        P("mp", "segment"),
        P("mp", "segment"),
    )
    return jax.shard_map(
        local,
        mesh=mesh,
        in_specs=placed,
        out_specs=(P("mp", "dp", "segment"), P("dp")),
        check_vma=False,
    )
```

```python
import functools

import jax
import jax.numpy as jnp
import numpy as np
from jax import lax
from jax.experimental import pallas as pl
from jax.experimental.pallas import tpu as pltpu
from jax.sharding import PartitionSpec as P

D = 8192
S = 5120
RANK = 64
TOK_DEV = 256
TEACH = 3
LANES = 128
bf16 = jnp.bfloat16
f32 = jnp.float32


def dot(a, b):
    return jnp.dot(a, b, preferred_element_type=f32)


def remote(src, dst, send, recv, **where):
    return pltpu.make_async_remote_copy(
        src_ref=src,
        dst_ref=dst,
        send_sem=send,
        recv_sem=recv,
        device_id=where,
        device_id_type=pl.DeviceIdType.MESH,
    )


def iota(shape, dim):
    return lax.broadcasted_iota(jnp.int32, shape, dim)


def ones_where(mask):
    return jnp.where(mask, 1.0, 0.0).astype(bf16)


def dot_nt(a, b):
    return lax.dot_general(a, b, (((1,), (1,)), ((), ())), preferred_element_type=f32)


def turned(row):
    return jnp.broadcast_to(row, (LANES, row.shape[1])).T


def fold(wide, keep):
    kept = jnp.where(keep, wide, 0.0)
    both = kept[:, :LANES] + kept[:, LANES:]
    return both + pltpu.roll(both, RANK, 1)


def step_kernel(
    n_seg, side, cap,
    h_hbm, down_hbm, up_hbm, x_hbm, w_hbm, p_hbm, xmap_hbm,
    ids, dest, counts, gain, sgain, kcol,
    out, loss_out,
    h, down, up, x, w, p, xmap,
    usend, ugot, ucat, wide_a, wide_b, abx, abgot, sel, pay, aslots, agot, aall,
    mgx, mggot, mgs, upx, upgot, blocks, tables,
    hpx, hpsend, hpgot, hslots, hgot,
    sg, sox, sosend, sogot, sxx, sxgot, ctil, base,
    sgt, nb, held, finsend, fingot, losspart, lossgot, losses,
    lsem, s_m, r_m, s_x, r_x, s_d, r_d, s_n, r_n, s_r, r_r,
):
    me_s = lax.axis_index("segment")
    me_m = lax.axis_index("mp")
    me_d = lax.axis_index("dp")
    other = 1 - me_m
    n_dp = side * side
    tok, half = h.shape
    slots = x.shape[0]
    cols = p.shape[1]
    out_half = cols // 2
    rows_u = mgx.shape[0]
    per = rows_u // n_seg
    part = half // n_seg
    tile = 2 * LANES
    tiles = cols // tile
    pair = n_seg // 2

    def load(n, src, dst):
        copy = pltpu.make_async_copy(src, dst, lsem.at[n])
        copy.start()
        return copy

    def p_copy(n):
        span = pl.ds(pl.multiple_of(n * tile, tile), tile)
        return pltpu.make_async_copy(p_hbm.at[:, span], p.at[:, span], lsem.at[5 + n])

    def w_copy(n):
        span = pl.ds(pl.multiple_of(n * tile, tile), tile)
        return pltpu.make_async_copy(w_hbm.at[:, span], w.at[:, span], lsem.at[5 + tiles + n])

    up_in = load(0, up_hbm, up)
    x_in = load(3, x_hbm, x)
    h_in = load(1, h_hbm, h)
    for n in range(tiles):
        p_copy(n).start()
    down_in = load(2, down_hbm, down)
    for n in range(tiles):
        w_copy(n).start()
    xmap_in = load(4, xmap_hbm, xmap)

    z = me_d // side
    y = me_d % side

    def place(first, second):
        a = ((z * other + y * me_m) + second) % side
        b = ((y * other + z * me_m) + first) % side
        return (a * other + b * me_m) * side + b * other + a * me_m

    barrier = pltpu.get_barrier_semaphore()
    mesh_id = pl.DeviceIdType.MESH
    pl.semaphore_signal(barrier, inc=1, device_id={"mp": other}, device_id_type=mesh_id)
    for n in range(1, n_seg):
        pl.semaphore_signal(barrier, inc=1, device_id={"segment": (me_s + n) % n_seg}, device_id_type=mesh_id)

    @pl.loop(1, n_dp)
    def _(n):
        pl.semaphore_signal(barrier, inc=1, device_id={"dp": (me_d + n) % n_dp}, device_id_type=mesh_id)

    for n in range(1, side):
        pl.semaphore_signal(barrier, inc=1, device_id={"dp": place(n, 0), "mp": other}, device_id_type=mesh_id)

    def to_peer(n, src, dst):
        return remote(src, dst, s_m.at[n], r_m.at[n], mp=other)

    def to_seg(kind, n, src, dst):
        number = kind * (n_seg - 1) + n - 1
        return remote(src, dst, s_x.at[number], r_x.at[number], segment=(me_s + n) % n_seg)

    def to_dp(kind, n, src, dst):
        number = kind * (n_dp - 1) + n - 1
        return remote(src, dst, s_d.at[number], r_d.at[number], dp=(me_d + n) % n_dp)

    def gather_first(n):
        return remote(blocks.at[me_d], blocks.at[me_d], s_d.at[n + 44], r_d.at[n + 44], dp=place(n, 0))

    def gather_second(k, n):
        source = place(side - k, 0)
        number = 48 + k * (side - 1) + n - 1
        return remote(blocks.at[source], blocks.at[source], s_d.at[number], r_d.at[number], dp=place(0, n))

    packed = n_seg * per
    row = iota((packed, up.shape[0]), 0)
    col = iota((packed, up.shape[0]), 1)
    quad = row >> 2
    block = (quad >= 3).astype(jnp.int32) + (quad >= 6).astype(jnp.int32) + (quad >= 9).astype(jnp.int32)
    teacher = quad - 3 * block
    hit = ((col >> 6) == teacher) & (((col & 63) >> 2) == me_d) & ((col & 3) == (row & 3))
    up_in.wait()
    mine = jnp.zeros((packed, part), f32)
    for g in range(n_seg):
        mine = mine + dot(ones_where(hit & (block == g)), up[:, g * part : (g + 1) * part])
    usend[...] = mine.astype(bf16)
    ugot[me_s] = usend[...]
    wide_a[...] = jnp.zeros(wide_a.shape, f32)
    wide_b[...] = jnp.zeros(wide_b.shape, f32)
    abx[...] = jnp.zeros(abx.shape, f32)

    x_in.wait()
    sxx[...] = jnp.zeros(sxx.shape, f32)

    @pl.loop(0, x.shape[1] // LANES)
    def _(n):
        span = pl.ds(pl.multiple_of(n * LANES, LANES), LANES)
        wide = x[:, span].astype(f32)
        sxx[...] += wide * wide
        scaled = (wide * sgain[pl.ds(n, 1), :]).astype(bf16)
        sg[:, span] = scaled
        sgt[span, :] = scaled.T

    pl.semaphore_wait(barrier, 1 + (n_seg - 1) + (n_dp - 1) + (side - 1))
    u_sent = [to_seg(0, n, usend, ugot.at[me_s]) for n in range(1, n_seg)]
    for copy in u_sent:
        copy.start()

    share = out.shape[0]

    def rows_of(owner):
        return sgt.at[pl.ds(pl.multiple_of(owner * share, share), share)]

    def owner_of(f, other_ring):
        return (1 - f) * (other_ring * side + y) + f * (z * side + other_ring)

    def block_copy(f, n):
        if f == 0:
            where = z * side + (y + n) % side
            owner = me_s * side + (y + n) % side
        else:
            where = ((z + n) % side) * side + y
            owner = ((z + n) % side) * side + me_s
        number = f * (side - 1) + n - 1
        return remote(
            rows_of(owner), nb.at[me_s, side - n, me_m], s_n.at[number], r_n.at[(n - 1) * 2 + me_m], dp=where, mp=f
        )

    def block_landed(m, n):
        where = nb.at[me_s, side - n, m]
        return remote(where, where, s_n.at[0], r_n.at[(n - 1) * 2 + m], mp=other)

    def chip_copy(n):
        return remote(rows_of(owner_of(other, n)), nb.at[n, 0, me_m], s_n.at[6 + n], r_n.at[6 + n], mp=other)

    def plane_copy(way, m, k):
        number = 10 + (way * 2 + m) * (side - 1) + k - 1
        block = nb.at[me_s, k, m]
        return remote(block, block, s_n.at[number], r_n.at[number], segment=(me_s + 1 + way * (n_seg - 2)) % n_seg)

    def plane_forward(way, k):
        number = 10 + (4 + way) * (side - 1) + k - 1
        block = nb.at[(me_s + n_seg - 1 + 2 * way) % n_seg, k, way]
        return remote(block, block, s_n.at[number], r_n.at[number], segment=(me_s + 1 + way * (n_seg - 2)) % n_seg)

    for n in (1, side - 1, 2):
        for f in (0, 1):
            block_copy(f, n).start()
    for n in range(side):
        chip_copy(n).start()
    sx_sent = to_peer(4, sxx, sxgot)
    sx_sent.start()
    for n in range(side):
        nb[n, 0, me_m] = rows_of(owner_of(me_m, n))[...]

    away = pl.ds(pl.multiple_of(other * out_half, LANES), out_half)
    kept = pl.ds(pl.multiple_of(me_m * out_half, LANES), out_half)
    h_in.wait()
    down_in.wait()
    rank_all = down.shape[0]

    @pl.loop(0, n_seg)
    def _(g):
        span = pl.ds(pl.multiple_of(g * part, part), part)
        here = h[:, span]
        wide = here.astype(f32)
        scaled = (wide * gain[:, span].astype(f32)).astype(bf16)
        wide_a[:, :rank_all] += dot_nt(scaled, down[:, span])
        wide_b[:, :rank_all] += dot_nt(here, up[:, span])
        abx[:, LANES:] += jnp.broadcast_to(jnp.sum(wide * wide, axis=1, keepdims=True), (tok, LANES))

    id_col = turned(ids[...].astype(f32))
    lane2 = iota((tok, 2 * LANES), 1)
    own = (lane2 >> 6).astype(f32) == jnp.concatenate([id_col, id_col], axis=1)
    lane = iota((tok, LANES), 1)
    abx[:, :LANES] = jnp.where(lane < RANK, fold(wide_a[...], own), fold(wide_b[...], own))
    ab_sent = to_peer(0, abx, abgot)
    ab_sent.start()


    @pl.loop(0, tiles)
    def _(n):
        span = pl.ds(pl.multiple_of(n * tile, tile), tile)
        p_copy(n).wait()
        hpx[:, span] = dot(h[...], p[:, span])

    hpsend[...] = hpx[:, away].astype(bf16)
    hp_sent = to_peer(3, hpsend, hpgot)
    hp_sent.start()
    for n in (1, side - 1):
        for m in (0, 1):
            block_landed(m, n).wait_recv()
    for n in (1, side - 1):
        for way in (0, 1):
            plane_copy(way, way, n).start()

    dest_f = dest[...].astype(f32)
    onehot = jnp.where(iota((n_dp, tok), 0).astype(f32) == dest_f, 1.0, 0.0)
    before = ones_where(iota((tok, tok), 0) < iota((tok, tok), 1))
    earlier = dot(onehot.astype(bf16), before)
    position = dest_f * cap + jnp.sum(earlier * onehot, axis=0, keepdims=True)
    sel[...] = ones_where(iota((slots, tok), 0).astype(f32) == position)
    ab_sent.wait_recv()
    total = abx[...] + abgot[...]
    sq = total[:, LANES:]
    sq_hi = sq.astype(bf16).astype(f32)
    extra = jnp.where(lane == 0, id_col, jnp.where(lane == 1, sq_hi, jnp.where(lane == 2, sq - sq_hi, 0.0)))
    pay[:, :LANES] = total[:, :LANES].astype(bf16)
    pay[:, LANES:] = extra.astype(bf16)
    lanes_here = pl.ds(pl.multiple_of(me_m * LANES, LANES), LANES)
    aslots[...] = dot(sel[...], pay[:, lanes_here]).astype(bf16).reshape(aslots.shape)
    agot[me_m, me_d] = aslots[me_d]

    def a_copy(n):
        return to_dp(0, n, aslots.at[(me_d + n) % n_dp], agot.at[me_m, me_d])

    @pl.loop(1, n_dp)
    def _(n):
        a_copy(n).start()

    hp_sent.wait_recv()
    hp = (hpx[:, kept] + hpgot[...].astype(f32)).astype(bf16)
    hslots[...] = dot(sel[...], hp).astype(bf16).reshape(hslots.shape)
    hgot[me_d] = hslots[me_d]

    def h_copy(n):
        return to_dp(1, n, hslots.at[(me_d + n) % n_dp], hgot.at[me_d])

    @pl.loop(1, n_dp)
    def _(n):
        h_copy(n).start()

    for copy in u_sent:
        copy.wait_recv()
    row = iota((packed, n_seg * packed), 0)
    col = iota((packed, n_seg * packed), 1)
    quad = row >> 2
    block = (quad >= 3).astype(jnp.int32) + (quad >= 6).astype(jnp.int32) + (quad >= 9).astype(jnp.int32)
    got_u = ugot[...].reshape(n_seg * packed, part)
    for g in range(n_seg):
        take = ones_where(col == row + (packed - per) * block + per * g)
        ucat[:, g * part : (g + 1) * part] = dot(take, got_u).astype(bf16)
    u = ucat[...]
    u_scaled = (u.astype(f32) * gain[...].astype(f32)).astype(bf16)
    wide_a[:rows_u, :rank_all] = dot_nt(u_scaled, down[...])
    wide_b[:rows_u, :rank_all] = dot_nt(u, up[...])
    row = iota((rows_u, 2 * LANES), 0)
    quad = row >> 2
    block = (quad >= 3).astype(jnp.int32) + (quad >= 6).astype(jnp.int32) + (quad >= 9).astype(jnp.int32)
    same = (quad - 3 * block) == (iota((rows_u, 2 * LANES), 1) >> 6)
    lane_u = iota((rows_u, LANES), 1)
    mgx[...] = jnp.where(lane_u < RANK, fold(wide_a[:rows_u, :], same), fold(wide_b[:rows_u, :], same))
    mg_sent = to_peer(1, mgx, mggot)
    mg_sent.start()

    def up_tile(n):
        span = pl.ds(pl.multiple_of(n * tile, tile), tile)
        upx[:, span] = dot(ucat[...], p[:, span])

    pl.loop(0, 2)(up_tile)
    mg_sent.wait_recv()
    mgs[me_s] = (mgx[...] + mggot[...]).astype(bf16)
    mg_x = [to_seg(1, n, mgs.at[me_s], mgs.at[me_s]) for n in range(1, n_seg)]
    for copy in mg_x:
        copy.start()

    pl.loop(2, tiles)(up_tile)
    up_sent = to_peer(2, upx.at[:, away], upgot)
    up_sent.start()

    def student(n):
        span = pl.ds(pl.multiple_of(n * tile, tile), tile)
        w_copy(n).wait()
        sox[:, span] = dot(sg[...], w[:, span])

    pl.loop(0, 1)(student)

    for copy in mg_x:
        copy.wait_recv()
    for n in range(pair):
        tables[me_m, me_d, :, n * LANES : (n + 1) * LANES] = mgs[me_m * pair + n]

    def m_copy(n):
        return to_dp(2, n, tables.at[me_m, me_d], tables.at[me_m, me_d])

    @pl.loop(1, n_dp)
    def _(n):
        m_copy(n).start()

    up_sent.wait_recv()
    blocks[me_d] = (upx[:, kept] + upgot[...]).astype(bf16)
    firsts = [gather_first(n) for n in range(1, side)]
    for copy in firsts:
        copy.start()
    seconds = [gather_second(0, n) for n in range(1, side)]
    for copy in seconds:
        copy.start()

    @pl.loop(1, n_dp)
    def _(n):
        a_copy(n).wait_recv()

    a_x = [to_seg(2, n, aall.at[me_s], aall.at[me_s]) for n in range(1, n_seg)]
    extra_swap = to_peer(6, agot.at[1], agot.at[1])

    @pl.when(me_m == 0)
    def _():
        aall[me_s] = agot[0].reshape(slots, LANES)
        for copy in a_x:
            copy.start()

    @pl.when(me_m == 1)
    def _():
        extra_swap.start()

    for m in (0, 1):
        block_landed(m, 2).wait_recv()
    for way in (0, 1):
        plane_copy(way, way, 2).start()
    for n in (1, side - 1):
        for way in (0, 1):
            plane_copy(way, way, n).wait_recv()
            plane_forward(way, n).start()
    for n in (1, side - 1, 2):
        for way in (0, 1):
            plane_copy(way, 1 - way, n).start()

    pl.loop(1, 4)(student)
    for k in range(1, side):
        firsts[k - 1].wait_recv()
        for n in range(1, side):
            copy = gather_second(k, n)
            copy.start()
            seconds.append(copy)

    pl.loop(4, tiles)(student)
    sosend[...] = sox[:, away].astype(bf16)
    so_sent = to_peer(5, sosend, sogot)
    so_sent.start()
    a_swap = to_peer(7, aall, aall)

    @pl.when(me_m == 0)
    def _():
        for copy in a_x:
            copy.wait_recv()
        a_swap.start()

    for way in (0, 1):
        plane_copy(way, way, 2).wait_recv()
        plane_forward(way, 2).start()

    @pl.loop(1, n_dp)
    def _(n):
        m_copy(n).wait_recv()

    table_swap = to_peer(8, tables.at[me_m], tables.at[me_m])
    table_swap.start()

    @pl.when(me_m == 0)
    def _():
        extra_swap.wait_recv()

    @pl.when(me_m == 1)
    def _():
        a_swap.wait_recv()

    xmap_in.wait()
    extra = agot[1].reshape(slots, LANES).astype(f32)
    id_slot = extra[:, 0:1]
    norm = extra[:, 1:2] + extra[:, 2:3]
    keep = kcol[...] == id_slot
    lane = iota((slots, LANES), 1)
    known = rows_u * n_dp
    both = jnp.zeros((slots, LANES), f32)
    table_swap.wait_recv()
    for s in range(n_seg):
        ab = aall[s].astype(f32)
        lat = (ab + both) * lax.rsqrt(jnp.maximum(norm, 0.0) * (1.0 / D) + 1e-06)
        lat = lat.astype(bf16)
        lat_low = jnp.where(lane < RANK, lat.astype(f32), 0.0)
        wide_c = jnp.where(keep, dot(lat_low.astype(bf16), xmap[s]), 0.0).astype(bf16)
        if s == 0:
            ctil[...] = wide_c
        else:
            ctil[...] += wide_c
        if s + 1 < n_seg:
            low, high = (s % pair) * LANES, ((s + 1) % pair) * LANES
            here = tables[s // pair, :, :, low : low + LANES].reshape(known, LANES)
            after = tables[(s + 1) // pair, :, :, high : high + LANES].reshape(known, LANES)
            self_part = dot(ctil[...], here)
            lat_high = pltpu.roll(lat_low, RANK, 1)
            norm = norm + jnp.sum(lat_high * (2.0 * ab + both + self_part), axis=1, keepdims=True)
            both = dot(ctil[...], after)

    @pl.loop(1, n_dp)
    def _(n):
        h_copy(n).wait_recv()

    sx_sent.wait()
    so_sent.wait_recv()
    slot = iota((slots, n_dp), 0)
    source = iota((slots, n_dp), 1)
    room = slot - source * cap
    valid = jnp.sum(
        jnp.where((room >= 0) & (room < cap) & (room < counts[...]), 1.0, 0.0), axis=1, keepdims=True
    )
    square = jnp.sum(sxx[...] + sxgot[...], axis=1, keepdims=True)
    recip = lax.rsqrt(square * (1.0 / S) + 1e-06)
    student_out = (sox[:, kept] + sogot[...].astype(f32)) * recip
    base[...] = jnp.where(valid > 0.0, student_out - hgot[...].reshape(slots, out_half).astype(f32), 0.0)
    sxx[...] = jnp.broadcast_to(recip * (1.0 / TOK_DEV), sxx.shape)
    for copy in seconds:
        copy.wait_recv()
    table = blocks[...].reshape(known, out_half)
    edge = slots // 2

    def gathered(ahead, low=0, count=slots):
        return p.at[pl.ds(ahead * slots + low, count), :out_half]

    def diff_copy(way, part):
        ahead = (side - 1, 1)[way]
        number = way * 2 + part
        return remote(
            gathered(0, part * edge, edge), gathered(ahead, part * edge, edge),
            s_r.at[number], r_r.at[number], dp=place(1 + way * (side - 2), 0),
        )

    def diff_forward(way):
        ahead = (side - 1, 1)[way]
        return remote(
            gathered(ahead, way * edge, edge), gathered(2, way * edge, edge),
            s_r.at[4 + way], r_r.at[4 + way], dp=place(1 + way * (side - 2), 0),
        )

    def difference(part):
        rows = slice(part * edge, (part + 1) * edge)
        diff = base[rows, :] - dot(ctil[rows, :], table)
        gathered(0, part * edge, edge)[...] = (diff * sxx[rows, 0:1]).astype(bf16)
        loss = jnp.sum(diff * diff, axis=1, keepdims=True)
        losspart[:, rows] = jnp.broadcast_to(loss, (edge, LANES)).T[0:1, :]

    difference(0)
    diff_copy(0, 0).start()
    difference(1)
    diff_copy(1, 1).start()
    for way in (0, 1):
        diff_copy(way, 1 - way).start()
    loss_swap = to_peer(9, losspart, lossgot)
    loss_swap.start()
    def product(owner, ahead):
        return dot(nb[owner, ahead].reshape(2 * share, slots), gathered(ahead)[...])

    for n in range(side):
        chip_copy(n).wait_recv()

    @pl.loop(0, side)
    def _(n):
        held[n] = product(n, 0)

    for way in (0, 1):
        diff_copy(way, way).wait_recv()
        diff_forward(way).start()
    loss_swap.wait_recv()
    losses[me_s] = losspart[...] + lossgot[...]
    tells = [to_seg(3, n, losses.at[me_s], losses.at[me_s]) for n in range(1, n_seg)]
    for copy in tells:
        copy.start()
    for way in (0, 1):
        for n in range(1, side):
            plane_copy(way, 1 - way, n).wait_recv()
            plane_forward(way, n).wait_recv()
    for way in (0, 1):
        diff_copy(way, 1 - way).wait_recv()

    @pl.loop(0, side)
    def _(n):
        held[n] += product(n, 1) + product(n, 3)

    for copy in tells:
        copy.wait_recv()
    total = losses[0]
    for n in range(1, n_seg):
        total = total + losses[n]
    loss_out[...] = total * (1.0 / S)

    ring_at = z * other + y * me_m
    below = side * slots

    def sent(slot, m):
        return p.at[pl.ds(below + (slot * 2 + m) * share, share), :out_half]

    def landed(way, msg):
        return p.at[pl.ds(pl.multiple_of(below + (way * 3 + msg) * share, 16), share), out_half:]

    def sum_copy(way, msg):
        slot = 0 if msg == 0 else 1 + way
        m = 1 - way if msg == 1 else way
        number = 6 + way * 3 + msg
        return remote(
            sent(slot, m), landed(way, msg), s_r.at[number], r_r.at[number], dp=place(0, 1 + way * (side - 2))
        )

    for way in (0, 1):
        diff_forward(way).wait_recv()
    far = (ring_at + 2) % side
    nears = [(ring_at + 1) % side, (ring_at + side - 1) % side]

    def half_rows(m):
        return pl.ds(m * share, share)

    block = held[far] + product(far, 2)
    for way in (0, 1):
        sent(0, way)[...] = block[way * share : (way + 1) * share].astype(bf16)
        sum_copy(way, 0).start()
    for way in (0, 1):
        block = held[nears[way]] + product(nears[way], 2)
        sent(1 + way, 1 - way)[...] = block[(1 - way) * share : (2 - way) * share].astype(bf16)
        sum_copy(way, 1).start()
        held[nears[way], half_rows(way)] = block[way * share : (way + 1) * share]
    held[ring_at] += product(ring_at, 2)
    for way in (0, 1):
        sum_copy(way, 0).wait_recv()
        sent(1 + way, way)[...] = (held[nears[way], half_rows(way)] + landed(way, 0)[...].astype(f32)).astype(bf16)
        sum_copy(way, 2).start()
    for msg in (1, 2):
        for way in (0, 1):
            sum_copy(way, msg).wait_recv()

    def summed(m):
        mine = held[ring_at, pl.ds(pl.multiple_of(m * share, share), share)]
        return mine + landed(0, 2 - m)[...].astype(f32) + landed(1, 1 + m)[...].astype(f32)

    finsend[...] = summed(other)
    last_swap = to_peer(10, finsend, fingot)
    last_swap.start()
    out[:, kept] = summed(me_m)
    last_swap.wait_recv()
    out[:, away] = fingot[...]

    for n in range(1, side):
        for f in (0, 1):
            block_copy(f, n).wait_send()
    for n in range(side):
        chip_copy(n).wait_send()
    for way in (0, 1):
        for n in range(1, side):
            for m in (0, 1):
                plane_copy(way, m, n).wait_send()
            plane_forward(way, n).wait_send()
        for m in (0, 1):
            diff_copy(way, m).wait_send()
        diff_forward(way).wait_send()
        for msg in range(3):
            sum_copy(way, msg).wait_send()
    for copy in u_sent + mg_x + firsts + seconds + [ab_sent, mg_sent, up_sent, hp_sent, so_sent, table_swap, loss_swap, last_swap] + tells:
        copy.wait_send()

    @pl.when(me_m == 0)
    def _():
        for copy in a_x + [a_swap]:
            copy.wait_send()

    @pl.when(me_m == 1)
    def _():
        extra_swap.wait_send()

    @pl.loop(1, n_dp)
    def _(n):
        a_copy(n).wait_send()
        m_copy(n).wait_send()
        h_copy(n).wait_send()


def run_step(h, ids, dest, counts, gain, down, up, x, sgain, w, p):
    side = 4
    n_seg = lax.axis_size("segment")
    n_dp = lax.axis_size("dp")
    tok, half = h.shape
    slots, width = x.shape
    cols = p.shape[1]
    out_half = cols // 2
    cap = slots // n_dp
    q = RANK // n_dp
    per = TEACH * q
    rows_u = n_seg * per
    known = rows_u * n_dp
    share = width // n_dp
    c = np.arange(known)
    c_i, c_t, c_k, c_q = c // rows_u, c % rows_u // per, c % per // q, c % q
    spot = np.arange(LANES)[None, :, None]
    xmap = (np.arange(n_seg)[:, None, None] == c_t) & (spot == c_i * q + c_q)
    xmap = jnp.asarray(xmap.astype(np.float32), dtype=bf16)
    kcol = jnp.asarray(c_k[None, :].astype(np.float32))
    vmem = pl.BlockSpec(memory_space=pltpu.VMEM)
    hbm = pl.BlockSpec(memory_space=pl.ANY)
    flops = 2 * (tok * half * cols + 2 * slots * width * cols)
    scratch = [
        (h.shape, bf16), (down.shape, bf16), (up.shape, bf16), (x.shape, bf16), (w.shape, bf16), (p.shape, bf16),
        (xmap.shape, bf16),
        ((rows_u, half // n_seg), bf16), ((n_seg, rows_u, half // n_seg), bf16), ((rows_u, half), bf16),
        ((tok, 2 * LANES), f32), ((tok, 2 * LANES), f32), ((tok, 2 * LANES), f32), ((tok, 2 * LANES), f32),
        ((slots, tok), bf16), ((tok, 2 * LANES), bf16),
        ((n_dp, cap, LANES), bf16), ((2, n_dp, cap, LANES), bf16), ((n_seg, slots, LANES), bf16),
        ((rows_u, LANES), f32), ((rows_u, LANES), f32), ((n_seg, rows_u, LANES), bf16),
        ((rows_u, cols), f32), ((rows_u, out_half), f32),
        ((n_dp, rows_u, out_half), bf16), ((2, n_dp, rows_u, n_seg // 2 * LANES), bf16),
        ((tok, cols), f32), ((tok, out_half), bf16), ((tok, out_half), bf16),
        ((n_dp, cap, out_half), bf16), ((n_dp, cap, out_half), bf16),
        (x.shape, bf16), ((slots, cols), f32), ((slots, out_half), bf16), ((slots, out_half), bf16),
        ((slots, LANES), f32), ((slots, LANES), f32), ((slots, known), bf16), ((slots, out_half), f32),
        ((width, slots), bf16), ((n_seg, side, 2, share, slots), bf16), ((side, 2 * share, out_half), f32),
        ((share, out_half), f32), ((share, out_half), f32),
        ((1, slots), f32), ((1, slots), f32), ((n_seg, 1, slots), f32),
    ]
    sems = [5 + cols // LANES, 11, 11, 4 * (n_seg - 1), 4 * (n_seg - 1), 4 * (n_dp - 1), 4 * (n_dp - 1), 28, 28, 12, 12]
    return pl.pallas_call(
        functools.partial(step_kernel, n_seg, side, cap),
        out_shape=(
            jax.ShapeDtypeStruct((share, cols), f32),
            jax.ShapeDtypeStruct((1, slots), f32),
        ),
        in_specs=[hbm] * 7 + [vmem] * 6,
        out_specs=(vmem, vmem),
        scratch_shapes=[pltpu.VMEM(*s) for s in scratch] + [pltpu.SemaphoreType.DMA((n,)) for n in sems],
        compiler_params=pltpu.CompilerParams(
            collective_id=0, has_side_effects=True, vmem_limit_bytes=60 * 2**20
        ),
        cost_estimate=pl.CostEstimate(flops=flops, bytes_accessed=25 * 2**20, transcendentals=0),
    )(
        h, down, up, x, w, p, xmap,
        ids.reshape(1, tok), dest.reshape(1, tok), counts, gain, sgain.reshape(width // LANES, LANES), kcol,
    )


def finish_kernel(grad, loss, grad_out, loss_out):
    grad_out[...] = grad[...]
    loss_out[...] = loss[...]


def finish(grad, loss):
    vmem = pl.BlockSpec(memory_space=pltpu.VMEM)
    return pl.pallas_call(
        finish_kernel,
        out_shape=(jax.ShapeDtypeStruct(grad.shape, f32), jax.ShapeDtypeStruct(loss.shape, f32)),
        in_specs=[vmem, vmem],
        out_specs=(vmem, vmem),
    )(grad, loss)


def local(
    teacher_hidden,
    teacher_id,
    destination,
    row_counts,
    section_gain,
    adapter_down,
    adapter_up,
    student_in,
    student_gain,
    student_weight,
    projector,
):
    weight_grad, row_loss = run_step(
        teacher_hidden,
        teacher_id,
        destination,
        row_counts,
        section_gain,
        adapter_down[0].T,
        adapter_up[0],
        student_in,
        student_gain,
        student_weight,
        projector,
    )
    weight_grad, row_loss = finish(weight_grad, row_loss)
    share, cols = weight_grad.shape
    return (weight_grad.reshape(1, share, cols), row_loss.reshape(student_in.shape[0]))


def solution(mesh):
    placed = (
        P("dp", "mp"),
        P("dp"),
        P("dp"),
        P("dp", None),
        P("segment", "mp"),
        P("segment", "mp", None),
        P("segment", None, "mp"),
        P("dp", "mp"),
        P("mp"),
        P("mp", "segment"),
        P("mp", "segment"),
    )
    return jax.shard_map(
        local,
        mesh=mesh,
        in_specs=placed,
        out_specs=(P("mp", "dp", "segment"), P("dp")),
        check_vma=False,
    )
```

```python
import functools

import jax
import jax.numpy as jnp
import numpy as np
from jax import lax
from jax.experimental import pallas as pl
from jax.experimental.pallas import tpu as pltpu
from jax.sharding import PartitionSpec as P

D = 8192
S = 5120
RANK = 64
TOK_DEV = 256
TEACH = 3
LANES = 128
bf16 = jnp.bfloat16
f32 = jnp.float32


def dot(a, b):
    return jnp.dot(a, b, preferred_element_type=f32)


def remote(src, dst, send, recv, **where):
    return pltpu.make_async_remote_copy(
        src_ref=src,
        dst_ref=dst,
        send_sem=send,
        recv_sem=recv,
        device_id=where,
        device_id_type=pl.DeviceIdType.MESH,
    )


def iota(shape, dim):
    return lax.broadcasted_iota(jnp.int32, shape, dim)


def ones_where(mask):
    return jnp.where(mask, 1.0, 0.0).astype(bf16)


def dot_nt(a, b):
    return lax.dot_general(a, b, (((1,), (1,)), ((), ())), preferred_element_type=f32)


def turned(row):
    return jnp.broadcast_to(row, (LANES, row.shape[1])).T


def fold(wide, keep):
    kept = jnp.where(keep, wide, 0.0)
    both = kept[:, :LANES] + kept[:, LANES:]
    return both + pltpu.roll(both, RANK, 1)


def step_kernel(
    n_seg, side, cap,
    h_hbm, down_hbm, up_hbm, x_hbm, w_hbm, p_hbm, xmap_hbm,
    ids, dest, counts, gain, sgain, kcol,
    out, loss_out,
    h, down, up, x, w, p, xmap,
    usend, ugot, ucat, wide_a, wide_b, abx, abgot, sel, pay, aslots, agot, aall,
    mgx, mggot, mgs, upx, upgot, blocks, tables,
    hpx, hpsend, hpgot, hslots, hgot,
    sg, sox, sosend, sogot, sxx, sxgot, ctil, base,
    sgt, nb, held, finsend, fingot, losspart, lossgot, losses,
    lsem, s_m, r_m, s_x, r_x, s_d, r_d, s_n, r_n, s_r, r_r,
):
    me_s = lax.axis_index("segment")
    me_m = lax.axis_index("mp")
    me_d = lax.axis_index("dp")
    other = 1 - me_m
    n_dp = side * side
    tok, half = h.shape
    slots = x.shape[0]
    cols = p.shape[1]
    out_half = cols // 2
    rows_u = mgx.shape[0]
    per = rows_u // n_seg
    part = half // n_seg
    tile = 2 * LANES
    tiles = cols // tile
    pair = n_seg // 2

    def load(n, src, dst):
        copy = pltpu.make_async_copy(src, dst, lsem.at[n])
        copy.start()
        return copy

    def p_copy(n):
        span = pl.ds(pl.multiple_of(n * tile, tile), tile)
        return pltpu.make_async_copy(p_hbm.at[:, span], p.at[:, span], lsem.at[5 + n])

    def w_copy(n):
        span = pl.ds(pl.multiple_of(n * tile, tile), tile)
        return pltpu.make_async_copy(w_hbm.at[:, span], w.at[:, span], lsem.at[5 + tiles + n])

    up_in = load(0, up_hbm, up)
    x_in = load(3, x_hbm, x)
    h_in = load(1, h_hbm, h)
    for n in range(tiles):
        p_copy(n).start()
    down_in = load(2, down_hbm, down)
    for n in range(tiles):
        w_copy(n).start()
    xmap_in = load(4, xmap_hbm, xmap)

    z = me_d // side
    y = me_d % side

    def place(first, second):
        a = ((z * other + y * me_m) + second) % side
        b = ((y * other + z * me_m) + first) % side
        return (a * other + b * me_m) * side + b * other + a * me_m

    barrier = pltpu.get_barrier_semaphore()
    mesh_id = pl.DeviceIdType.MESH
    pl.semaphore_signal(barrier, inc=1, device_id={"mp": other}, device_id_type=mesh_id)
    for n in range(1, n_seg):
        pl.semaphore_signal(barrier, inc=1, device_id={"segment": (me_s + n) % n_seg}, device_id_type=mesh_id)

    @pl.loop(1, n_dp)
    def _(n):
        pl.semaphore_signal(barrier, inc=1, device_id={"dp": (me_d + n) % n_dp}, device_id_type=mesh_id)

    for n in range(1, side):
        pl.semaphore_signal(barrier, inc=1, device_id={"dp": place(n, 0), "mp": other}, device_id_type=mesh_id)

    def to_peer(n, src, dst):
        return remote(src, dst, s_m.at[n], r_m.at[n], mp=other)

    def to_seg(kind, n, src, dst):
        number = kind * (n_seg - 1) + n - 1
        return remote(src, dst, s_x.at[number], r_x.at[number], segment=(me_s + n) % n_seg)

    def to_dp(kind, n, src, dst):
        number = kind * (n_dp - 1) + n - 1
        return remote(src, dst, s_d.at[number], r_d.at[number], dp=(me_d + n) % n_dp)

    def gather_first(n):
        return remote(blocks.at[me_d], blocks.at[me_d], s_d.at[n + 44], r_d.at[n + 44], dp=place(n, 0))

    def gather_second(k, n):
        source = place(side - k, 0)
        number = 48 + k * (side - 1) + n - 1
        return remote(blocks.at[source], blocks.at[source], s_d.at[number], r_d.at[number], dp=place(0, n))

    packed = n_seg * per
    row = iota((packed, up.shape[0]), 0)
    col = iota((packed, up.shape[0]), 1)
    quad = row >> 2
    block = (quad >= 3).astype(jnp.int32) + (quad >= 6).astype(jnp.int32) + (quad >= 9).astype(jnp.int32)
    teacher = quad - 3 * block
    hit = ((col >> 6) == teacher) & (((col & 63) >> 2) == me_d) & ((col & 3) == (row & 3))
    up_in.wait()
    mine = jnp.zeros((packed, part), f32)
    for g in range(n_seg):
        mine = mine + dot(ones_where(hit & (block == g)), up[:, g * part : (g + 1) * part])
    usend[...] = mine.astype(bf16)
    ugot[me_s] = usend[...]
    wide_a[...] = jnp.zeros(wide_a.shape, f32)
    wide_b[...] = jnp.zeros(wide_b.shape, f32)
    abx[...] = jnp.zeros(abx.shape, f32)

    x_in.wait()
    sxx[...] = jnp.zeros(sxx.shape, f32)

    @pl.loop(0, x.shape[1] // LANES)
    def _(n):
        span = pl.ds(pl.multiple_of(n * LANES, LANES), LANES)
        wide = x[:, span].astype(f32)
        sxx[...] += wide * wide
        scaled = (wide * sgain[pl.ds(n, 1), :]).astype(bf16)
        sg[:, span] = scaled
        sgt[span, :] = scaled.T

    pl.semaphore_wait(barrier, 1 + (n_seg - 1) + (n_dp - 1) + (side - 1))
    u_sent = [to_seg(0, n, usend, ugot.at[me_s]) for n in range(1, n_seg)]
    for copy in u_sent:
        copy.start()

    share = out.shape[0]

    def rows_of(owner):
        return sgt.at[pl.ds(pl.multiple_of(owner * share, share), share)]

    def owner_of(f, other_ring):
        return (1 - f) * (other_ring * side + y) + f * (z * side + other_ring)

    def block_copy(f, n):
        if f == 0:
            where = z * side + (y + n) % side
            owner = me_s * side + (y + n) % side
        else:
            where = ((z + n) % side) * side + y
            owner = ((z + n) % side) * side + me_s
        number = f * (side - 1) + n - 1
        return remote(
            rows_of(owner), nb.at[me_s, side - n, me_m], s_n.at[number], r_n.at[(n - 1) * 2 + me_m], dp=where, mp=f
        )

    def block_landed(m, n):
        where = nb.at[me_s, side - n, m]
        return remote(where, where, s_n.at[0], r_n.at[(n - 1) * 2 + m], mp=other)

    def chip_copy(n):
        return remote(rows_of(owner_of(other, n)), nb.at[n, 0, me_m], s_n.at[6 + n], r_n.at[6 + n], mp=other)

    def plane_copy(way, m, k):
        number = 10 + (way * 2 + m) * (side - 1) + k - 1
        block = nb.at[me_s, k, m]
        return remote(block, block, s_n.at[number], r_n.at[number], segment=(me_s + 1 + way * (n_seg - 2)) % n_seg)

    def plane_forward(way, k):
        number = 10 + (4 + way) * (side - 1) + k - 1
        block = nb.at[(me_s + n_seg - 1 + 2 * way) % n_seg, k, way]
        return remote(block, block, s_n.at[number], r_n.at[number], segment=(me_s + 1 + way * (n_seg - 2)) % n_seg)

    for n in (1, side - 1, 2):
        for f in (0, 1):
            block_copy(f, n).start()
    for n in range(side):
        chip_copy(n).start()
    sx_sent = to_peer(4, sxx, sxgot)
    sx_sent.start()
    for n in range(side):
        nb[n, 0, me_m] = rows_of(owner_of(me_m, n))[...]

    away = pl.ds(pl.multiple_of(other * out_half, LANES), out_half)
    kept = pl.ds(pl.multiple_of(me_m * out_half, LANES), out_half)
    h_in.wait()
    down_in.wait()
    rank_all = down.shape[0]

    @pl.loop(0, n_seg)
    def _(g):
        span = pl.ds(pl.multiple_of(g * part, part), part)
        here = h[:, span]
        wide = here.astype(f32)
        scaled = (wide * gain[:, span].astype(f32)).astype(bf16)
        wide_a[:, :rank_all] += dot_nt(scaled, down[:, span])
        wide_b[:, :rank_all] += dot_nt(here, up[:, span])
        abx[:, LANES:] += jnp.broadcast_to(jnp.sum(wide * wide, axis=1, keepdims=True), (tok, LANES))

    id_col = turned(ids[...].astype(f32))
    lane2 = iota((tok, 2 * LANES), 1)
    own = (lane2 >> 6).astype(f32) == jnp.concatenate([id_col, id_col], axis=1)
    lane = iota((tok, LANES), 1)
    abx[:, :LANES] = jnp.where(lane < RANK, fold(wide_a[...], own), fold(wide_b[...], own))
    ab_sent = to_peer(0, abx, abgot)
    ab_sent.start()


    @pl.loop(0, tiles)
    def _(n):
        span = pl.ds(pl.multiple_of(n * tile, tile), tile)
        p_copy(n).wait()
        hpx[:, span] = dot(h[...], p[:, span])

    hpsend[...] = hpx[:, away].astype(bf16)
    hp_sent = to_peer(3, hpsend, hpgot)
    hp_sent.start()
    for n in (1, side - 1):
        for m in (0, 1):
            block_landed(m, n).wait_recv()
    for n in (1, side - 1):
        for way in (0, 1):
            plane_copy(way, way, n).start()

    dest_f = dest[...].astype(f32)
    onehot = jnp.where(iota((n_dp, tok), 0).astype(f32) == dest_f, 1.0, 0.0)
    before = ones_where(iota((tok, tok), 0) < iota((tok, tok), 1))
    earlier = dot(onehot.astype(bf16), before)
    position = dest_f * cap + jnp.sum(earlier * onehot, axis=0, keepdims=True)
    sel[...] = ones_where(iota((slots, tok), 0).astype(f32) == position)
    ab_sent.wait_recv()
    total = abx[...] + abgot[...]
    sq = total[:, LANES:]
    sq_hi = sq.astype(bf16).astype(f32)
    extra = jnp.where(lane == 0, id_col, jnp.where(lane == 1, sq_hi, jnp.where(lane == 2, sq - sq_hi, 0.0)))
    pay[:, :LANES] = total[:, :LANES].astype(bf16)
    pay[:, LANES:] = extra.astype(bf16)
    lanes_here = pl.ds(pl.multiple_of(me_m * LANES, LANES), LANES)
    aslots[...] = dot(sel[...], pay[:, lanes_here]).astype(bf16).reshape(aslots.shape)
    agot[me_m, me_d] = aslots[me_d]

    def a_copy(n):
        return to_dp(0, n, aslots.at[(me_d + n) % n_dp], agot.at[me_m, me_d])

    @pl.loop(1, n_dp)
    def _(n):
        a_copy(n).start()

    hp_sent.wait_recv()
    hp = (hpx[:, kept] + hpgot[...].astype(f32)).astype(bf16)
    hslots[...] = dot(sel[...], hp).astype(bf16).reshape(hslots.shape)
    hgot[me_d] = hslots[me_d]

    def h_copy(n):
        return to_dp(1, n, hslots.at[(me_d + n) % n_dp], hgot.at[me_d])

    @pl.loop(1, n_dp)
    def _(n):
        h_copy(n).start()

    for copy in u_sent:
        copy.wait_recv()
    row = iota((packed, n_seg * packed), 0)
    col = iota((packed, n_seg * packed), 1)
    quad = row >> 2
    block = (quad >= 3).astype(jnp.int32) + (quad >= 6).astype(jnp.int32) + (quad >= 9).astype(jnp.int32)
    got_u = ugot[...].reshape(n_seg * packed, part)
    for g in range(n_seg):
        take = ones_where(col == row + (packed - per) * block + per * g)
        ucat[:, g * part : (g + 1) * part] = dot(take, got_u).astype(bf16)
    u = ucat[...]
    u_scaled = (u.astype(f32) * gain[...].astype(f32)).astype(bf16)
    wide_a[:rows_u, :rank_all] = dot_nt(u_scaled, down[...])
    wide_b[:rows_u, :rank_all] = dot_nt(u, up[...])
    row = iota((rows_u, 2 * LANES), 0)
    quad = row >> 2
    block = (quad >= 3).astype(jnp.int32) + (quad >= 6).astype(jnp.int32) + (quad >= 9).astype(jnp.int32)
    same = (quad - 3 * block) == (iota((rows_u, 2 * LANES), 1) >> 6)
    lane_u = iota((rows_u, LANES), 1)
    mgx[...] = jnp.where(lane_u < RANK, fold(wide_a[:rows_u, :], same), fold(wide_b[:rows_u, :], same))
    mg_sent = to_peer(1, mgx, mggot)
    mg_sent.start()

    def up_tile(n):
        span = pl.ds(pl.multiple_of(n * tile, tile), tile)
        upx[:, span] = dot(ucat[...], p[:, span])

    pl.loop(0, 2)(up_tile)
    mg_sent.wait_recv()
    mgs[me_s] = (mgx[...] + mggot[...]).astype(bf16)
    mg_x = [to_seg(1, n, mgs.at[me_s], mgs.at[me_s]) for n in range(1, n_seg)]
    for copy in mg_x:
        copy.start()

    pl.loop(2, tiles)(up_tile)
    up_sent = to_peer(2, upx.at[:, away], upgot)
    up_sent.start()

    def student(n):
        span = pl.ds(pl.multiple_of(n * tile, tile), tile)
        w_copy(n).wait()
        sox[:, span] = dot(sg[...], w[:, span])

    pl.loop(0, 1)(student)

    up_sent.wait_recv()
    blocks[me_d] = (upx[:, kept] + upgot[...]).astype(bf16)
    firsts = [gather_first(n) for n in range(1, side)]
    for copy in firsts:
        copy.start()
    seconds = [gather_second(0, n) for n in range(1, side)]
    for copy in seconds:
        copy.start()

    for copy in mg_x:
        copy.wait_recv()
    for n in range(pair):
        tables[me_m, me_d, :, n * LANES : (n + 1) * LANES] = mgs[me_m * pair + n]

    def m_copy(n):
        return to_dp(2, n, tables.at[me_m, me_d], tables.at[me_m, me_d])

    @pl.loop(1, n_dp)
    def _(n):
        m_copy(n).start()

    @pl.loop(1, n_dp)
    def _(n):
        a_copy(n).wait_recv()

    a_x = [to_seg(2, n, aall.at[me_s], aall.at[me_s]) for n in range(1, n_seg)]
    extra_swap = to_peer(6, agot.at[1], agot.at[1])

    @pl.when(me_m == 0)
    def _():
        aall[me_s] = agot[0].reshape(slots, LANES)
        for copy in a_x:
            copy.start()

    @pl.when(me_m == 1)
    def _():
        extra_swap.start()

    for m in (0, 1):
        block_landed(m, 2).wait_recv()
    for way in (0, 1):
        plane_copy(way, way, 2).start()
    for n in (1, side - 1, 2):
        for way in (0, 1):
            plane_copy(way, 1 - way, n).start()

    pl.loop(1, 3)(student)

    def gather_on(k):
        firsts[k - 1].wait_recv()
        copies = [gather_second(k, n) for n in range(1, side)]
        for copy in copies:
            copy.start()
        return copies

    seconds += gather_on(1) + gather_on(side - 1)
    pl.loop(3, 4)(student)
    seconds += gather_on(2)
    pl.loop(4, tiles)(student)
    sosend[...] = sox[:, away].astype(bf16)
    so_sent = to_peer(5, sosend, sogot)
    so_sent.start()
    a_swap = to_peer(7, aall, aall)

    @pl.when(me_m == 0)
    def _():
        for copy in a_x:
            copy.wait_recv()
        a_swap.start()

    for n in (1, side - 1, 2):
        for way in (0, 1):
            plane_copy(way, way, n).wait_recv()
            plane_forward(way, n).start()

    @pl.loop(1, n_dp)
    def _(n):
        m_copy(n).wait_recv()

    table_swap = to_peer(8, tables.at[me_m], tables.at[me_m])
    table_swap.start()

    @pl.when(me_m == 0)
    def _():
        extra_swap.wait_recv()

    @pl.when(me_m == 1)
    def _():
        a_swap.wait_recv()

    xmap_in.wait()
    extra = agot[1].reshape(slots, LANES).astype(f32)
    id_slot = extra[:, 0:1]
    norm = extra[:, 1:2] + extra[:, 2:3]
    keep = kcol[...] == id_slot
    lane = iota((slots, LANES), 1)
    known = rows_u * n_dp
    both = jnp.zeros((slots, LANES), f32)
    table_swap.wait_recv()
    for s in range(n_seg):
        ab = aall[s].astype(f32)
        lat = (ab + both) * lax.rsqrt(jnp.maximum(norm, 0.0) * (1.0 / D) + 1e-06)
        lat = lat.astype(bf16)
        lat_low = jnp.where(lane < RANK, lat.astype(f32), 0.0)
        wide_c = jnp.where(keep, dot(lat_low.astype(bf16), xmap[s]), 0.0).astype(bf16)
        if s == 0:
            ctil[...] = wide_c
        else:
            ctil[...] += wide_c
        if s + 1 < n_seg:
            low, high = (s % pair) * LANES, ((s + 1) % pair) * LANES
            here = tables[s // pair, :, :, low : low + LANES].reshape(known, LANES)
            after = tables[(s + 1) // pair, :, :, high : high + LANES].reshape(known, LANES)
            self_part = dot(ctil[...], here)
            lat_high = pltpu.roll(lat_low, RANK, 1)
            norm = norm + jnp.sum(lat_high * (2.0 * ab + both + self_part), axis=1, keepdims=True)
            both = dot(ctil[...], after)

    @pl.loop(1, n_dp)
    def _(n):
        h_copy(n).wait_recv()

    sx_sent.wait()
    so_sent.wait_recv()
    slot = iota((slots, n_dp), 0)
    source = iota((slots, n_dp), 1)
    room = slot - source * cap
    valid = jnp.sum(
        jnp.where((room >= 0) & (room < cap) & (room < counts[...]), 1.0, 0.0), axis=1, keepdims=True
    )
    square = jnp.sum(sxx[...] + sxgot[...], axis=1, keepdims=True)
    recip = lax.rsqrt(square * (1.0 / S) + 1e-06)
    student_out = (sox[:, kept] + sogot[...].astype(f32)) * recip
    base[...] = jnp.where(valid > 0.0, student_out - hgot[...].reshape(slots, out_half).astype(f32), 0.0)
    sxx[...] = jnp.broadcast_to(recip * (1.0 / TOK_DEV), sxx.shape)
    for copy in seconds:
        copy.wait_recv()
    table = blocks[...].reshape(known, out_half)
    edge = slots // 2

    def gathered(ahead, low=0, count=slots):
        return p.at[pl.ds(ahead * slots + low, count), :out_half]

    def diff_copy(way, part):
        ahead = (side - 1, 1)[way]
        number = way * 2 + part
        return remote(
            gathered(0, part * edge, edge), gathered(ahead, part * edge, edge),
            s_r.at[number], r_r.at[number], dp=place(1 + way * (side - 2), 0),
        )

    def diff_forward(way):
        ahead = (side - 1, 1)[way]
        return remote(
            gathered(ahead, way * edge, edge), gathered(2, way * edge, edge),
            s_r.at[4 + way], r_r.at[4 + way], dp=place(1 + way * (side - 2), 0),
        )

    def difference(part):
        rows = slice(part * edge, (part + 1) * edge)
        diff = base[rows, :] - dot(ctil[rows, :], table)
        gathered(0, part * edge, edge)[...] = (diff * sxx[rows, 0:1]).astype(bf16)
        loss = jnp.sum(diff * diff, axis=1, keepdims=True)
        losspart[:, rows] = jnp.broadcast_to(loss, (edge, LANES)).T[0:1, :]

    difference(0)
    diff_copy(0, 0).start()
    difference(1)
    diff_copy(1, 1).start()
    for way in (0, 1):
        diff_copy(way, 1 - way).start()
    loss_swap = to_peer(9, losspart, lossgot)
    loss_swap.start()
    def product(owner, ahead):
        return dot(nb[owner, ahead].reshape(2 * share, slots), gathered(ahead)[...])

    for n in range(side):
        chip_copy(n).wait_recv()

    @pl.loop(0, side)
    def _(n):
        held[n] = product(n, 0)

    for way in (0, 1):
        diff_copy(way, way).wait_recv()
        diff_forward(way).start()
    loss_swap.wait_recv()
    losses[me_s] = losspart[...] + lossgot[...]
    tells = [to_seg(3, n, losses.at[me_s], losses.at[me_s]) for n in range(1, n_seg)]
    for copy in tells:
        copy.start()
    for way in (0, 1):
        for n in range(1, side):
            plane_copy(way, 1 - way, n).wait_recv()
            plane_forward(way, n).wait_recv()
    for way in (0, 1):
        diff_copy(way, 1 - way).wait_recv()

    @pl.loop(0, side)
    def _(n):
        held[n] += product(n, 1) + product(n, 3)

    for copy in tells:
        copy.wait_recv()
    total = losses[0]
    for n in range(1, n_seg):
        total = total + losses[n]
    loss_out[...] = total * (1.0 / S)

    ring_at = z * other + y * me_m
    below = side * slots

    def sent(slot, m):
        return p.at[pl.ds(below + (slot * 2 + m) * share, share), :out_half]

    def landed(way, msg):
        return p.at[pl.ds(pl.multiple_of(below + (way * 3 + msg) * share, 16), share), out_half:]

    def sum_copy(way, msg):
        slot = 0 if msg == 0 else 1 + way
        m = 1 - way if msg == 1 else way
        number = 6 + way * 3 + msg
        return remote(
            sent(slot, m), landed(way, msg), s_r.at[number], r_r.at[number], dp=place(0, 1 + way * (side - 2))
        )

    for way in (0, 1):
        diff_forward(way).wait_recv()
    far = (ring_at + 2) % side
    nears = [(ring_at + 1) % side, (ring_at + side - 1) % side]

    def half_rows(m):
        return pl.ds(m * share, share)

    block = held[far] + product(far, 2)
    for way in (0, 1):
        sent(0, way)[...] = block[way * share : (way + 1) * share].astype(bf16)
        sum_copy(way, 0).start()
    for way in (0, 1):
        block = held[nears[way]] + product(nears[way], 2)
        sent(1 + way, 1 - way)[...] = block[(1 - way) * share : (2 - way) * share].astype(bf16)
        sum_copy(way, 1).start()
        held[nears[way], half_rows(way)] = block[way * share : (way + 1) * share]
    held[ring_at] += product(ring_at, 2)
    for way in (0, 1):
        sum_copy(way, 0).wait_recv()
        sent(1 + way, way)[...] = (held[nears[way], half_rows(way)] + landed(way, 0)[...].astype(f32)).astype(bf16)
        sum_copy(way, 2).start()
    for msg in (1, 2):
        for way in (0, 1):
            sum_copy(way, msg).wait_recv()

    def summed(m):
        mine = held[ring_at, pl.ds(pl.multiple_of(m * share, share), share)]
        return mine + landed(0, 2 - m)[...].astype(f32) + landed(1, 1 + m)[...].astype(f32)

    finsend[...] = summed(other)
    last_swap = to_peer(10, finsend, fingot)
    last_swap.start()
    out[:, kept] = summed(me_m)
    last_swap.wait_recv()
    out[:, away] = fingot[...]

    for n in range(1, side):
        for f in (0, 1):
            block_copy(f, n).wait_send()
    for n in range(side):
        chip_copy(n).wait_send()
    for way in (0, 1):
        for n in range(1, side):
            for m in (0, 1):
                plane_copy(way, m, n).wait_send()
            plane_forward(way, n).wait_send()
        for m in (0, 1):
            diff_copy(way, m).wait_send()
        diff_forward(way).wait_send()
        for msg in range(3):
            sum_copy(way, msg).wait_send()
    for copy in u_sent + mg_x + firsts + seconds + [ab_sent, mg_sent, up_sent, hp_sent, so_sent, table_swap, loss_swap, last_swap] + tells:
        copy.wait_send()

    @pl.when(me_m == 0)
    def _():
        for copy in a_x + [a_swap]:
            copy.wait_send()

    @pl.when(me_m == 1)
    def _():
        extra_swap.wait_send()

    @pl.loop(1, n_dp)
    def _(n):
        a_copy(n).wait_send()
        m_copy(n).wait_send()
        h_copy(n).wait_send()


def run_step(h, ids, dest, counts, gain, down, up, x, sgain, w, p):
    side = 4
    n_seg = lax.axis_size("segment")
    n_dp = lax.axis_size("dp")
    tok, half = h.shape
    slots, width = x.shape
    cols = p.shape[1]
    out_half = cols // 2
    cap = slots // n_dp
    q = RANK // n_dp
    per = TEACH * q
    rows_u = n_seg * per
    known = rows_u * n_dp
    share = width // n_dp
    c = np.arange(known)
    c_i, c_t, c_k, c_q = c // rows_u, c % rows_u // per, c % per // q, c % q
    spot = np.arange(LANES)[None, :, None]
    xmap = (np.arange(n_seg)[:, None, None] == c_t) & (spot == c_i * q + c_q)
    xmap = jnp.asarray(xmap.astype(np.float32), dtype=bf16)
    kcol = jnp.asarray(c_k[None, :].astype(np.float32))
    vmem = pl.BlockSpec(memory_space=pltpu.VMEM)
    hbm = pl.BlockSpec(memory_space=pl.ANY)
    flops = 2 * (tok * half * cols + 2 * slots * width * cols)
    scratch = [
        (h.shape, bf16), (down.shape, bf16), (up.shape, bf16), (x.shape, bf16), (w.shape, bf16), (p.shape, bf16),
        (xmap.shape, bf16),
        ((rows_u, half // n_seg), bf16), ((n_seg, rows_u, half // n_seg), bf16), ((rows_u, half), bf16),
        ((tok, 2 * LANES), f32), ((tok, 2 * LANES), f32), ((tok, 2 * LANES), f32), ((tok, 2 * LANES), f32),
        ((slots, tok), bf16), ((tok, 2 * LANES), bf16),
        ((n_dp, cap, LANES), bf16), ((2, n_dp, cap, LANES), bf16), ((n_seg, slots, LANES), bf16),
        ((rows_u, LANES), f32), ((rows_u, LANES), f32), ((n_seg, rows_u, LANES), bf16),
        ((rows_u, cols), f32), ((rows_u, out_half), f32),
        ((n_dp, rows_u, out_half), bf16), ((2, n_dp, rows_u, n_seg // 2 * LANES), bf16),
        ((tok, cols), f32), ((tok, out_half), bf16), ((tok, out_half), bf16),
        ((n_dp, cap, out_half), bf16), ((n_dp, cap, out_half), bf16),
        (x.shape, bf16), ((slots, cols), f32), ((slots, out_half), bf16), ((slots, out_half), bf16),
        ((slots, LANES), f32), ((slots, LANES), f32), ((slots, known), bf16), ((slots, out_half), f32),
        ((width, slots), bf16), ((n_seg, side, 2, share, slots), bf16), ((side, 2 * share, out_half), f32),
        ((share, out_half), f32), ((share, out_half), f32),
        ((1, slots), f32), ((1, slots), f32), ((n_seg, 1, slots), f32),
    ]
    sems = [5 + cols // LANES, 11, 11, 4 * (n_seg - 1), 4 * (n_seg - 1), 4 * (n_dp - 1), 4 * (n_dp - 1), 28, 28, 12, 12]
    return pl.pallas_call(
        functools.partial(step_kernel, n_seg, side, cap),
        out_shape=(
            jax.ShapeDtypeStruct((share, cols), f32),
            jax.ShapeDtypeStruct((1, slots), f32),
        ),
        in_specs=[hbm] * 7 + [vmem] * 6,
        out_specs=(vmem, vmem),
        scratch_shapes=[pltpu.VMEM(*s) for s in scratch] + [pltpu.SemaphoreType.DMA((n,)) for n in sems],
        compiler_params=pltpu.CompilerParams(
            collective_id=0, has_side_effects=True, vmem_limit_bytes=60 * 2**20
        ),
        cost_estimate=pl.CostEstimate(flops=flops, bytes_accessed=25 * 2**20, transcendentals=0),
    )(
        h, down, up, x, w, p, xmap,
        ids.reshape(1, tok), dest.reshape(1, tok), counts, gain, sgain.reshape(width // LANES, LANES), kcol,
    )


def finish_kernel(grad, loss, grad_out, loss_out):
    grad_out[...] = grad[...]
    loss_out[...] = loss[...]


def finish(grad, loss):
    vmem = pl.BlockSpec(memory_space=pltpu.VMEM)
    return pl.pallas_call(
        finish_kernel,
        out_shape=(jax.ShapeDtypeStruct(grad.shape, f32), jax.ShapeDtypeStruct(loss.shape, f32)),
        in_specs=[vmem, vmem],
        out_specs=(vmem, vmem),
    )(grad, loss)


def local(
    teacher_hidden,
    teacher_id,
    destination,
    row_counts,
    section_gain,
    adapter_down,
    adapter_up,
    student_in,
    student_gain,
    student_weight,
    projector,
):
    weight_grad, row_loss = run_step(
        teacher_hidden,
        teacher_id,
        destination,
        row_counts,
        section_gain,
        adapter_down[0].T,
        adapter_up[0],
        student_in,
        student_gain,
        student_weight,
        projector,
    )
    weight_grad, row_loss = finish(weight_grad, row_loss)
    share, cols = weight_grad.shape
    return (weight_grad.reshape(1, share, cols), row_loss.reshape(student_in.shape[0]))


def solution(mesh):
    placed = (
        P("dp", "mp"),
        P("dp"),
        P("dp"),
        P("dp", None),
        P("segment", "mp"),
        P("segment", "mp", None),
        P("segment", None, "mp"),
        P("dp", "mp"),
        P("mp"),
        P("mp", "segment"),
        P("mp", "segment"),
    )
    return jax.shard_map(
        local,
        mesh=mesh,
        in_specs=placed,
        out_specs=(P("mp", "dp", "segment"), P("dp")),
        check_vma=False,
    )
```

```python
import functools

import jax
import jax.numpy as jnp
import numpy as np
from jax import lax
from jax.experimental import pallas as pl
from jax.experimental.pallas import tpu as pltpu
from jax.sharding import PartitionSpec as P

D = 8192
S = 5120
RANK = 64
TOK_DEV = 256
TEACH = 3
LANES = 128
bf16 = jnp.bfloat16
f32 = jnp.float32


def dot(a, b):
    return jnp.dot(a, b, preferred_element_type=f32)


def remote(src, dst, send, recv, **where):
    return pltpu.make_async_remote_copy(
        src_ref=src,
        dst_ref=dst,
        send_sem=send,
        recv_sem=recv,
        device_id=where,
        device_id_type=pl.DeviceIdType.MESH,
    )


def iota(shape, dim):
    return lax.broadcasted_iota(jnp.int32, shape, dim)


def ones_where(mask):
    return jnp.where(mask, 1.0, 0.0).astype(bf16)


def dot_nt(a, b):
    return lax.dot_general(a, b, (((1,), (1,)), ((), ())), preferred_element_type=f32)


def turned(row):
    return jnp.broadcast_to(row, (LANES, row.shape[1])).T


def fold(wide, keep):
    kept = jnp.where(keep, wide, 0.0)
    both = kept[:, :LANES] + kept[:, LANES:]
    return both + pltpu.roll(both, RANK, 1)


def step_kernel(
    n_seg, side, cap,
    h_hbm, down_hbm, up_hbm, x_hbm, w_hbm, p_hbm, xmap_hbm,
    ids, dest, counts, gain, sgain, kcol,
    out, loss_out,
    h, down, up, x, w, p, xmap,
    usend, ugot, ucat, wide_a, wide_b, abx, abgot, sel, pay, aslots, agot, aall,
    mgx, mggot, mgs, upx, upgot, blocks, tables,
    hpx, hpsend, hpgot, hslots, hgot,
    sg, sox, sosend, sogot, sxx, sxgot, ctil, base,
    sgt, nb, held, finsend, fingot, losspart, lossgot, losses,
    lsem, s_m, r_m, s_x, r_x, s_d, r_d, s_n, r_n, s_r, r_r,
):
    me_s = lax.axis_index("segment")
    me_m = lax.axis_index("mp")
    me_d = lax.axis_index("dp")
    other = 1 - me_m
    n_dp = side * side
    tok, half = h.shape
    slots = x.shape[0]
    cols = p.shape[1]
    out_half = cols // 2
    rows_u = mgx.shape[0]
    per = rows_u // n_seg
    part = half // n_seg
    tile = 2 * LANES
    tiles = cols // tile
    pair = n_seg // 2

    def load(n, src, dst):
        copy = pltpu.make_async_copy(src, dst, lsem.at[n])
        copy.start()
        return copy

    def p_copy(n):
        span = pl.ds(pl.multiple_of(n * tile, tile), tile)
        return pltpu.make_async_copy(p_hbm.at[:, span], p.at[:, span], lsem.at[5 + n])

    def w_copy(n):
        span = pl.ds(pl.multiple_of(n * tile, tile), tile)
        return pltpu.make_async_copy(w_hbm.at[:, span], w.at[:, span], lsem.at[5 + tiles + n])

    up_in = load(0, up_hbm, up)
    x_in = load(3, x_hbm, x)
    h_in = load(1, h_hbm, h)
    for n in range(tiles):
        p_copy(n).start()
    down_in = load(2, down_hbm, down)
    for n in range(tiles):
        w_copy(n).start()
    xmap_in = load(4, xmap_hbm, xmap)

    z = me_d // side
    y = me_d % side

    def place(first, second):
        a = ((z * other + y * me_m) + second) % side
        b = ((y * other + z * me_m) + first) % side
        return (a * other + b * me_m) * side + b * other + a * me_m

    barrier = pltpu.get_barrier_semaphore()
    mesh_id = pl.DeviceIdType.MESH
    pl.semaphore_signal(barrier, inc=1, device_id={"mp": other}, device_id_type=mesh_id)
    for n in range(1, n_seg):
        pl.semaphore_signal(barrier, inc=1, device_id={"segment": (me_s + n) % n_seg}, device_id_type=mesh_id)

    @pl.loop(1, n_dp)
    def _(n):
        pl.semaphore_signal(barrier, inc=1, device_id={"dp": (me_d + n) % n_dp}, device_id_type=mesh_id)

    for n in range(1, side):
        pl.semaphore_signal(barrier, inc=1, device_id={"dp": place(n, 0), "mp": other}, device_id_type=mesh_id)

    def to_peer(n, src, dst):
        return remote(src, dst, s_m.at[n], r_m.at[n], mp=other)

    def to_seg(kind, n, src, dst):
        number = kind * (n_seg - 1) + n - 1
        return remote(src, dst, s_x.at[number], r_x.at[number], segment=(me_s + n) % n_seg)

    def to_dp(kind, n, src, dst):
        number = kind * (n_dp - 1) + n - 1
        return remote(src, dst, s_d.at[number], r_d.at[number], dp=(me_d + n) % n_dp)

    def gather_first(n):
        return remote(blocks.at[me_d], blocks.at[me_d], s_d.at[n + 44], r_d.at[n + 44], dp=place(n, 0))

    def gather_second(k, n):
        source = place(side - k, 0)
        number = 48 + k * (side - 1) + n - 1
        return remote(blocks.at[source], blocks.at[source], s_d.at[number], r_d.at[number], dp=place(0, n))

    packed = n_seg * per
    row = iota((packed, up.shape[0]), 0)
    col = iota((packed, up.shape[0]), 1)
    quad = row >> 2
    block = (quad >= 3).astype(jnp.int32) + (quad >= 6).astype(jnp.int32) + (quad >= 9).astype(jnp.int32)
    teacher = quad - 3 * block
    hit = ((col >> 6) == teacher) & (((col & 63) >> 2) == me_d) & ((col & 3) == (row & 3))
    up_in.wait()
    mine = jnp.zeros((packed, part), f32)
    for g in range(n_seg):
        mine = mine + dot(ones_where(hit & (block == g)), up[:, g * part : (g + 1) * part])
    usend[...] = mine.astype(bf16)
    ugot[me_s] = usend[...]
    wide_a[...] = jnp.zeros(wide_a.shape, f32)
    wide_b[...] = jnp.zeros(wide_b.shape, f32)
    abx[...] = jnp.zeros(abx.shape, f32)

    x_in.wait()
    sxx[...] = jnp.zeros(sxx.shape, f32)

    def scale(n):
        span = pl.ds(pl.multiple_of(n * LANES, LANES), LANES)
        wide = x[:, span].astype(f32)
        sxx[...] += wide * wide
        scaled = (wide * sgain[pl.ds(n, 1), :]).astype(bf16)
        sg[:, span] = scaled
        sgt[span, :] = scaled.T

    groups = x.shape[1] // LANES
    pl.loop(0, groups // 2)(scale)
    pl.semaphore_wait(barrier, 1 + (n_seg - 1) + (n_dp - 1) + (side - 1))
    u_sent = [to_seg(0, n, usend, ugot.at[me_s]) for n in range(1, n_seg)]
    for copy in u_sent:
        copy.start()
    pl.loop(groups // 2, groups)(scale)

    share = out.shape[0]

    def rows_of(owner):
        return sgt.at[pl.ds(pl.multiple_of(owner * share, share), share)]

    def owner_of(f, other_ring):
        return (1 - f) * (other_ring * side + y) + f * (z * side + other_ring)

    def block_copy(f, n):
        if f == 0:
            where = z * side + (y + n) % side
            owner = me_s * side + (y + n) % side
        else:
            where = ((z + n) % side) * side + y
            owner = ((z + n) % side) * side + me_s
        number = f * (side - 1) + n - 1
        return remote(
            rows_of(owner), nb.at[me_s, side - n, me_m], s_n.at[number], r_n.at[(n - 1) * 2 + me_m], dp=where, mp=f
        )

    def block_landed(m, n):
        where = nb.at[me_s, side - n, m]
        return remote(where, where, s_n.at[0], r_n.at[(n - 1) * 2 + m], mp=other)

    def chip_copy(n):
        return remote(rows_of(owner_of(other, n)), nb.at[n, 0, me_m], s_n.at[6 + n], r_n.at[6 + n], mp=other)

    def plane_copy(way, m, k):
        number = 10 + (way * 2 + m) * (side - 1) + k - 1
        block = nb.at[me_s, k, m]
        return remote(block, block, s_n.at[number], r_n.at[number], segment=(me_s + 1 + way * (n_seg - 2)) % n_seg)

    def plane_forward(way, k):
        number = 10 + (4 + way) * (side - 1) + k - 1
        block = nb.at[(me_s + n_seg - 1 + 2 * way) % n_seg, k, way]
        return remote(block, block, s_n.at[number], r_n.at[number], segment=(me_s + 1 + way * (n_seg - 2)) % n_seg)

    for n in (1, side - 1, 2):
        for f in (0, 1):
            block_copy(f, n).start()
    for n in range(side):
        chip_copy(n).start()
    sx_sent = to_peer(4, sxx, sxgot)
    sx_sent.start()
    for n in range(side):
        nb[n, 0, me_m] = rows_of(owner_of(me_m, n))[...]

    away = pl.ds(pl.multiple_of(other * out_half, LANES), out_half)
    kept = pl.ds(pl.multiple_of(me_m * out_half, LANES), out_half)
    h_in.wait()
    down_in.wait()
    rank_all = down.shape[0]

    @pl.loop(0, n_seg)
    def _(g):
        span = pl.ds(pl.multiple_of(g * part, part), part)
        here = h[:, span]
        wide = here.astype(f32)
        scaled = (wide * gain[:, span].astype(f32)).astype(bf16)
        wide_a[:, :rank_all] += dot_nt(scaled, down[:, span])
        wide_b[:, :rank_all] += dot_nt(here, up[:, span])
        abx[:, LANES:] += jnp.broadcast_to(jnp.sum(wide * wide, axis=1, keepdims=True), (tok, LANES))

    id_col = turned(ids[...].astype(f32))
    lane2 = iota((tok, 2 * LANES), 1)
    own = (lane2 >> 6).astype(f32) == jnp.concatenate([id_col, id_col], axis=1)
    lane = iota((tok, LANES), 1)
    abx[:, :LANES] = jnp.where(lane < RANK, fold(wide_a[...], own), fold(wide_b[...], own))
    ab_sent = to_peer(0, abx, abgot)
    ab_sent.start()


    @pl.loop(0, tiles)
    def _(n):
        span = pl.ds(pl.multiple_of(n * tile, tile), tile)
        p_copy(n).wait()
        hpx[:, span] = dot(h[...], p[:, span])

    hpsend[...] = hpx[:, away].astype(bf16)
    hp_sent = to_peer(3, hpsend, hpgot)
    hp_sent.start()
    for n in (1, side - 1):
        for m in (0, 1):
            block_landed(m, n).wait_recv()
    for n in (1, side - 1):
        for way in (0, 1):
            plane_copy(way, way, n).start()

    dest_f = dest[...].astype(f32)
    onehot = jnp.where(iota((n_dp, tok), 0).astype(f32) == dest_f, 1.0, 0.0)
    before = ones_where(iota((tok, tok), 0) < iota((tok, tok), 1))
    earlier = dot(onehot.astype(bf16), before)
    position = dest_f * cap + jnp.sum(earlier * onehot, axis=0, keepdims=True)
    sel[...] = ones_where(iota((slots, tok), 0).astype(f32) == position)
    ab_sent.wait_recv()
    total = abx[...] + abgot[...]
    sq = total[:, LANES:]
    sq_hi = sq.astype(bf16).astype(f32)
    extra = jnp.where(lane == 0, id_col, jnp.where(lane == 1, sq_hi, jnp.where(lane == 2, sq - sq_hi, 0.0)))
    pay[:, :LANES] = total[:, :LANES].astype(bf16)
    pay[:, LANES:] = extra.astype(bf16)
    lanes_here = pl.ds(pl.multiple_of(me_m * LANES, LANES), LANES)
    aslots[...] = dot(sel[...], pay[:, lanes_here]).astype(bf16).reshape(aslots.shape)
    agot[me_m, me_d] = aslots[me_d]

    def a_copy(n):
        return to_dp(0, n, aslots.at[(me_d + n) % n_dp], agot.at[me_m, me_d])

    @pl.loop(1, n_dp)
    def _(n):
        a_copy(n).start()

    hp_sent.wait_recv()
    hp = (hpx[:, kept] + hpgot[...].astype(f32)).astype(bf16)
    hslots[...] = dot(sel[...], hp).astype(bf16).reshape(hslots.shape)
    hgot[me_d] = hslots[me_d]

    def h_copy(n):
        return to_dp(1, n, hslots.at[(me_d + n) % n_dp], hgot.at[me_d])

    @pl.loop(1, n_dp)
    def _(n):
        h_copy(n).start()

    for copy in u_sent:
        copy.wait_recv()
    row = iota((packed, n_seg * packed), 0)
    col = iota((packed, n_seg * packed), 1)
    quad = row >> 2
    block = (quad >= 3).astype(jnp.int32) + (quad >= 6).astype(jnp.int32) + (quad >= 9).astype(jnp.int32)
    got_u = ugot[...].reshape(n_seg * packed, part)
    for g in range(n_seg):
        take = ones_where(col == row + (packed - per) * block + per * g)
        ucat[:, g * part : (g + 1) * part] = dot(take, got_u).astype(bf16)
    u = ucat[...]
    u_scaled = (u.astype(f32) * gain[...].astype(f32)).astype(bf16)
    wide_a[:rows_u, :rank_all] = dot_nt(u_scaled, down[...])
    wide_b[:rows_u, :rank_all] = dot_nt(u, up[...])
    row = iota((rows_u, 2 * LANES), 0)
    quad = row >> 2
    block = (quad >= 3).astype(jnp.int32) + (quad >= 6).astype(jnp.int32) + (quad >= 9).astype(jnp.int32)
    same = (quad - 3 * block) == (iota((rows_u, 2 * LANES), 1) >> 6)
    lane_u = iota((rows_u, LANES), 1)
    mgx[...] = jnp.where(lane_u < RANK, fold(wide_a[:rows_u, :], same), fold(wide_b[:rows_u, :], same))
    mg_sent = to_peer(1, mgx, mggot)
    mg_sent.start()

    def up_tile(n):
        span = pl.ds(pl.multiple_of(n * tile, tile), tile)
        upx[:, span] = dot(ucat[...], p[:, span])

    pl.loop(0, 2)(up_tile)
    mg_sent.wait_recv()
    mgs[me_s] = (mgx[...] + mggot[...]).astype(bf16)
    mg_x = [to_seg(1, n, mgs.at[me_s], mgs.at[me_s]) for n in range(1, n_seg)]
    for copy in mg_x:
        copy.start()

    pl.loop(2, tiles)(up_tile)
    up_sent = to_peer(2, upx.at[:, away], upgot)
    up_sent.start()

    def student(n):
        span = pl.ds(pl.multiple_of(n * tile, tile), tile)
        w_copy(n).wait()
        sox[:, span] = dot(sg[...], w[:, span])

    pl.loop(0, 1)(student)

    up_sent.wait_recv()
    blocks[me_d] = (upx[:, kept] + upgot[...]).astype(bf16)
    firsts = [gather_first(n) for n in range(1, side)]
    for copy in firsts:
        copy.start()
    seconds = [gather_second(0, n) for n in range(1, side)]
    for copy in seconds:
        copy.start()

    for copy in mg_x:
        copy.wait_recv()
    for n in range(pair):
        tables[me_m, me_d, :, n * LANES : (n + 1) * LANES] = mgs[me_m * pair + n]

    def m_copy(n):
        return to_dp(2, n, tables.at[me_m, me_d], tables.at[me_m, me_d])

    @pl.loop(1, n_dp)
    def _(n):
        m_copy(n).start()

    @pl.loop(1, n_dp)
    def _(n):
        a_copy(n).wait_recv()

    a_x = [to_seg(2, n, aall.at[me_s], aall.at[me_s]) for n in range(1, n_seg)]
    extra_swap = to_peer(6, agot.at[1], agot.at[1])

    @pl.when(me_m == 0)
    def _():
        aall[me_s] = agot[0].reshape(slots, LANES)
        for copy in a_x:
            copy.start()

    @pl.when(me_m == 1)
    def _():
        extra_swap.start()

    for m in (0, 1):
        block_landed(m, 2).wait_recv()
    for way in (0, 1):
        plane_copy(way, way, 2).start()
    for n in (1, side - 1, 2):
        for way in (0, 1):
            plane_copy(way, 1 - way, n).start()

    pl.loop(1, 3)(student)

    def gather_on(k):
        firsts[k - 1].wait_recv()
        copies = [gather_second(k, n) for n in range(1, side)]
        for copy in copies:
            copy.start()
        return copies

    seconds += gather_on(1) + gather_on(side - 1)
    pl.loop(3, 4)(student)
    seconds += gather_on(2)
    pl.loop(4, tiles)(student)
    sosend[...] = sox[:, away].astype(bf16)
    so_sent = to_peer(5, sosend, sogot)
    so_sent.start()
    a_swap = to_peer(7, aall, aall)

    @pl.when(me_m == 0)
    def _():
        for copy in a_x:
            copy.wait_recv()
        a_swap.start()

    for n in (1, side - 1, 2):
        for way in (0, 1):
            plane_copy(way, way, n).wait_recv()
            plane_forward(way, n).start()

    @pl.loop(1, n_dp)
    def _(n):
        m_copy(n).wait_recv()

    table_swap = to_peer(8, tables.at[me_m], tables.at[me_m])
    table_swap.start()

    @pl.when(me_m == 0)
    def _():
        extra_swap.wait_recv()

    @pl.when(me_m == 1)
    def _():
        a_swap.wait_recv()

    xmap_in.wait()
    extra = agot[1].reshape(slots, LANES).astype(f32)
    id_slot = extra[:, 0:1]
    norm = extra[:, 1:2] + extra[:, 2:3]
    keep = kcol[...] == id_slot
    lane = iota((slots, LANES), 1)
    known = rows_u * n_dp
    both = jnp.zeros((slots, LANES), f32)
    table_swap.wait_recv()
    for s in range(n_seg):
        ab = aall[s].astype(f32)
        lat = (ab + both) * lax.rsqrt(jnp.maximum(norm, 0.0) * (1.0 / D) + 1e-06)
        lat = lat.astype(bf16)
        lat_low = jnp.where(lane < RANK, lat.astype(f32), 0.0)
        wide_c = jnp.where(keep, dot(lat_low.astype(bf16), xmap[s]), 0.0).astype(bf16)
        if s == 0:
            ctil[...] = wide_c
        else:
            ctil[...] += wide_c
        if s + 1 < n_seg:
            low, high = (s % pair) * LANES, ((s + 1) % pair) * LANES
            here = tables[s // pair, :, :, low : low + LANES].reshape(known, LANES)
            after = tables[(s + 1) // pair, :, :, high : high + LANES].reshape(known, LANES)
            self_part = dot(ctil[...], here)
            lat_high = pltpu.roll(lat_low, RANK, 1)
            norm = norm + jnp.sum(lat_high * (2.0 * ab + both + self_part), axis=1, keepdims=True)
            both = dot(ctil[...], after)

    @pl.loop(1, n_dp)
    def _(n):
        h_copy(n).wait_recv()

    sx_sent.wait()
    so_sent.wait_recv()
    slot = iota((slots, n_dp), 0)
    source = iota((slots, n_dp), 1)
    room = slot - source * cap
    valid = jnp.sum(
        jnp.where((room >= 0) & (room < cap) & (room < counts[...]), 1.0, 0.0), axis=1, keepdims=True
    )
    square = jnp.sum(sxx[...] + sxgot[...], axis=1, keepdims=True)
    recip = lax.rsqrt(square * (1.0 / S) + 1e-06)
    student_out = (sox[:, kept] + sogot[...].astype(f32)) * recip
    base[...] = jnp.where(valid > 0.0, student_out - hgot[...].reshape(slots, out_half).astype(f32), 0.0)
    sxx[...] = jnp.broadcast_to(recip * (1.0 / TOK_DEV), sxx.shape)
    for copy in seconds:
        copy.wait_recv()
    table = blocks[...].reshape(known, out_half)
    edge = slots // 2

    def gathered(ahead, low=0, count=slots):
        return p.at[pl.ds(ahead * slots + low, count), :out_half]

    def diff_copy(way, part):
        ahead = (side - 1, 1)[way]
        number = way * 2 + part
        return remote(
            gathered(0, part * edge, edge), gathered(ahead, part * edge, edge),
            s_r.at[number], r_r.at[number], dp=place(1 + way * (side - 2), 0),
        )

    def diff_forward(way):
        ahead = (side - 1, 1)[way]
        return remote(
            gathered(ahead, way * edge, edge), gathered(2, way * edge, edge),
            s_r.at[4 + way], r_r.at[4 + way], dp=place(1 + way * (side - 2), 0),
        )

    def difference(part):
        rows = slice(part * edge, (part + 1) * edge)
        diff = base[rows, :] - dot(ctil[rows, :], table)
        gathered(0, part * edge, edge)[...] = (diff * sxx[rows, 0:1]).astype(bf16)
        loss = jnp.sum(diff * diff, axis=1, keepdims=True)
        losspart[:, rows] = jnp.broadcast_to(loss, (edge, LANES)).T[0:1, :]

    difference(0)
    diff_copy(0, 0).start()
    difference(1)
    diff_copy(1, 1).start()
    for way in (0, 1):
        diff_copy(way, 1 - way).start()
    loss_swap = to_peer(9, losspart, lossgot)
    loss_swap.start()
    def product(owner, ahead):
        return dot(nb[owner, ahead].reshape(2 * share, slots), gathered(ahead)[...])

    for n in range(side):
        chip_copy(n).wait_recv()

    @pl.loop(0, side)
    def _(n):
        held[n] = product(n, 0)

    for way in (0, 1):
        diff_copy(way, way).wait_recv()
        diff_forward(way).start()
    loss_swap.wait_recv()
    losses[me_s] = losspart[...] + lossgot[...]
    tells = [to_seg(3, n, losses.at[me_s], losses.at[me_s]) for n in range(1, n_seg)]
    for copy in tells:
        copy.start()
    for way in (0, 1):
        for n in range(1, side):
            plane_copy(way, 1 - way, n).wait_recv()
            plane_forward(way, n).wait_recv()
    for way in (0, 1):
        diff_copy(way, 1 - way).wait_recv()

    @pl.loop(0, side)
    def _(n):
        held[n] += product(n, 1) + product(n, 3)

    for copy in tells:
        copy.wait_recv()
    total = losses[0]
    for n in range(1, n_seg):
        total = total + losses[n]
    loss_out[...] = total * (1.0 / S)

    ring_at = z * other + y * me_m
    below = side * slots

    def sent(slot, m):
        return p.at[pl.ds(below + (slot * 2 + m) * share, share), :out_half]

    def landed(number):
        return p.at[pl.ds(pl.multiple_of(below + number * share, 16), share), out_half:]

    def far_copy(way):
        return remote(
            sent(0, way), landed(way), s_r.at[6 + way], r_r.at[6 + way], dp=place(0, 1 + way * (side - 2))
        )

    def near_copy(way, last):
        m = way if last else 1 - way
        number = 2 * me_m + last
        return remote(
            sent(1 + way, m), landed(2 + number), s_r.at[8 + 2 * way + last], r_r.at[8 + number],
            dp=place(0, 1 + way * (side - 2)), mp=m,
        )

    def near_landed(f, last):
        where = landed(2 + 2 * f + last)
        return remote(where, where, s_r.at[0], r_r.at[8 + 2 * f + last], mp=other)

    for way in (0, 1):
        diff_forward(way).wait_recv()
    far = (ring_at + 2) % side
    nears = [(ring_at + 1) % side, (ring_at + side - 1) % side]

    def half_rows(m):
        return pl.ds(m * share, share)

    block = held[far] + product(far, 2)
    for way in (0, 1):
        sent(0, way)[...] = block[way * share : (way + 1) * share].astype(bf16)
        far_copy(way).start()
    for way in (0, 1):
        block = held[nears[way]] + product(nears[way], 2)
        sent(1 + way, 1 - way)[...] = block[(1 - way) * share : (2 - way) * share].astype(bf16)
        near_copy(way, 0).start()
        held[nears[way], half_rows(way)] = block[way * share : (way + 1) * share]
    held[ring_at] += product(ring_at, 2)
    finsend[...] = held[ring_at, pl.ds(pl.multiple_of(other * share, share), share)]
    own_swap = to_peer(10, finsend, fingot)
    own_swap.start()
    for way in (0, 1):
        far_copy(way).wait_recv()
        sent(1 + way, way)[...] = (held[nears[way], half_rows(way)] + landed(way)[...].astype(f32)).astype(bf16)
        near_copy(way, 1).start()
    own_swap.wait_recv()
    mine = held[ring_at, pl.ds(pl.multiple_of(me_m * share, share), share)]
    for last in (0, 1):
        near_landed(me_m, last).wait_recv()
        near_landed(other, last).wait_recv()
    out[:, kept] = mine + landed(2 + 2 * me_m)[...].astype(f32) + landed(3 + 2 * me_m)[...].astype(f32)
    out[:, away] = fingot[...] + landed(2 + 2 * other)[...].astype(f32) + landed(3 + 2 * other)[...].astype(f32)

    for n in range(1, side):
        for f in (0, 1):
            block_copy(f, n).wait_send()
    for n in range(side):
        chip_copy(n).wait_send()
    for way in (0, 1):
        for n in range(1, side):
            for m in (0, 1):
                plane_copy(way, m, n).wait_send()
            plane_forward(way, n).wait_send()
        for m in (0, 1):
            diff_copy(way, m).wait_send()
        diff_forward(way).wait_send()
        far_copy(way).wait_send()
        for last in (0, 1):
            near_copy(way, last).wait_send()
    for copy in u_sent + mg_x + firsts + seconds + [ab_sent, mg_sent, up_sent, hp_sent, so_sent, table_swap, loss_swap, own_swap] + tells:
        copy.wait_send()

    @pl.when(me_m == 0)
    def _():
        for copy in a_x + [a_swap]:
            copy.wait_send()

    @pl.when(me_m == 1)
    def _():
        extra_swap.wait_send()

    @pl.loop(1, n_dp)
    def _(n):
        a_copy(n).wait_send()
        m_copy(n).wait_send()
        h_copy(n).wait_send()


def run_step(h, ids, dest, counts, gain, down, up, x, sgain, w, p):
    side = 4
    n_seg = lax.axis_size("segment")
    n_dp = lax.axis_size("dp")
    tok, half = h.shape
    slots, width = x.shape
    cols = p.shape[1]
    out_half = cols // 2
    cap = slots // n_dp
    q = RANK // n_dp
    per = TEACH * q
    rows_u = n_seg * per
    known = rows_u * n_dp
    share = width // n_dp
    c = np.arange(known)
    c_i, c_t, c_k, c_q = c // rows_u, c % rows_u // per, c % per // q, c % q
    spot = np.arange(LANES)[None, :, None]
    xmap = (np.arange(n_seg)[:, None, None] == c_t) & (spot == c_i * q + c_q)
    xmap = jnp.asarray(xmap.astype(np.float32), dtype=bf16)
    kcol = jnp.asarray(c_k[None, :].astype(np.float32))
    vmem = pl.BlockSpec(memory_space=pltpu.VMEM)
    hbm = pl.BlockSpec(memory_space=pl.ANY)
    flops = 2 * (tok * half * cols + 2 * slots * width * cols)
    scratch = [
        (h.shape, bf16), (down.shape, bf16), (up.shape, bf16), (x.shape, bf16), (w.shape, bf16), (p.shape, bf16),
        (xmap.shape, bf16),
        ((rows_u, half // n_seg), bf16), ((n_seg, rows_u, half // n_seg), bf16), ((rows_u, half), bf16),
        ((tok, 2 * LANES), f32), ((tok, 2 * LANES), f32), ((tok, 2 * LANES), f32), ((tok, 2 * LANES), f32),
        ((slots, tok), bf16), ((tok, 2 * LANES), bf16),
        ((n_dp, cap, LANES), bf16), ((2, n_dp, cap, LANES), bf16), ((n_seg, slots, LANES), bf16),
        ((rows_u, LANES), f32), ((rows_u, LANES), f32), ((n_seg, rows_u, LANES), bf16),
        ((rows_u, cols), f32), ((rows_u, out_half), f32),
        ((n_dp, rows_u, out_half), bf16), ((2, n_dp, rows_u, n_seg // 2 * LANES), bf16),
        ((tok, cols), f32), ((tok, out_half), bf16), ((tok, out_half), bf16),
        ((n_dp, cap, out_half), bf16), ((n_dp, cap, out_half), bf16),
        (x.shape, bf16), ((slots, cols), f32), ((slots, out_half), bf16), ((slots, out_half), bf16),
        ((slots, LANES), f32), ((slots, LANES), f32), ((slots, known), bf16), ((slots, out_half), f32),
        ((width, slots), bf16), ((n_seg, side, 2, share, slots), bf16), ((side, 2 * share, out_half), f32),
        ((share, out_half), f32), ((share, out_half), f32),
        ((1, slots), f32), ((1, slots), f32), ((n_seg, 1, slots), f32),
    ]
    sems = [5 + cols // LANES, 11, 11, 4 * (n_seg - 1), 4 * (n_seg - 1), 4 * (n_dp - 1), 4 * (n_dp - 1), 28, 28, 12, 12]
    return pl.pallas_call(
        functools.partial(step_kernel, n_seg, side, cap),
        out_shape=(
            jax.ShapeDtypeStruct((share, cols), f32),
            jax.ShapeDtypeStruct((1, slots), f32),
        ),
        in_specs=[hbm] * 7 + [vmem] * 6,
        out_specs=(vmem, vmem),
        scratch_shapes=[pltpu.VMEM(*s) for s in scratch] + [pltpu.SemaphoreType.DMA((n,)) for n in sems],
        compiler_params=pltpu.CompilerParams(
            collective_id=0, has_side_effects=True, vmem_limit_bytes=60 * 2**20
        ),
        cost_estimate=pl.CostEstimate(flops=flops, bytes_accessed=25 * 2**20, transcendentals=0),
    )(
        h, down, up, x, w, p, xmap,
        ids.reshape(1, tok), dest.reshape(1, tok), counts, gain, sgain.reshape(width // LANES, LANES), kcol,
    )


def finish_kernel(grad, loss, grad_out, loss_out):
    grad_out[...] = grad[...]
    loss_out[...] = loss[...]


def finish(grad, loss):
    vmem = pl.BlockSpec(memory_space=pltpu.VMEM)
    return pl.pallas_call(
        finish_kernel,
        out_shape=(jax.ShapeDtypeStruct(grad.shape, f32), jax.ShapeDtypeStruct(loss.shape, f32)),
        in_specs=[vmem, vmem],
        out_specs=(vmem, vmem),
    )(grad, loss)


def local(
    teacher_hidden,
    teacher_id,
    destination,
    row_counts,
    section_gain,
    adapter_down,
    adapter_up,
    student_in,
    student_gain,
    student_weight,
    projector,
):
    weight_grad, row_loss = run_step(
        teacher_hidden,
        teacher_id,
        destination,
        row_counts,
        section_gain,
        adapter_down[0].T,
        adapter_up[0],
        student_in,
        student_gain,
        student_weight,
        projector,
    )
    weight_grad, row_loss = finish(weight_grad, row_loss)
    share, cols = weight_grad.shape
    return (weight_grad.reshape(1, share, cols), row_loss.reshape(student_in.shape[0]))


def solution(mesh):
    placed = (
        P("dp", "mp"),
        P("dp"),
        P("dp"),
        P("dp", None),
        P("segment", "mp"),
        P("segment", "mp", None),
        P("segment", None, "mp"),
        P("dp", "mp"),
        P("mp"),
        P("mp", "segment"),
        P("mp", "segment"),
    )
    return jax.shard_map(
        local,
        mesh=mesh,
        in_specs=placed,
        out_specs=(P("mp", "dp", "segment"), P("dp")),
        check_vma=False,
    )
```

```python
import functools

import jax
import jax.numpy as jnp
import numpy as np
from jax import lax
from jax.experimental import pallas as pl
from jax.experimental.pallas import tpu as pltpu
from jax.sharding import PartitionSpec as P

D = 8192
S = 5120
RANK = 64
TOK_DEV = 256
TEACH = 3
LANES = 128
bf16 = jnp.bfloat16
f32 = jnp.float32


def dot(a, b):
    return jnp.dot(a, b, preferred_element_type=f32)


def remote(src, dst, send, recv, **where):
    return pltpu.make_async_remote_copy(
        src_ref=src,
        dst_ref=dst,
        send_sem=send,
        recv_sem=recv,
        device_id=where,
        device_id_type=pl.DeviceIdType.MESH,
    )


def iota(shape, dim):
    return lax.broadcasted_iota(jnp.int32, shape, dim)


def ones_where(mask):
    return jnp.where(mask, 1.0, 0.0).astype(bf16)


def dot_nt(a, b):
    return lax.dot_general(a, b, (((1,), (1,)), ((), ())), preferred_element_type=f32)


def turned(row):
    return jnp.broadcast_to(row, (LANES, row.shape[1])).T


def fold(wide, keep):
    kept = jnp.where(keep, wide, 0.0)
    both = kept[:, :LANES] + kept[:, LANES:]
    return both + pltpu.roll(both, RANK, 1)


def step_kernel(
    n_seg, side, cap,
    h_hbm, down_hbm, up_hbm, x_hbm, w_hbm, p_hbm, xmap_hbm,
    ids, dest, counts, gain, sgain, kcol,
    out, loss_out,
    h, down, up, x, w, p, xmap,
    usend, ugot, ucat, wide_a, wide_b, abx, abgot, sel, pay, aslots, agot, aall,
    mgx, mggot, mgs, upx, upgot, blocks, tables,
    hpx, hpsend, hpgot, hslots, hgot,
    sg, sox, sosend, sogot, sxx, sxgot, ctil, base,
    sgt, nb, held, finsend, fingot, losspart, lossgot, losses,
    lsem, s_m, r_m, s_x, r_x, s_d, r_d, s_n, r_n, s_r, r_r,
):
    me_s = lax.axis_index("segment")
    me_m = lax.axis_index("mp")
    me_d = lax.axis_index("dp")
    other = 1 - me_m
    n_dp = side * side
    tok, half = h.shape
    slots = x.shape[0]
    cols = p.shape[1]
    out_half = cols // 2
    rows_u = mgx.shape[0]
    per = rows_u // n_seg
    part = half // n_seg
    tile = 2 * LANES
    tiles = cols // tile
    pair = n_seg // 2

    def load(n, src, dst):
        copy = pltpu.make_async_copy(src, dst, lsem.at[n])
        copy.start()
        return copy

    def p_copy(n):
        span = pl.ds(pl.multiple_of(n * tile, tile), tile)
        return pltpu.make_async_copy(p_hbm.at[:, span], p.at[:, span], lsem.at[5 + n])

    def w_copy(n):
        span = pl.ds(pl.multiple_of(n * tile, tile), tile)
        return pltpu.make_async_copy(w_hbm.at[:, span], w.at[:, span], lsem.at[5 + tiles + n])

    up_in = load(0, up_hbm, up)
    x_in = load(3, x_hbm, x)
    h_in = load(1, h_hbm, h)
    down_in = load(2, down_hbm, down)
    for n in range(tiles):
        p_copy(n).start()
    for n in range(tiles):
        w_copy(n).start()
    xmap_in = load(4, xmap_hbm, xmap)

    z = me_d // side
    y = me_d % side

    def place(first, second):
        a = ((z * other + y * me_m) + second) % side
        b = ((y * other + z * me_m) + first) % side
        return (a * other + b * me_m) * side + b * other + a * me_m

    barrier = pltpu.get_barrier_semaphore()
    mesh_id = pl.DeviceIdType.MESH
    pl.semaphore_signal(barrier, inc=1, device_id={"mp": other}, device_id_type=mesh_id)
    for n in range(1, n_seg):
        pl.semaphore_signal(barrier, inc=1, device_id={"segment": (me_s + n) % n_seg}, device_id_type=mesh_id)

    @pl.loop(1, n_dp)
    def _(n):
        pl.semaphore_signal(barrier, inc=1, device_id={"dp": (me_d + n) % n_dp}, device_id_type=mesh_id)

    for n in range(1, side):
        pl.semaphore_signal(barrier, inc=1, device_id={"dp": place(n, 0), "mp": other}, device_id_type=mesh_id)

    def to_peer(n, src, dst):
        return remote(src, dst, s_m.at[n], r_m.at[n], mp=other)

    def to_seg(kind, n, src, dst):
        number = kind * (n_seg - 1) + n - 1
        return remote(src, dst, s_x.at[number], r_x.at[number], segment=(me_s + n) % n_seg)

    def to_dp(kind, n, src, dst):
        number = kind * (n_dp - 1) + n - 1
        return remote(src, dst, s_d.at[number], r_d.at[number], dp=(me_d + n) % n_dp)

    def gather_first(n):
        return remote(blocks.at[me_d], blocks.at[me_d], s_d.at[n + 44], r_d.at[n + 44], dp=place(n, 0))

    def gather_second(k, n):
        source = place(side - k, 0)
        number = 48 + k * (side - 1) + n - 1
        return remote(blocks.at[source], blocks.at[source], s_d.at[number], r_d.at[number], dp=place(0, n))

    packed = n_seg * per
    row = iota((packed, up.shape[0]), 0)
    col = iota((packed, up.shape[0]), 1)
    quad = row >> 2
    block = (quad >= 3).astype(jnp.int32) + (quad >= 6).astype(jnp.int32) + (quad >= 9).astype(jnp.int32)
    teacher = quad - 3 * block
    hit = ((col >> 6) == teacher) & (((col & 63) >> 2) == me_d) & ((col & 3) == (row & 3))
    up_in.wait()
    mine = jnp.zeros((packed, part), f32)
    for g in range(n_seg):
        mine = mine + dot(ones_where(hit & (block == g)), up[:, g * part : (g + 1) * part])
    usend[...] = mine.astype(bf16)
    ugot[me_s] = usend[...]
    wide_a[...] = jnp.zeros(wide_a.shape, f32)
    wide_b[...] = jnp.zeros(wide_b.shape, f32)
    abx[...] = jnp.zeros(abx.shape, f32)

    x_in.wait()
    sxx[...] = jnp.zeros(sxx.shape, f32)

    def scale(n):
        span = pl.ds(pl.multiple_of(n * LANES, LANES), LANES)
        wide = x[:, span].astype(f32)
        sxx[...] += wide * wide
        scaled = (wide * sgain[pl.ds(n, 1), :]).astype(bf16)
        sg[:, span] = scaled
        sgt[span, :] = scaled.T

    groups = x.shape[1] // LANES
    pl.loop(0, groups // 2)(scale)
    pl.semaphore_wait(barrier, 1 + (n_seg - 1) + (n_dp - 1) + (side - 1))
    u_sent = [to_seg(0, n, usend, ugot.at[me_s]) for n in range(1, n_seg)]
    for copy in u_sent:
        copy.start()
    pl.loop(groups // 2, groups)(scale)

    share = out.shape[0]

    def rows_of(owner):
        return sgt.at[pl.ds(pl.multiple_of(owner * share, share), share)]

    def owner_of(f, other_ring):
        return (1 - f) * (other_ring * side + y) + f * (z * side + other_ring)

    def block_copy(f, n):
        if f == 0:
            where = z * side + (y + n) % side
            owner = me_s * side + (y + n) % side
        else:
            where = ((z + n) % side) * side + y
            owner = ((z + n) % side) * side + me_s
        number = f * (side - 1) + n - 1
        return remote(
            rows_of(owner), nb.at[me_s, side - n, me_m], s_n.at[number], r_n.at[(n - 1) * 2 + me_m], dp=where, mp=f
        )

    def block_landed(m, n):
        where = nb.at[me_s, side - n, m]
        return remote(where, where, s_n.at[0], r_n.at[(n - 1) * 2 + m], mp=other)

    def chip_copy(n):
        return remote(rows_of(owner_of(other, n)), nb.at[n, 0, me_m], s_n.at[6 + n], r_n.at[6 + n], mp=other)

    def plane_copy(way, m, k):
        number = 10 + (way * 2 + m) * (side - 1) + k - 1
        block = nb.at[me_s, k, m]
        return remote(block, block, s_n.at[number], r_n.at[number], segment=(me_s + 1 + way * (n_seg - 2)) % n_seg)

    def plane_forward(way, k):
        number = 10 + (4 + way) * (side - 1) + k - 1
        block = nb.at[(me_s + n_seg - 1 + 2 * way) % n_seg, k, way]
        return remote(block, block, s_n.at[number], r_n.at[number], segment=(me_s + 1 + way * (n_seg - 2)) % n_seg)

    for n in (1, side - 1, 2):
        for f in (0, 1):
            block_copy(f, n).start()
    for n in range(side):
        chip_copy(n).start()
    sx_sent = to_peer(4, sxx, sxgot)
    sx_sent.start()

    away = pl.ds(pl.multiple_of(other * out_half, LANES), out_half)
    kept = pl.ds(pl.multiple_of(me_m * out_half, LANES), out_half)
    h_in.wait()
    down_in.wait()
    rank_all = down.shape[0]

    @pl.loop(0, n_seg)
    def _(g):
        span = pl.ds(pl.multiple_of(g * part, part), part)
        here = h[:, span]
        wide = here.astype(f32)
        scaled = (wide * gain[:, span].astype(f32)).astype(bf16)
        wide_a[:, :rank_all] += dot_nt(scaled, down[:, span])
        wide_b[:, :rank_all] += dot_nt(here, up[:, span])
        abx[:, LANES:] += jnp.broadcast_to(jnp.sum(wide * wide, axis=1, keepdims=True), (tok, LANES))

    id_col = turned(ids[...].astype(f32))
    lane2 = iota((tok, 2 * LANES), 1)
    own = (lane2 >> 6).astype(f32) == jnp.concatenate([id_col, id_col], axis=1)
    lane = iota((tok, LANES), 1)
    abx[:, :LANES] = jnp.where(lane < RANK, fold(wide_a[...], own), fold(wide_b[...], own))
    ab_sent = to_peer(0, abx, abgot)
    ab_sent.start()


    @pl.loop(0, tiles)
    def _(n):
        span = pl.ds(pl.multiple_of(n * tile, tile), tile)
        p_copy(n).wait()
        hpx[:, span] = dot(h[...], p[:, span])

    hpsend[...] = hpx[:, away].astype(bf16)
    hp_sent = to_peer(3, hpsend, hpgot)
    hp_sent.start()

    dest_f = dest[...].astype(f32)
    onehot = jnp.where(iota((n_dp, tok), 0).astype(f32) == dest_f, 1.0, 0.0)
    before = ones_where(iota((tok, tok), 0) < iota((tok, tok), 1))
    earlier = dot(onehot.astype(bf16), before)
    position = dest_f * cap + jnp.sum(earlier * onehot, axis=0, keepdims=True)
    sel[...] = ones_where(iota((slots, tok), 0).astype(f32) == position)
    ab_sent.wait_recv()
    total = abx[...] + abgot[...]
    sq = total[:, LANES:]
    sq_hi = sq.astype(bf16).astype(f32)
    extra = jnp.where(lane == 0, id_col, jnp.where(lane == 1, sq_hi, jnp.where(lane == 2, sq - sq_hi, 0.0)))
    pay[:, :LANES] = total[:, :LANES].astype(bf16)
    pay[:, LANES:] = extra.astype(bf16)
    lanes_here = pl.ds(pl.multiple_of(me_m * LANES, LANES), LANES)
    aslots[...] = dot(sel[...], pay[:, lanes_here]).astype(bf16).reshape(aslots.shape)
    agot[me_m, me_d] = aslots[me_d]

    def a_copy(n):
        return to_dp(0, n, aslots.at[(me_d + n) % n_dp], agot.at[me_m, me_d])

    @pl.loop(1, n_dp)
    def _(n):
        a_copy(n).start()

    hp_sent.wait_recv()
    hp = (hpx[:, kept] + hpgot[...].astype(f32)).astype(bf16)
    hslots[...] = dot(sel[...], hp).astype(bf16).reshape(hslots.shape)
    hgot[me_d] = hslots[me_d]

    def h_copy(n):
        return to_dp(1, n, hslots.at[(me_d + n) % n_dp], hgot.at[me_d])

    @pl.loop(1, n_dp)
    def _(n):
        h_copy(n).start()

    for n in (1, side - 1):
        for m in (0, 1):
            block_landed(m, n).wait_recv()
    for n in (1, side - 1):
        for way in (0, 1):
            plane_copy(way, way, n).start()

    for copy in u_sent:
        copy.wait_recv()
    row = iota((packed, n_seg * packed), 0)
    col = iota((packed, n_seg * packed), 1)
    quad = row >> 2
    block = (quad >= 3).astype(jnp.int32) + (quad >= 6).astype(jnp.int32) + (quad >= 9).astype(jnp.int32)
    got_u = ugot[...].reshape(n_seg * packed, part)
    for g in range(n_seg):
        take = ones_where(col == row + (packed - per) * block + per * g)
        ucat[:, g * part : (g + 1) * part] = dot(take, got_u).astype(bf16)
    u = ucat[...]
    u_scaled = (u.astype(f32) * gain[...].astype(f32)).astype(bf16)
    wide_a[:rows_u, :rank_all] = dot_nt(u_scaled, down[...])
    wide_b[:rows_u, :rank_all] = dot_nt(u, up[...])
    row = iota((rows_u, 2 * LANES), 0)
    quad = row >> 2
    block = (quad >= 3).astype(jnp.int32) + (quad >= 6).astype(jnp.int32) + (quad >= 9).astype(jnp.int32)
    same = (quad - 3 * block) == (iota((rows_u, 2 * LANES), 1) >> 6)
    lane_u = iota((rows_u, LANES), 1)
    mgx[...] = jnp.where(lane_u < RANK, fold(wide_a[:rows_u, :], same), fold(wide_b[:rows_u, :], same))
    mg_sent = to_peer(1, mgx, mggot)
    mg_sent.start()

    def up_tile(n):
        span = pl.ds(pl.multiple_of(n * tile, tile), tile)
        upx[:, span] = dot(ucat[...], p[:, span])

    pl.loop(0, 2)(up_tile)
    mg_sent.wait_recv()
    mgs[me_s] = (mgx[...] + mggot[...]).astype(bf16)
    mg_x = [to_seg(1, n, mgs.at[me_s], mgs.at[me_s]) for n in range(1, n_seg)]
    for copy in mg_x:
        copy.start()

    pl.loop(2, tiles)(up_tile)
    up_sent = to_peer(2, upx.at[:, away], upgot)
    up_sent.start()

    def student(n):
        span = pl.ds(pl.multiple_of(n * tile, tile), tile)
        w_copy(n).wait()
        sox[:, span] = dot(sg[...], w[:, span])

    pl.loop(0, 1)(student)

    up_sent.wait_recv()
    blocks[me_d] = (upx[:, kept] + upgot[...]).astype(bf16)
    firsts = [gather_first(n) for n in range(1, side)]
    for copy in firsts:
        copy.start()
    seconds = [gather_second(0, n) for n in range(1, side)]
    for copy in seconds:
        copy.start()

    for copy in mg_x:
        copy.wait_recv()
    for n in range(pair):
        tables[me_m, me_d, :, n * LANES : (n + 1) * LANES] = mgs[me_m * pair + n]

    def m_copy(n):
        return to_dp(2, n, tables.at[me_m, me_d], tables.at[me_m, me_d])

    @pl.loop(1, n_dp)
    def _(n):
        m_copy(n).start()

    @pl.loop(1, n_dp)
    def _(n):
        a_copy(n).wait_recv()

    a_x = [to_seg(2, n, aall.at[me_s], aall.at[me_s]) for n in range(1, n_seg)]
    extra_swap = to_peer(6, agot.at[1], agot.at[1])

    @pl.when(me_m == 0)
    def _():
        aall[me_s] = agot[0].reshape(slots, LANES)
        for copy in a_x:
            copy.start()

    @pl.when(me_m == 1)
    def _():
        extra_swap.start()

    for m in (0, 1):
        block_landed(m, 2).wait_recv()
    for way in (0, 1):
        plane_copy(way, way, 2).start()
    for n in (1, side - 1, 2):
        for way in (0, 1):
            plane_copy(way, 1 - way, n).start()

    pl.loop(1, 3)(student)

    def gather_on(k):
        firsts[k - 1].wait_recv()
        copies = [gather_second(k, n) for n in range(1, side)]
        for copy in copies:
            copy.start()
        return copies

    seconds += gather_on(1) + gather_on(side - 1)
    pl.loop(3, 4)(student)
    seconds += gather_on(2)
    pl.loop(4, tiles)(student)
    sosend[...] = sox[:, away].astype(bf16)
    so_sent = to_peer(5, sosend, sogot)
    so_sent.start()
    a_swap = to_peer(7, aall, aall)

    @pl.when(me_m == 0)
    def _():
        for copy in a_x:
            copy.wait_recv()
        a_swap.start()

    for n in (1, side - 1, 2):
        for way in (0, 1):
            plane_copy(way, way, n).wait_recv()
            plane_forward(way, n).start()

    for n in range(side):
        nb[n, 0, me_m] = rows_of(owner_of(me_m, n))[...]

    @pl.loop(1, n_dp)
    def _(n):
        m_copy(n).wait_recv()

    table_swap = to_peer(8, tables.at[me_m], tables.at[me_m])
    table_swap.start()

    @pl.when(me_m == 0)
    def _():
        extra_swap.wait_recv()

    @pl.when(me_m == 1)
    def _():
        a_swap.wait_recv()

    xmap_in.wait()
    extra = agot[1].reshape(slots, LANES).astype(f32)
    id_slot = extra[:, 0:1]
    norm = extra[:, 1:2] + extra[:, 2:3]
    keep = kcol[...] == id_slot
    lane = iota((slots, LANES), 1)
    known = rows_u * n_dp
    both = jnp.zeros((slots, LANES), f32)
    table_swap.wait_recv()
    for s in range(n_seg):
        ab = aall[s].astype(f32)
        lat = (ab + both) * lax.rsqrt(jnp.maximum(norm, 0.0) * (1.0 / D) + 1e-06)
        lat = lat.astype(bf16)
        lat_low = jnp.where(lane < RANK, lat.astype(f32), 0.0)
        wide_c = jnp.where(keep, dot(lat_low.astype(bf16), xmap[s]), 0.0).astype(bf16)
        if s == 0:
            ctil[...] = wide_c
        else:
            ctil[...] += wide_c
        if s + 1 < n_seg:
            low, high = (s % pair) * LANES, ((s + 1) % pair) * LANES
            here = tables[s // pair, :, :, low : low + LANES].reshape(known, LANES)
            after = tables[(s + 1) // pair, :, :, high : high + LANES].reshape(known, LANES)
            self_part = dot(ctil[...], here)
            lat_high = pltpu.roll(lat_low, RANK, 1)
            norm = norm + jnp.sum(lat_high * (2.0 * ab + both + self_part), axis=1, keepdims=True)
            both = dot(ctil[...], after)

    @pl.loop(1, n_dp)
    def _(n):
        h_copy(n).wait_recv()

    sx_sent.wait()
    so_sent.wait_recv()
    slot = iota((slots, n_dp), 0)
    source = iota((slots, n_dp), 1)
    room = slot - source * cap
    valid = jnp.sum(
        jnp.where((room >= 0) & (room < cap) & (room < counts[...]), 1.0, 0.0), axis=1, keepdims=True
    )
    square = jnp.sum(sxx[...] + sxgot[...], axis=1, keepdims=True)
    recip = lax.rsqrt(square * (1.0 / S) + 1e-06)
    student_out = (sox[:, kept] + sogot[...].astype(f32)) * recip
    base[...] = jnp.where(valid > 0.0, student_out - hgot[...].reshape(slots, out_half).astype(f32), 0.0)
    sxx[...] = jnp.broadcast_to(recip * (1.0 / TOK_DEV), sxx.shape)
    for copy in seconds:
        copy.wait_recv()
    table = blocks[...].reshape(known, out_half)
    edge = slots // 2

    def gathered(ahead, low=0, count=slots):
        return p.at[pl.ds(ahead * slots + low, count), :out_half]

    def diff_copy(way, part):
        ahead = (side - 1, 1)[way]
        number = way * 2 + part
        return remote(
            gathered(0, part * edge, edge), gathered(ahead, part * edge, edge),
            s_r.at[number], r_r.at[number], dp=place(1 + way * (side - 2), 0),
        )

    def diff_forward(way):
        ahead = (side - 1, 1)[way]
        return remote(
            gathered(ahead, way * edge, edge), gathered(2, way * edge, edge),
            s_r.at[4 + way], r_r.at[4 + way], dp=place(1 + way * (side - 2), 0),
        )

    def difference(part):
        rows = slice(part * edge, (part + 1) * edge)
        diff = base[rows, :] - dot(ctil[rows, :], table)
        gathered(0, part * edge, edge)[...] = (diff * sxx[rows, 0:1]).astype(bf16)
        loss = jnp.sum(diff * diff, axis=1, keepdims=True)
        losspart[:, rows] = jnp.broadcast_to(loss, (edge, LANES)).T[0:1, :]

    difference(0)
    diff_copy(0, 0).start()
    difference(1)
    diff_copy(1, 1).start()
    for way in (0, 1):
        diff_copy(way, 1 - way).start()
    loss_swap = to_peer(9, losspart, lossgot)
    loss_swap.start()
    def product(owner, ahead):
        return dot(nb[owner, ahead].reshape(2 * share, slots), gathered(ahead)[...])

    for n in range(side):
        chip_copy(n).wait_recv()

    @pl.loop(0, side)
    def _(n):
        held[n] = product(n, 0)

    for way in (0, 1):
        diff_copy(way, way).wait_recv()
        diff_forward(way).start()
    loss_swap.wait_recv()
    losses[me_s] = losspart[...] + lossgot[...]
    tells = [to_seg(3, n, losses.at[me_s], losses.at[me_s]) for n in range(1, n_seg)]
    for copy in tells:
        copy.start()
    for way in (0, 1):
        for n in range(1, side):
            plane_copy(way, 1 - way, n).wait_recv()
            plane_forward(way, n).wait_recv()
    for way in (0, 1):
        diff_copy(way, 1 - way).wait_recv()

    @pl.loop(0, side)
    def _(n):
        held[n] += product(n, 1) + product(n, 3)

    for copy in tells:
        copy.wait_recv()
    total = losses[0]
    for n in range(1, n_seg):
        total = total + losses[n]
    loss_out[...] = total * (1.0 / S)

    ring_at = z * other + y * me_m
    below = side * slots

    def sent(slot, m):
        return p.at[pl.ds(below + (slot * 2 + m) * share, share), :out_half]

    def landed(number):
        return p.at[pl.ds(pl.multiple_of(below + number * share, 16), share), out_half:]

    def far_copy(way):
        return remote(
            sent(0, way), landed(way), s_r.at[6 + way], r_r.at[6 + way], dp=place(0, 1 + way * (side - 2))
        )

    def near_copy(way, last):
        m = way if last else 1 - way
        number = 2 * me_m + last
        return remote(
            sent(1 + way, m), landed(2 + number), s_r.at[8 + 2 * way + last], r_r.at[8 + number],
            dp=place(0, 1 + way * (side - 2)), mp=m,
        )

    def near_landed(f, last):
        where = landed(2 + 2 * f + last)
        return remote(where, where, s_r.at[0], r_r.at[8 + 2 * f + last], mp=other)

    for way in (0, 1):
        diff_forward(way).wait_recv()
    far = (ring_at + 2) % side
    nears = [(ring_at + 1) % side, (ring_at + side - 1) % side]

    def half_rows(m):
        return pl.ds(m * share, share)

    block = held[far] + product(far, 2)
    for way in (0, 1):
        sent(0, way)[...] = block[way * share : (way + 1) * share].astype(bf16)
        far_copy(way).start()
    for way in (0, 1):
        block = held[nears[way]] + product(nears[way], 2)
        sent(1 + way, 1 - way)[...] = block[(1 - way) * share : (2 - way) * share].astype(bf16)
        near_copy(way, 0).start()
        held[nears[way], half_rows(way)] = block[way * share : (way + 1) * share]
    held[ring_at] += product(ring_at, 2)
    finsend[...] = held[ring_at, pl.ds(pl.multiple_of(other * share, share), share)]
    own_swap = to_peer(10, finsend, fingot)
    own_swap.start()
    for way in (0, 1):
        far_copy(way).wait_recv()
        sent(1 + way, way)[...] = (held[nears[way], half_rows(way)] + landed(way)[...].astype(f32)).astype(bf16)
        near_copy(way, 1).start()
    own_swap.wait_recv()
    mine = held[ring_at, pl.ds(pl.multiple_of(me_m * share, share), share)]
    for last in (0, 1):
        near_landed(me_m, last).wait_recv()
        near_landed(other, last).wait_recv()
    out[:, kept] = mine + landed(2 + 2 * me_m)[...].astype(f32) + landed(3 + 2 * me_m)[...].astype(f32)
    out[:, away] = fingot[...] + landed(2 + 2 * other)[...].astype(f32) + landed(3 + 2 * other)[...].astype(f32)

    for n in range(1, side):
        for f in (0, 1):
            block_copy(f, n).wait_send()
    for n in range(side):
        chip_copy(n).wait_send()
    for way in (0, 1):
        for n in range(1, side):
            for m in (0, 1):
                plane_copy(way, m, n).wait_send()
            plane_forward(way, n).wait_send()
        for m in (0, 1):
            diff_copy(way, m).wait_send()
        diff_forward(way).wait_send()
        far_copy(way).wait_send()
        for last in (0, 1):
            near_copy(way, last).wait_send()
    for copy in u_sent + mg_x + firsts + seconds + [ab_sent, mg_sent, up_sent, hp_sent, so_sent, table_swap, loss_swap, own_swap] + tells:
        copy.wait_send()

    @pl.when(me_m == 0)
    def _():
        for copy in a_x + [a_swap]:
            copy.wait_send()

    @pl.when(me_m == 1)
    def _():
        extra_swap.wait_send()

    @pl.loop(1, n_dp)
    def _(n):
        a_copy(n).wait_send()
        m_copy(n).wait_send()
        h_copy(n).wait_send()


def run_step(h, ids, dest, counts, gain, down, up, x, sgain, w, p):
    side = 4
    n_seg = lax.axis_size("segment")
    n_dp = lax.axis_size("dp")
    tok, half = h.shape
    slots, width = x.shape
    cols = p.shape[1]
    out_half = cols // 2
    cap = slots // n_dp
    q = RANK // n_dp
    per = TEACH * q
    rows_u = n_seg * per
    known = rows_u * n_dp
    share = width // n_dp
    c = np.arange(known)
    c_i, c_t, c_k, c_q = c // rows_u, c % rows_u // per, c % per // q, c % q
    spot = np.arange(LANES)[None, :, None]
    xmap = (np.arange(n_seg)[:, None, None] == c_t) & (spot == c_i * q + c_q)
    xmap = jnp.asarray(xmap.astype(np.float32), dtype=bf16)
    kcol = jnp.asarray(c_k[None, :].astype(np.float32))
    vmem = pl.BlockSpec(memory_space=pltpu.VMEM)
    hbm = pl.BlockSpec(memory_space=pl.ANY)
    flops = 2 * (tok * half * cols + 2 * slots * width * cols)
    scratch = [
        (h.shape, bf16), (down.shape, bf16), (up.shape, bf16), (x.shape, bf16), (w.shape, bf16), (p.shape, bf16),
        (xmap.shape, bf16),
        ((rows_u, half // n_seg), bf16), ((n_seg, rows_u, half // n_seg), bf16), ((rows_u, half), bf16),
        ((tok, 2 * LANES), f32), ((tok, 2 * LANES), f32), ((tok, 2 * LANES), f32), ((tok, 2 * LANES), f32),
        ((slots, tok), bf16), ((tok, 2 * LANES), bf16),
        ((n_dp, cap, LANES), bf16), ((2, n_dp, cap, LANES), bf16), ((n_seg, slots, LANES), bf16),
        ((rows_u, LANES), f32), ((rows_u, LANES), f32), ((n_seg, rows_u, LANES), bf16),
        ((rows_u, cols), f32), ((rows_u, out_half), f32),
        ((n_dp, rows_u, out_half), bf16), ((2, n_dp, rows_u, n_seg // 2 * LANES), bf16),
        ((tok, cols), f32), ((tok, out_half), bf16), ((tok, out_half), bf16),
        ((n_dp, cap, out_half), bf16), ((n_dp, cap, out_half), bf16),
        (x.shape, bf16), ((slots, cols), f32), ((slots, out_half), bf16), ((slots, out_half), bf16),
        ((slots, LANES), f32), ((slots, LANES), f32), ((slots, known), bf16), ((slots, out_half), f32),
        ((width, slots), bf16), ((n_seg, side, 2, share, slots), bf16), ((side, 2 * share, out_half), f32),
        ((share, out_half), f32), ((share, out_half), f32),
        ((1, slots), f32), ((1, slots), f32), ((n_seg, 1, slots), f32),
    ]
    sems = [5 + cols // LANES, 11, 11, 4 * (n_seg - 1), 4 * (n_seg - 1), 4 * (n_dp - 1), 4 * (n_dp - 1), 28, 28, 12, 12]
    return pl.pallas_call(
        functools.partial(step_kernel, n_seg, side, cap),
        out_shape=(
            jax.ShapeDtypeStruct((share, cols), f32),
            jax.ShapeDtypeStruct((1, slots), f32),
        ),
        in_specs=[hbm] * 7 + [vmem] * 6,
        out_specs=(vmem, vmem),
        scratch_shapes=[pltpu.VMEM(*s) for s in scratch] + [pltpu.SemaphoreType.DMA((n,)) for n in sems],
        compiler_params=pltpu.CompilerParams(
            collective_id=0, has_side_effects=True, vmem_limit_bytes=60 * 2**20
        ),
        cost_estimate=pl.CostEstimate(flops=flops, bytes_accessed=25 * 2**20, transcendentals=0),
    )(
        h, down, up, x, w, p, xmap,
        ids.reshape(1, tok), dest.reshape(1, tok), counts, gain, sgain.reshape(width // LANES, LANES), kcol,
    )


def finish_kernel(grad, loss, grad_out, loss_out):
    grad_out[...] = grad[...]
    loss_out[...] = loss[...]


def finish(grad, loss):
    vmem = pl.BlockSpec(memory_space=pltpu.VMEM)
    return pl.pallas_call(
        finish_kernel,
        out_shape=(jax.ShapeDtypeStruct(grad.shape, f32), jax.ShapeDtypeStruct(loss.shape, f32)),
        in_specs=[vmem, vmem],
        out_specs=(vmem, vmem),
    )(grad, loss)


def local(
    teacher_hidden,
    teacher_id,
    destination,
    row_counts,
    section_gain,
    adapter_down,
    adapter_up,
    student_in,
    student_gain,
    student_weight,
    projector,
):
    weight_grad, row_loss = run_step(
        teacher_hidden,
        teacher_id,
        destination,
        row_counts,
        section_gain,
        adapter_down[0].T,
        adapter_up[0],
        student_in,
        student_gain,
        student_weight,
        projector,
    )
    weight_grad, row_loss = finish(weight_grad, row_loss)
    share, cols = weight_grad.shape
    return (weight_grad.reshape(1, share, cols), row_loss.reshape(student_in.shape[0]))


def solution(mesh):
    placed = (
        P("dp", "mp"),
        P("dp"),
        P("dp"),
        P("dp", None),
        P("segment", "mp"),
        P("segment", "mp", None),
        P("segment", None, "mp"),
        P("dp", "mp"),
        P("mp"),
        P("mp", "segment"),
        P("mp", "segment"),
    )
    return jax.shard_map(
        local,
        mesh=mesh,
        in_specs=placed,
        out_specs=(P("mp", "dp", "segment"), P("dp")),
        check_vma=False,
    )
```

```python
import functools

import jax
import jax.numpy as jnp
import numpy as np
from jax import lax
from jax.experimental import pallas as pl
from jax.experimental.pallas import tpu as pltpu
from jax.sharding import PartitionSpec as P

D = 8192
S = 5120
RANK = 64
TOK_DEV = 256
TEACH = 3
LANES = 128
bf16 = jnp.bfloat16
f32 = jnp.float32


def dot(a, b):
    return jnp.dot(a, b, preferred_element_type=f32)


def remote(src, dst, send, recv, **where):
    return pltpu.make_async_remote_copy(
        src_ref=src,
        dst_ref=dst,
        send_sem=send,
        recv_sem=recv,
        device_id=where,
        device_id_type=pl.DeviceIdType.MESH,
    )


def iota(shape, dim):
    return lax.broadcasted_iota(jnp.int32, shape, dim)


def ones_where(mask):
    return jnp.where(mask, 1.0, 0.0).astype(bf16)


def dot_nt(a, b):
    return lax.dot_general(a, b, (((1,), (1,)), ((), ())), preferred_element_type=f32)


def turned(row):
    return jnp.broadcast_to(row, (LANES, row.shape[1])).T


def fold(wide, keep):
    kept = jnp.where(keep, wide, 0.0)
    both = kept[:, :LANES] + kept[:, LANES:]
    return both + pltpu.roll(both, RANK, 1)


def step_kernel(
    n_seg, side, cap,
    h_hbm, down_hbm, up_hbm, x_hbm, w_hbm, p_hbm, xmap_hbm,
    ids, dest, counts, gain, sgain, kcol,
    out, loss_out,
    h, down, up, x, w, p, xmap,
    usend, ugot, ucat, wide_a, wide_b, abx, abgot, sel, pay, aslots, agot, aall,
    mgx, mggot, mgs, upx, upgot, blocks, tables,
    hpx, hpsend, hpgot, hslots, hgot,
    sg, sox, sosend, sogot, sxx, sxgot, ctil, base,
    sgt, nb, held, finsend, fingot, losspart, lossgot, losses,
    lsem, s_m, r_m, s_x, r_x, s_d, r_d, s_n, r_n, s_r, r_r,
):
    me_s = lax.axis_index("segment")
    me_m = lax.axis_index("mp")
    me_d = lax.axis_index("dp")
    other = 1 - me_m
    n_dp = side * side
    tok, half = h.shape
    slots = x.shape[0]
    cols = p.shape[1]
    out_half = cols // 2
    rows_u = mgx.shape[0]
    per = rows_u // n_seg
    part = half // n_seg
    tile = 2 * LANES
    tiles = cols // tile
    pair = n_seg // 2

    def load(n, src, dst):
        copy = pltpu.make_async_copy(src, dst, lsem.at[n])
        copy.start()
        return copy

    def p_copy(n):
        span = pl.ds(pl.multiple_of(n * tile, tile), tile)
        return pltpu.make_async_copy(p_hbm.at[:, span], p.at[:, span], lsem.at[5 + n])

    def w_copy(n):
        span = pl.ds(pl.multiple_of(n * tile, tile), tile)
        return pltpu.make_async_copy(w_hbm.at[:, span], w.at[:, span], lsem.at[5 + tiles + n])

    up_in = load(0, up_hbm, up)
    x_in = load(3, x_hbm, x)
    h_in = load(1, h_hbm, h)
    down_in = load(2, down_hbm, down)
    for n in range(tiles):
        p_copy(n).start()
    for n in range(tiles):
        w_copy(n).start()
    xmap_in = load(4, xmap_hbm, xmap)

    z = me_d // side
    y = me_d % side

    def place(first, second):
        a = ((z * other + y * me_m) + second) % side
        b = ((y * other + z * me_m) + first) % side
        return (a * other + b * me_m) * side + b * other + a * me_m

    barrier = pltpu.get_barrier_semaphore()
    mesh_id = pl.DeviceIdType.MESH
    pl.semaphore_signal(barrier, inc=1, device_id={"mp": other}, device_id_type=mesh_id)
    for n in range(1, n_seg):
        pl.semaphore_signal(barrier, inc=1, device_id={"segment": (me_s + n) % n_seg}, device_id_type=mesh_id)

    @pl.loop(1, n_dp)
    def _(n):
        pl.semaphore_signal(barrier, inc=1, device_id={"dp": (me_d + n) % n_dp}, device_id_type=mesh_id)

    for n in range(1, side):
        pl.semaphore_signal(barrier, inc=1, device_id={"dp": place(n, 0), "mp": other}, device_id_type=mesh_id)

    def to_peer(n, src, dst):
        return remote(src, dst, s_m.at[n], r_m.at[n], mp=other)

    def to_seg(kind, n, src, dst):
        number = kind * (n_seg - 1) + n - 1
        return remote(src, dst, s_x.at[number], r_x.at[number], segment=(me_s + n) % n_seg)

    def to_dp(kind, n, src, dst):
        number = kind * (n_dp - 1) + n - 1
        return remote(src, dst, s_d.at[number], r_d.at[number], dp=(me_d + n) % n_dp)

    def gather_first(n):
        return remote(blocks.at[me_d], blocks.at[me_d], s_d.at[n + 44], r_d.at[n + 44], dp=place(n, 0))

    def gather_second(k, n):
        source = place(side - k, 0)
        number = 48 + k * (side - 1) + n - 1
        return remote(blocks.at[source], blocks.at[source], s_d.at[number], r_d.at[number], dp=place(0, n))

    packed = n_seg * per
    row = iota((packed, up.shape[0]), 0)
    col = iota((packed, up.shape[0]), 1)
    quad = row >> 2
    block = (quad >= 3).astype(jnp.int32) + (quad >= 6).astype(jnp.int32) + (quad >= 9).astype(jnp.int32)
    teacher = quad - 3 * block
    hit = ((col >> 6) == teacher) & (((col & 63) >> 2) == me_d) & ((col & 3) == (row & 3))
    up_in.wait()
    mine = jnp.zeros((packed, part), f32)
    for g in range(n_seg):
        mine = mine + dot(ones_where(hit & (block == g)), up[:, g * part : (g + 1) * part])
    usend[...] = mine.astype(bf16)
    ugot[me_s] = usend[...]
    wide_a[...] = jnp.zeros(wide_a.shape, f32)
    wide_b[...] = jnp.zeros(wide_b.shape, f32)
    abx[...] = jnp.zeros(abx.shape, f32)

    x_in.wait()
    sxx[...] = jnp.zeros(sxx.shape, f32)

    def scale(n):
        span = pl.ds(pl.multiple_of(n * LANES, LANES), LANES)
        wide = x[:, span].astype(f32)
        sxx[...] += wide * wide
        scaled = (wide * sgain[pl.ds(n, 1), :]).astype(bf16)
        sg[:, span] = scaled
        sgt[span, :] = scaled.T

    groups = x.shape[1] // LANES
    pl.loop(0, groups // 2)(scale)
    pl.semaphore_wait(barrier, 1 + (n_seg - 1) + (n_dp - 1) + (side - 1))
    u_sent = [to_seg(0, n, usend, ugot.at[me_s]) for n in range(1, n_seg)]
    for copy in u_sent:
        copy.start()
    pl.loop(groups // 2, groups)(scale)

    share = out.shape[0]

    def rows_of(owner):
        return sgt.at[pl.ds(pl.multiple_of(owner * share, share), share)]

    def owner_of(f, other_ring):
        return (1 - f) * (other_ring * side + y) + f * (z * side + other_ring)

    def block_copy(f, n):
        if f == 0:
            where = z * side + (y + n) % side
            owner = me_s * side + (y + n) % side
        else:
            where = ((z + n) % side) * side + y
            owner = ((z + n) % side) * side + me_s
        number = f * (side - 1) + n - 1
        return remote(
            rows_of(owner), nb.at[me_s, side - n, me_m], s_n.at[number], r_n.at[(n - 1) * 2 + me_m], dp=where, mp=f
        )

    def block_landed(m, n):
        where = nb.at[me_s, side - n, m]
        return remote(where, where, s_n.at[0], r_n.at[(n - 1) * 2 + m], mp=other)

    def chip_copy(n):
        return remote(rows_of(owner_of(other, n)), nb.at[n, 0, me_m], s_n.at[6 + n], r_n.at[6 + n], mp=other)

    def plane_copy(way, m, k):
        number = 10 + (way * 2 + m) * (side - 1) + k - 1
        block = nb.at[me_s, k, m]
        return remote(block, block, s_n.at[number], r_n.at[number], segment=(me_s + 1 + way * (n_seg - 2)) % n_seg)

    def plane_forward(way, k):
        number = 10 + (4 + way) * (side - 1) + k - 1
        block = nb.at[(me_s + n_seg - 1 + 2 * way) % n_seg, k, way]
        return remote(block, block, s_n.at[number], r_n.at[number], segment=(me_s + 1 + way * (n_seg - 2)) % n_seg)

    for n in (1, side - 1, 2):
        for f in (0, 1):
            block_copy(f, n).start()
    for n in range(side):
        chip_copy(n).start()
    sx_sent = to_peer(4, sxx, sxgot)
    sx_sent.start()

    away = pl.ds(pl.multiple_of(other * out_half, LANES), out_half)
    kept = pl.ds(pl.multiple_of(me_m * out_half, LANES), out_half)
    h_in.wait()
    down_in.wait()
    rank_all = down.shape[0]

    @pl.loop(0, n_seg)
    def _(g):
        span = pl.ds(pl.multiple_of(g * part, part), part)
        here = h[:, span]
        wide = here.astype(f32)
        scaled = (wide * gain[:, span].astype(f32)).astype(bf16)
        wide_a[:, :rank_all] += dot_nt(scaled, down[:, span])
        wide_b[:, :rank_all] += dot_nt(here, up[:, span])
        abx[:, LANES:] += jnp.broadcast_to(jnp.sum(wide * wide, axis=1, keepdims=True), (tok, LANES))

    id_col = turned(ids[...].astype(f32))
    lane2 = iota((tok, 2 * LANES), 1)
    own = (lane2 >> 6).astype(f32) == jnp.concatenate([id_col, id_col], axis=1)
    lane = iota((tok, LANES), 1)
    abx[:, :LANES] = jnp.where(lane < RANK, fold(wide_a[...], own), fold(wide_b[...], own))
    ab_sent = to_peer(0, abx, abgot)
    ab_sent.start()


    @pl.loop(0, tiles)
    def _(n):
        span = pl.ds(pl.multiple_of(n * tile, tile), tile)
        p_copy(n).wait()
        hpx[:, span] = dot(h[...], p[:, span])

    hpsend[...] = hpx[:, away].astype(bf16)
    hp_sent = to_peer(3, hpsend, hpgot)
    hp_sent.start()
    for n in (1, side - 1):
        for m in (0, 1):
            block_landed(m, n).wait_recv()
    for n in (1, side - 1):
        for way in (0, 1):
            plane_copy(way, way, n).start()

    dest_f = dest[...].astype(f32)
    onehot = jnp.where(iota((n_dp, tok), 0).astype(f32) == dest_f, 1.0, 0.0)
    before = ones_where(iota((tok, tok), 0) < iota((tok, tok), 1))
    earlier = dot(onehot.astype(bf16), before)
    position = dest_f * cap + jnp.sum(earlier * onehot, axis=0, keepdims=True)
    sel[...] = ones_where(iota((slots, tok), 0).astype(f32) == position)
    ab_sent.wait_recv()
    total = abx[...] + abgot[...]
    sq = total[:, LANES:]
    sq_hi = sq.astype(bf16).astype(f32)
    extra = jnp.where(lane == 0, id_col, jnp.where(lane == 1, sq_hi, jnp.where(lane == 2, sq - sq_hi, 0.0)))
    pay[:, :LANES] = total[:, :LANES].astype(bf16)
    pay[:, LANES:] = extra.astype(bf16)
    lanes_here = pl.ds(pl.multiple_of(me_m * LANES, LANES), LANES)
    aslots[...] = dot(sel[...], pay[:, lanes_here]).astype(bf16).reshape(aslots.shape)
    agot[me_m, me_d] = aslots[me_d]

    def a_copy(n):
        return to_dp(0, n, aslots.at[(me_d + n) % n_dp], agot.at[me_m, me_d])

    @pl.loop(1, n_dp)
    def _(n):
        a_copy(n).start()

    hp_sent.wait_recv()
    hp = (hpx[:, kept] + hpgot[...].astype(f32)).astype(bf16)
    hslots[...] = dot(sel[...], hp).astype(bf16).reshape(hslots.shape)
    hgot[me_d] = hslots[me_d]

    def h_copy(n):
        return to_dp(1, n, hslots.at[(me_d + n) % n_dp], hgot.at[me_d])

    @pl.loop(1, n_dp)
    def _(n):
        h_copy(n).start()

    for copy in u_sent:
        copy.wait_recv()
    row = iota((packed, n_seg * packed), 0)
    col = iota((packed, n_seg * packed), 1)
    quad = row >> 2
    block = (quad >= 3).astype(jnp.int32) + (quad >= 6).astype(jnp.int32) + (quad >= 9).astype(jnp.int32)
    got_u = ugot[...].reshape(n_seg * packed, part)
    for g in range(n_seg):
        take = ones_where(col == row + (packed - per) * block + per * g)
        ucat[:, g * part : (g + 1) * part] = dot(take, got_u).astype(bf16)
    u = ucat[...]
    u_scaled = (u.astype(f32) * gain[...].astype(f32)).astype(bf16)
    wide_a[:rows_u, :rank_all] = dot_nt(u_scaled, down[...])
    wide_b[:rows_u, :rank_all] = dot_nt(u, up[...])
    row = iota((rows_u, 2 * LANES), 0)
    quad = row >> 2
    block = (quad >= 3).astype(jnp.int32) + (quad >= 6).astype(jnp.int32) + (quad >= 9).astype(jnp.int32)
    same = (quad - 3 * block) == (iota((rows_u, 2 * LANES), 1) >> 6)
    lane_u = iota((rows_u, LANES), 1)
    mgx[...] = jnp.where(lane_u < RANK, fold(wide_a[:rows_u, :], same), fold(wide_b[:rows_u, :], same))
    mg_sent = to_peer(1, mgx, mggot)
    mg_sent.start()

    def up_tile(n):
        span = pl.ds(pl.multiple_of(n * tile, tile), tile)
        upx[:, span] = dot(ucat[...], p[:, span])

    pl.loop(0, 2)(up_tile)
    mg_sent.wait_recv()
    mgs[me_s] = (mgx[...] + mggot[...]).astype(bf16)
    mg_x = [to_seg(1, n, mgs.at[me_s], mgs.at[me_s]) for n in range(1, n_seg)]
    for copy in mg_x:
        copy.start()

    pl.loop(2, tiles)(up_tile)
    up_sent = to_peer(2, upx.at[:, away], upgot)
    up_sent.start()

    def student(n):
        span = pl.ds(pl.multiple_of(n * tile, tile), tile)
        w_copy(n).wait()
        sox[:, span] = dot(sg[...], w[:, span])

    pl.loop(0, 1)(student)

    up_sent.wait_recv()
    blocks[me_d] = (upx[:, kept] + upgot[...]).astype(bf16)
    firsts = [gather_first(n) for n in range(1, side)]
    for copy in firsts:
        copy.start()
    seconds = [gather_second(0, n) for n in range(1, side)]
    for copy in seconds:
        copy.start()

    for copy in mg_x:
        copy.wait_recv()
    for n in range(pair):
        tables[me_m, me_d, :, n * LANES : (n + 1) * LANES] = mgs[me_m * pair + n]

    def m_copy(n):
        return to_dp(2, n, tables.at[me_m, me_d], tables.at[me_m, me_d])

    @pl.loop(1, n_dp)
    def _(n):
        m_copy(n).start()

    @pl.loop(1, n_dp)
    def _(n):
        a_copy(n).wait_recv()

    a_x = [to_seg(2, n, aall.at[me_s], aall.at[me_s]) for n in range(1, n_seg)]
    extra_swap = to_peer(6, agot.at[1], agot.at[1])

    @pl.when(me_m == 0)
    def _():
        aall[me_s] = agot[0].reshape(slots, LANES)
        for copy in a_x:
            copy.start()

    @pl.when(me_m == 1)
    def _():
        extra_swap.start()

    for m in (0, 1):
        block_landed(m, 2).wait_recv()
    for way in (0, 1):
        plane_copy(way, way, 2).start()
    for n in (1, side - 1, 2):
        for way in (0, 1):
            plane_copy(way, 1 - way, n).start()

    pl.loop(1, 3)(student)

    def gather_on(k):
        firsts[k - 1].wait_recv()
        copies = [gather_second(k, n) for n in range(1, side)]
        for copy in copies:
            copy.start()
        return copies

    seconds += gather_on(1) + gather_on(side - 1)
    pl.loop(3, 4)(student)
    seconds += gather_on(2)
    pl.loop(4, tiles)(student)
    sosend[...] = sox[:, away].astype(bf16)
    so_sent = to_peer(5, sosend, sogot)
    so_sent.start()
    a_swap = to_peer(7, aall, aall)

    @pl.when(me_m == 0)
    def _():
        for copy in a_x:
            copy.wait_recv()
        a_swap.start()

    for n in (1, side - 1, 2):
        for way in (0, 1):
            plane_copy(way, way, n).wait_recv()
            plane_forward(way, n).start()

    for n in range(side):
        nb[n, 0, me_m] = rows_of(owner_of(me_m, n))[...]

    @pl.loop(1, n_dp)
    def _(n):
        m_copy(n).wait_recv()

    table_swap = to_peer(8, tables.at[me_m], tables.at[me_m])
    table_swap.start()

    @pl.when(me_m == 0)
    def _():
        extra_swap.wait_recv()

    @pl.when(me_m == 1)
    def _():
        a_swap.wait_recv()

    xmap_in.wait()
    extra = agot[1].reshape(slots, LANES).astype(f32)
    id_slot = extra[:, 0:1]
    norm = extra[:, 1:2] + extra[:, 2:3]
    keep = kcol[...] == id_slot
    lane = iota((slots, LANES), 1)
    known = rows_u * n_dp
    both = jnp.zeros((slots, LANES), f32)
    table_swap.wait_recv()
    for s in range(n_seg):
        ab = aall[s].astype(f32)
        lat = (ab + both) * lax.rsqrt(jnp.maximum(norm, 0.0) * (1.0 / D) + 1e-06)
        lat = lat.astype(bf16)
        lat_low = jnp.where(lane < RANK, lat.astype(f32), 0.0)
        wide_c = jnp.where(keep, dot(lat_low.astype(bf16), xmap[s]), 0.0).astype(bf16)
        if s == 0:
            ctil[...] = wide_c
        else:
            ctil[...] += wide_c
        if s + 1 < n_seg:
            low, high = (s % pair) * LANES, ((s + 1) % pair) * LANES
            here = tables[s // pair, :, :, low : low + LANES].reshape(known, LANES)
            after = tables[(s + 1) // pair, :, :, high : high + LANES].reshape(known, LANES)
            self_part = dot(ctil[...], here)
            lat_high = pltpu.roll(lat_low, RANK, 1)
            norm = norm + jnp.sum(lat_high * (2.0 * ab + both + self_part), axis=1, keepdims=True)
            both = dot(ctil[...], after)

    @pl.loop(1, n_dp)
    def _(n):
        h_copy(n).wait_recv()

    sx_sent.wait()
    so_sent.wait_recv()
    slot = iota((slots, n_dp), 0)
    source = iota((slots, n_dp), 1)
    room = slot - source * cap
    valid = jnp.sum(
        jnp.where((room >= 0) & (room < cap) & (room < counts[...]), 1.0, 0.0), axis=1, keepdims=True
    )
    square = jnp.sum(sxx[...] + sxgot[...], axis=1, keepdims=True)
    recip = lax.rsqrt(square * (1.0 / S) + 1e-06)
    student_out = (sox[:, kept] + sogot[...].astype(f32)) * recip
    base[...] = jnp.where(valid > 0.0, student_out - hgot[...].reshape(slots, out_half).astype(f32), 0.0)
    sxx[...] = jnp.broadcast_to(recip * (1.0 / TOK_DEV), sxx.shape)
    for copy in seconds:
        copy.wait_recv()
    table = blocks[...].reshape(known, out_half)
    edge = slots // 2

    def gathered(ahead, low=0, count=slots):
        return p.at[pl.ds(ahead * slots + low, count), :out_half]

    def diff_copy(way, part):
        ahead = (side - 1, 1)[way]
        number = way * 2 + part
        return remote(
            gathered(0, part * edge, edge), gathered(ahead, part * edge, edge),
            s_r.at[number], r_r.at[number], dp=place(1 + way * (side - 2), 0),
        )

    def diff_forward(way):
        ahead = (side - 1, 1)[way]
        return remote(
            gathered(ahead, way * edge, edge), gathered(2, way * edge, edge),
            s_r.at[4 + way], r_r.at[4 + way], dp=place(1 + way * (side - 2), 0),
        )

    def difference(part):
        rows = slice(part * edge, (part + 1) * edge)
        diff = base[rows, :] - dot(ctil[rows, :], table)
        gathered(0, part * edge, edge)[...] = (diff * sxx[rows, 0:1]).astype(bf16)
        loss = jnp.sum(diff * diff, axis=1, keepdims=True)
        losspart[:, rows] = jnp.broadcast_to(loss, (edge, LANES)).T[0:1, :]

    difference(0)
    diff_copy(0, 0).start()
    difference(1)
    diff_copy(1, 1).start()
    for way in (0, 1):
        diff_copy(way, 1 - way).start()
    loss_swap = to_peer(9, losspart, lossgot)
    loss_swap.start()
    def product(owner, ahead):
        return dot(nb[owner, ahead].reshape(2 * share, slots), gathered(ahead)[...])

    for n in range(side):
        chip_copy(n).wait_recv()

    @pl.loop(0, side)
    def _(n):
        held[n] = product(n, 0)

    for way in (0, 1):
        diff_copy(way, way).wait_recv()
        diff_forward(way).start()
    loss_swap.wait_recv()
    losses[me_s] = losspart[...] + lossgot[...]
    tells = [to_seg(3, n, losses.at[me_s], losses.at[me_s]) for n in range(1, n_seg)]
    for copy in tells:
        copy.start()
    for way in (0, 1):
        for n in range(1, side):
            plane_copy(way, 1 - way, n).wait_recv()
            plane_forward(way, n).wait_recv()
    for way in (0, 1):
        diff_copy(way, 1 - way).wait_recv()

    @pl.loop(0, side)
    def _(n):
        held[n] += product(n, 1) + product(n, 3)

    for copy in tells:
        copy.wait_recv()
    total = losses[0]
    for n in range(1, n_seg):
        total = total + losses[n]
    loss_out[...] = total * (1.0 / S)

    ring_at = z * other + y * me_m
    below = side * slots

    def sent(slot, m):
        return p.at[pl.ds(below + (slot * 2 + m) * share, share), :out_half]

    def landed(number):
        return p.at[pl.ds(pl.multiple_of(below + number * share, 16), share), out_half:]

    def far_copy(way):
        return remote(
            sent(0, way), landed(way), s_r.at[6 + way], r_r.at[6 + way], dp=place(0, 1 + way * (side - 2))
        )

    def near_copy(way, last):
        m = way if last else 1 - way
        number = 2 * me_m + last
        return remote(
            sent(1 + way, m), landed(2 + number), s_r.at[8 + 2 * way + last], r_r.at[8 + number],
            dp=place(0, 1 + way * (side - 2)), mp=m,
        )

    def near_landed(f, last):
        where = landed(2 + 2 * f + last)
        return remote(where, where, s_r.at[0], r_r.at[8 + 2 * f + last], mp=other)

    for way in (0, 1):
        diff_forward(way).wait_recv()
    far = (ring_at + 2) % side
    nears = [(ring_at + 1) % side, (ring_at + side - 1) % side]

    def half_rows(m):
        return pl.ds(m * share, share)

    block = held[far] + product(far, 2)
    for way in (0, 1):
        sent(0, way)[...] = block[way * share : (way + 1) * share].astype(bf16)
        far_copy(way).start()
    for way in (0, 1):
        block = held[nears[way]] + product(nears[way], 2)
        sent(1 + way, 1 - way)[...] = block[(1 - way) * share : (2 - way) * share].astype(bf16)
        near_copy(way, 0).start()
        held[nears[way], half_rows(way)] = block[way * share : (way + 1) * share]
    held[ring_at] += product(ring_at, 2)
    finsend[...] = held[ring_at, pl.ds(pl.multiple_of(other * share, share), share)]
    own_swap = to_peer(10, finsend, fingot)
    own_swap.start()
    for way in (0, 1):
        far_copy(way).wait_recv()
        sent(1 + way, way)[...] = (held[nears[way], half_rows(way)] + landed(way)[...].astype(f32)).astype(bf16)
        near_copy(way, 1).start()
    own_swap.wait_recv()
    mine = held[ring_at, pl.ds(pl.multiple_of(me_m * share, share), share)]
    for last in (0, 1):
        near_landed(me_m, last).wait_recv()
        near_landed(other, last).wait_recv()
    out[:, kept] = mine + landed(2 + 2 * me_m)[...].astype(f32) + landed(3 + 2 * me_m)[...].astype(f32)
    out[:, away] = fingot[...] + landed(2 + 2 * other)[...].astype(f32) + landed(3 + 2 * other)[...].astype(f32)

    for n in range(1, side):
        for f in (0, 1):
            block_copy(f, n).wait_send()
    for n in range(side):
        chip_copy(n).wait_send()
    for way in (0, 1):
        for n in range(1, side):
            for m in (0, 1):
                plane_copy(way, m, n).wait_send()
            plane_forward(way, n).wait_send()
        for m in (0, 1):
            diff_copy(way, m).wait_send()
        diff_forward(way).wait_send()
        far_copy(way).wait_send()
        for last in (0, 1):
            near_copy(way, last).wait_send()
    for copy in u_sent + mg_x + firsts + seconds + [ab_sent, mg_sent, up_sent, hp_sent, so_sent, table_swap, loss_swap, own_swap] + tells:
        copy.wait_send()

    @pl.when(me_m == 0)
    def _():
        for copy in a_x + [a_swap]:
            copy.wait_send()

    @pl.when(me_m == 1)
    def _():
        extra_swap.wait_send()

    @pl.loop(1, n_dp)
    def _(n):
        a_copy(n).wait_send()
        m_copy(n).wait_send()
        h_copy(n).wait_send()


def run_step(h, ids, dest, counts, gain, down, up, x, sgain, w, p):
    side = 4
    n_seg = lax.axis_size("segment")
    n_dp = lax.axis_size("dp")
    tok, half = h.shape
    slots, width = x.shape
    cols = p.shape[1]
    out_half = cols // 2
    cap = slots // n_dp
    q = RANK // n_dp
    per = TEACH * q
    rows_u = n_seg * per
    known = rows_u * n_dp
    share = width // n_dp
    c = np.arange(known)
    c_i, c_t, c_k, c_q = c // rows_u, c % rows_u // per, c % per // q, c % q
    spot = np.arange(LANES)[None, :, None]
    xmap = (np.arange(n_seg)[:, None, None] == c_t) & (spot == c_i * q + c_q)
    xmap = jnp.asarray(xmap.astype(np.float32), dtype=bf16)
    kcol = jnp.asarray(c_k[None, :].astype(np.float32))
    vmem = pl.BlockSpec(memory_space=pltpu.VMEM)
    hbm = pl.BlockSpec(memory_space=pl.ANY)
    flops = 2 * (tok * half * cols + 2 * slots * width * cols)
    scratch = [
        (h.shape, bf16), (down.shape, bf16), (up.shape, bf16), (x.shape, bf16), (w.shape, bf16), (p.shape, bf16),
        (xmap.shape, bf16),
        ((rows_u, half // n_seg), bf16), ((n_seg, rows_u, half // n_seg), bf16), ((rows_u, half), bf16),
        ((tok, 2 * LANES), f32), ((tok, 2 * LANES), f32), ((tok, 2 * LANES), f32), ((tok, 2 * LANES), f32),
        ((slots, tok), bf16), ((tok, 2 * LANES), bf16),
        ((n_dp, cap, LANES), bf16), ((2, n_dp, cap, LANES), bf16), ((n_seg, slots, LANES), bf16),
        ((rows_u, LANES), f32), ((rows_u, LANES), f32), ((n_seg, rows_u, LANES), bf16),
        ((rows_u, cols), f32), ((rows_u, out_half), f32),
        ((n_dp, rows_u, out_half), bf16), ((2, n_dp, rows_u, n_seg // 2 * LANES), bf16),
        ((tok, cols), f32), ((tok, out_half), bf16), ((tok, out_half), bf16),
        ((n_dp, cap, out_half), bf16), ((n_dp, cap, out_half), bf16),
        (x.shape, bf16), ((slots, cols), f32), ((slots, out_half), bf16), ((slots, out_half), bf16),
        ((slots, LANES), f32), ((slots, LANES), f32), ((slots, known), bf16), ((slots, out_half), f32),
        ((width, slots), bf16), ((n_seg, side, 2, share, slots), bf16), ((side, 2 * share, out_half), f32),
        ((share, out_half), f32), ((share, out_half), f32),
        ((1, slots), f32), ((1, slots), f32), ((n_seg, 1, slots), f32),
    ]
    sems = [5 + cols // LANES, 11, 11, 4 * (n_seg - 1), 4 * (n_seg - 1), 4 * (n_dp - 1), 4 * (n_dp - 1), 28, 28, 12, 12]
    return pl.pallas_call(
        functools.partial(step_kernel, n_seg, side, cap),
        out_shape=(
            jax.ShapeDtypeStruct((share, cols), f32),
            jax.ShapeDtypeStruct((1, slots), f32),
        ),
        in_specs=[hbm] * 7 + [vmem] * 6,
        out_specs=(vmem, vmem),
        scratch_shapes=[pltpu.VMEM(*s) for s in scratch] + [pltpu.SemaphoreType.DMA((n,)) for n in sems],
        compiler_params=pltpu.CompilerParams(
            collective_id=0, has_side_effects=True, vmem_limit_bytes=60 * 2**20
        ),
        cost_estimate=pl.CostEstimate(flops=flops, bytes_accessed=25 * 2**20, transcendentals=0),
    )(
        h, down, up, x, w, p, xmap,
        ids.reshape(1, tok), dest.reshape(1, tok), counts, gain, sgain.reshape(width // LANES, LANES), kcol,
    )


def finish_kernel(grad, loss, grad_out, loss_out):
    grad_out[...] = grad[...]
    loss_out[...] = loss[...]


def finish(grad, loss):
    vmem = pl.BlockSpec(memory_space=pltpu.VMEM)
    return pl.pallas_call(
        finish_kernel,
        out_shape=(jax.ShapeDtypeStruct(grad.shape, f32), jax.ShapeDtypeStruct(loss.shape, f32)),
        in_specs=[vmem, vmem],
        out_specs=(vmem, vmem),
    )(grad, loss)


def local(
    teacher_hidden,
    teacher_id,
    destination,
    row_counts,
    section_gain,
    adapter_down,
    adapter_up,
    student_in,
    student_gain,
    student_weight,
    projector,
):
    weight_grad, row_loss = run_step(
        teacher_hidden,
        teacher_id,
        destination,
        row_counts,
        section_gain,
        adapter_down[0].T,
        adapter_up[0],
        student_in,
        student_gain,
        student_weight,
        projector,
    )
    weight_grad, row_loss = finish(weight_grad, row_loss)
    share, cols = weight_grad.shape
    return (weight_grad.reshape(1, share, cols), row_loss.reshape(student_in.shape[0]))


def solution(mesh):
    placed = (
        P("dp", "mp"),
        P("dp"),
        P("dp"),
        P("dp", None),
        P("segment", "mp"),
        P("segment", "mp", None),
        P("segment", None, "mp"),
        P("dp", "mp"),
        P("mp"),
        P("mp", "segment"),
        P("mp", "segment"),
    )
    return jax.shard_map(
        local,
        mesh=mesh,
        in_specs=placed,
        out_specs=(P("mp", "dp", "segment"), P("dp")),
        check_vma=False,
    )
```
